32 devices in a mesh: req: 8 (over z, x), tp: 4 (over y, core).
Axes of the slice: x: 2, y: 2, z: 4, core: 2. Of those that a mesh axis runs over, the one named last changes fastest.
Arguments:
- tokens: bfloat16 [4096, 2560], P('req'), may hold values from -6 to 6
- lengths: int32 [8], P('req'), may hold values from 1 to 512, as said below
- page_slot: int32 [32], replicated, may hold values from 0 to 31, as said below
- trainer_layout: int32 [32], replicated, may hold values from 0 to 31, each once
- trainer_qkv: float32 [2560, 3840], P(('req', 'tp'))
- trainer_gateup: float32 [2560, 13824], P(('req', 'tp')), may hold values from -0.125 to 0.125
- attn_gain: float32 [2560], replicated, may hold values from 0.1 to 1.9
- ffn_gain: float32 [2560], replicated, may hold values from 0.1 to 1.9
- out_proj: bfloat16 [2560, 2560], P('tp'), may hold values from -0.125 to 0.125
- down_proj: bfloat16 [6912, 2560], P('tp'), may hold values from -0.078125 to 0.078125
Outputs:
- layer_out: bfloat16 [4096, 2560], P(('req', 'tp'))
- kv_cache: bfloat16 [32, 128, 1280], P('req', None, 'tp')
The draws below stay inside these ranges and needn't reach their ends.
Inputs may be any that keep to these rules, and one draw needn't show every extreme that they name: `lengths`: heavy-tailed; some request has exactly 512. `page_slot`: a permutation; pool slot s belongs to request device s // 4; the 4 pages of one request belong to 4 different devices. `trainer_layout`: a permutation; shard s is the trainer shard on the device with index s over req and tp together.
All inputs are finite; a program needn't handle non-finite values.
Results may differ from the reference program's by a relative error of at most 0.0065.
The reference program's roundings to bfloat16 on the way (of `x_norm`, `probs`, `context`, `h_norm` and `hidden`) count: a program that leaves them out, or rounds other values in their place, can miss the bound.
Values may be sent and summed in bfloat16 or wider, within the bound.
No kernel may reach another device: no remote copies, remote signals or barrier semaphores. Data moves between devices by JAX's collectives and lax.ppermute only.
A program may use at most 192 MiB of HBM per device.

```python
import jax
import jax.numpy as jnp
from jax import lax

D = 2560
HEADS = 32
KV_HEADS = 8
HD = 80
FF = 6912
PAGE = 128
LMAX = 512
REQUESTS = 8
TOKENS = 4096
PPR = 4
PAGES = 32
GROUP = 4
QKVW = 3840
GROUP_COLS = 960
N_REQ = 8
N_TP = 4


def draw_lengths(key, part):
    first, second, third, fourth = jax.random.split(key, 4)
    a_draw = jax.random.randint(first, (REQUESTS,), 1, LMAX + 1)
    b_draw = jax.random.randint(second, (REQUESTS,), 1, LMAX + 1)
    c_draw = jax.random.randint(third, (REQUESTS,), 1, LMAX + 1)
    length = jnp.maximum(a_draw * b_draw // LMAX * c_draw // LMAX, 1)
    where_max = jax.random.randint(fourth, (), 0, REQUESTS)
    return length.at[where_max].set(LMAX).astype(jnp.int32)


def draw_page_slot(key, part):
    first, second, third = jax.random.split(key, 3)
    sigma = jax.random.permutation(first, jnp.arange(N_REQ, dtype=jnp.int32))
    shifts = jax.random.permutation(second, jnp.arange(N_REQ, dtype=jnp.int32))[:PPR]
    offsets = jax.random.randint(third, (N_REQ,), 0, PPR)
    request = jnp.arange(PAGES, dtype=jnp.int32) // PPR
    page_in = jnp.arange(PAGES, dtype=jnp.int32) % PPR
    holder = (sigma[request] + shifts[page_in]) % N_REQ
    position = (page_in + offsets[holder]) % PPR
    return (holder * PPR + position).astype(jnp.int32)


def draw_trainer_qkv(key, part):
    column = jnp.arange(QKVW) % GROUP_COLS
    sharp = column < (HEADS + KV_HEADS) * HD // N_TP
    base = jax.random.normal(key, (D, QKVW), jnp.float32)
    factor = jnp.where(sharp, 1.5, 1.0)
    return (base * factor[None, :] * D ** (-0.5)).astype(jnp.float32)


def block_scale(own_key, dims, pieces, smallest, high):
    loudness = 1.0
    for dim, blocks in pieces:
        steps = jax.random.uniform(jax.random.fold_in(jax.random.fold_in(own_key, 6), dim), (blocks,), jnp.float32, smallest / len(pieces), high / len(pieces))
        loudness = loudness * jnp.repeat(jnp.exp(steps), dims[dim] // blocks).reshape((-1,) + (1,) * (len(dims) - 1 - dim))
    return loudness


def gaussian(rng, dims, scale, reach, cuts=(), held_as=jnp.bfloat16):
    factor_of = block_scale(rng, dims, cuts, -0.22, 0.18) if cuts else 1.0
    values = jax.random.normal(rng, dims, jnp.float32) * scale * factor_of
    return jnp.minimum(jnp.maximum(values, -reach), reach).astype(held_as)


def setup_inputs(seed: int = 0) -> dict:
    streams_of = jax.random.split(jax.random.key(seed), 11)
    return {
        "tokens": gaussian(streams_of[0], (TOKENS, D), 1.0, 6.0, ((0, 8),)),
        "lengths": draw_lengths(jax.random.fold_in(streams_of[10], 71), 0),
        "page_slot": draw_page_slot(jax.random.fold_in(streams_of[10], 71), 0),
        "trainer_layout": jax.random.permutation(streams_of[3], N_REQ * N_TP).astype(jnp.int32),
        "trainer_qkv": draw_trainer_qkv(jax.random.fold_in(streams_of[10], 71), 0),
        "trainer_gateup": gaussian(streams_of[5], (D, 2 * FF), D ** -0.5, 0.125, ((0, 32),), jnp.float32),
        "attn_gain": jnp.clip(1.0 + 0.18 * jax.random.normal(streams_of[6], (D,), jnp.float32), 0.1, 1.9),
        "ffn_gain": jnp.clip(1.0 + 0.18 * jax.random.normal(streams_of[7], (D,), jnp.float32), 0.1, 1.9),
        "out_proj": gaussian(streams_of[8], (HEADS * HD, D), (HEADS * HD) ** -0.5, 0.125, ((0, 4),)),
        "down_proj": gaussian(streams_of[9], (FF, D), FF ** -0.5, 0.078125, ((0, 4),)),
    }


eps_norm = 1e-05
theta_base = 10000.0

def normed(values, gain):
    scale = lax.rsqrt(lax.optimization_barrier(jnp.mean(values * values, axis=-1, keepdims=True)) + eps_norm)
    return (values * scale * gain).astype(jnp.bfloat16)

def rotary(field, head_dim):
    half = head_dim // 2
    count = field.shape[0]
    freq = theta_base ** (-jnp.arange(half, dtype=jnp.float32) * 2.0 / head_dim)
    angles = jnp.arange(count, dtype=jnp.float32)[:, None] * freq[None, :]
    cosine = jnp.cos(angles)[:, None, :]
    sine = jnp.sin(angles)[:, None, :]
    first = field[..., :half]
    second = field[..., half:]
    return jnp.concatenate([first * cosine - second * sine, second * cosine + first * sine], axis=-1)

def widen(value):
    return lax.optimization_barrier(value).astype(jnp.float32)

def reference(tokens, lengths, page_slot, trainer_layout, trainer_qkv, trainer_gateup, attn_gain, ffn_gain, out_proj, down_proj):
    devices = N_REQ * N_TP
    rows_each = D // devices
    inverse = jnp.zeros((devices,), jnp.int32).at[trainer_layout].set(jnp.arange(devices, dtype=jnp.int32))

    def regroup(weights):
        width = weights.shape[1]
        return weights.astype(jnp.bfloat16).reshape(devices, rows_each, width)[inverse].reshape(D, width)
    local_heads = HEADS // N_TP
    local_kv = KV_HEADS // N_TP
    q_cols = local_heads * HD
    k_cols = local_kv * HD
    ff_local = FF // N_TP
    w_qkv = regroup(trainer_qkv).reshape(D, N_TP, GROUP_COLS)
    w_query = w_qkv[:, :, :q_cols].reshape(D, HEADS * HD)
    w_key = w_qkv[:, :, q_cols:q_cols + k_cols].reshape(D, KV_HEADS * HD)
    w_value = w_qkv[:, :, q_cols + k_cols:].reshape(D, KV_HEADS * HD)
    w_gu = regroup(trainer_gateup).reshape(D, N_TP, 2 * ff_local)
    w_gate = w_gu[:, :, :ff_local].reshape(D, FF)
    w_up = w_gu[:, :, ff_local:].reshape(D, FF)
    x_f = tokens.astype(jnp.float32)
    x_norm = normed(x_f, attn_gain)
    query = jnp.dot(x_norm, w_query, preferred_element_type=jnp.float32).reshape(N_REQ, LMAX, HEADS * HD)
    keys = jnp.dot(x_norm, w_key, preferred_element_type=jnp.float32).reshape(N_REQ, LMAX, KV_HEADS * HD)
    values = jnp.dot(x_norm, w_value, preferred_element_type=jnp.float32).reshape(N_REQ, LMAX, KV_HEADS * HD)

    def attend(items):
        q_one, k_one, v_one, length = items
        q16 = rotary(q_one.reshape(LMAX, HEADS, HD), HD).astype(jnp.bfloat16).reshape(LMAX, KV_HEADS, GROUP, HD)
        k16 = rotary(k_one.reshape(LMAX, KV_HEADS, HD), HD).astype(jnp.bfloat16)
        v16 = v_one.reshape(LMAX, KV_HEADS, HD).astype(jnp.bfloat16)
        scores = jnp.einsum('qkgd,skd->kgqs', widen(q16), widen(k16)) * HD ** (-0.5)
        slots = jnp.arange(LMAX, dtype=jnp.int32)
        allowed = (slots[None, :] <= slots[:, None]) & (slots[None, :] < length)
        scores = jnp.where(allowed[None, None], scores, -1e+30)
        probs = jax.nn.softmax(scores, axis=-1).astype(jnp.bfloat16)
        context = jnp.einsum('kgqs,skd->qkgd', widen(probs), widen(v16)).astype(jnp.bfloat16)
        return (context.reshape(LMAX, HEADS * HD), k16, v16)
    context, k_all, v_all = lax.map(attend, (query, keys, values, lengths))
    context = context.reshape(TOKENS, HEADS * HD)
    resid = x_f + jnp.dot(context, out_proj, preferred_element_type=jnp.float32)
    h_norm = normed(resid, ffn_gain)
    gate = jnp.dot(h_norm, w_gate, preferred_element_type=jnp.float32)
    up = jnp.dot(h_norm, w_up, preferred_element_type=jnp.float32)
    hidden = (jax.nn.silu(gate) * up).astype(jnp.bfloat16)
    down = jnp.dot(hidden, down_proj, preferred_element_type=jnp.float32)
    live = (jnp.arange(LMAX, dtype=jnp.int32)[None, :] < lengths[:, None]).reshape(TOKENS).astype(jnp.float32)
    layer_out = ((resid + down) * live[:, None]).astype(jnp.bfloat16)
    live_kv = (jnp.arange(LMAX, dtype=jnp.int32)[None, :] < lengths[:, None])[:, :, None, None]
    k_all = jnp.where(live_kv, k_all, jnp.zeros_like(k_all)).reshape(N_REQ, LMAX, N_TP, k_cols)
    v_all = jnp.where(live_kv, v_all, jnp.zeros_like(v_all)).reshape(N_REQ, LMAX, N_TP, k_cols)
    rows = jnp.stack([k_all, v_all], axis=3).reshape(PAGES, PAGE, 2 * KV_HEADS * HD)
    kv_cache = jnp.zeros((PAGES, PAGE, 2 * KV_HEADS * HD), jnp.bfloat16).at[page_slot].set(rows)
    return (layer_out, kv_cache)
```

```python
import jax
import jax.numpy as jnp
import numpy as np
from jax import lax
from jax.sharding import PartitionSpec as P

HD = 80
PAGE = 128
BF = jnp.bfloat16
F32 = jnp.float32

eps_norm = 1e-05
theta_base = 10000.0

PAIR = 2
CHUNKS = (320, 320)


def normed(values, gain):
    scale = lax.rsqrt(jnp.mean(values * values, axis=-1, keepdims=True) + eps_norm)
    return (values * scale * gain).astype(BF)


def rotary(field, head_dim):
    half = head_dim // 2
    count = field.shape[0]
    freq = theta_base ** (-jnp.arange(half, dtype=F32) * 2.0 / head_dim)
    angles = jnp.arange(count, dtype=F32)[:, None] * freq[None, :]
    cosine = jnp.cos(angles)[:, None, :]
    sine = jnp.sin(angles)[:, None, :]
    first = field[..., :half]
    second = field[..., half:]
    return jnp.concatenate(
        [first * cosine - second * sine, second * cosine + first * sine], axis=-1
    )


def dot(a, b):
    return jnp.dot(a, b, preferred_element_type=F32)


def body(
    tokens,
    lengths,
    page_slot,
    trainer_layout,
    trainer_qkv,
    trainer_gateup,
    attn_gain,
    ffn_gain,
    out_proj,
    down_proj,
):
    n_tp = lax.axis_size("tp")
    n_req = lax.axis_size("req")
    devices = n_tp * n_req
    req = lax.axis_index("req")
    tp = lax.axis_index("tp")
    rows_each = trainer_qkv.shape[0]
    seq_len, model_dim = tokens.shape
    head_dim = HD
    local_heads = out_proj.shape[0] // head_dim
    group_cols = trainer_qkv.shape[1] // n_tp
    local_kv = (group_cols // head_dim - local_heads) // 2
    group = local_heads // local_kv
    q_cols = local_heads * head_dim
    k_cols = local_kv * head_dim
    ff_local = down_proj.shape[0]
    share = seq_len // n_tp

    def swap(value, req_mask, tp_mask):
        pairs = [(d, d ^ (req_mask * n_tp + tp_mask)) for d in range(devices)]
        return lax.ppermute(value, ("req", "tp"), pairs)

    def pick(stack, index):
        return lax.dynamic_index_in_dim(stack, index, 0, keepdims=False)

    def to_groups(blocks):
        lead, (rows, columns) = blocks.shape[1:-2], blocks.shape[-2:]
        held = jnp.zeros(lead + (n_tp, rows, columns), blocks.dtype)
        for s in range(n_tp):
            mine = pick(blocks, tp ^ s)
            if s:
                mine = swap(mine, 0, s)
            held = lax.dynamic_update_slice_in_dim(
                held, jnp.expand_dims(mine, len(lead)), tp ^ s, len(lead)
            )
        return held.reshape(lead + (n_tp * rows, columns))

    qkv_blocks = trainer_qkv.astype(BF).reshape(rows_each, n_tp, group_cols).transpose(1, 0, 2)
    qkv_own = to_groups(qkv_blocks)

    def gather_rows(block_for):
        out = []
        for g in range(0, n_req, 2):
            block = block_for(g)
            if g:
                block = swap(block, g, 0)
            out.append(block)
            out.append(swap(block, 1, 0))
        return out

    qkv_parts = gather_rows(lambda g: qkv_own)

    order = jnp.arange(n_req, dtype=jnp.int32) ^ req
    shards = (order[:, None] * n_tp + jnp.arange(n_tp, dtype=jnp.int32)[None, :]).reshape(-1)
    blocks_at = trainer_layout[shards]
    columns_at = (
        blocks_at[:, None] * rows_each + jnp.arange(rows_each, dtype=jnp.int32)[None, :]
    ).reshape(-1)
    onehot = (jnp.arange(model_dim, dtype=jnp.int32)[:, None] == columns_at[None, :]).astype(BF)
    tokens_in = dot(tokens, onehot)
    attn_gain_in = attn_gain.reshape(devices, rows_each)[blocks_at].reshape(-1)
    ffn_gain_in = ffn_gain.reshape(devices, rows_each)[blocks_at].reshape(-1)
    out_in = dot(out_proj, onehot).astype(BF)
    x_norm = normed(tokens_in, attn_gain_in)

    half = n_tp // 2
    out_rel = [out_in] + [None] * (n_tp - 1)
    step = 1
    bits = []
    while step < n_tp:
        bits.append(step)
        step *= 2
    have = [0]
    for bit in reversed(bits):
        for s in list(have):
            out_rel[s ^ bit] = swap(out_rel[s], 0, bit)
            have.append(s ^ bit)

    halves = 2
    units = ff_local // halves
    chunks = list(CHUNKS) + [units - sum(CHUNKS)]
    my_class = (req // PAIR) % 2
    gu = trainer_gateup.astype(BF).reshape(rows_each, n_tp, 2, halves, units)
    chunk_weights = []
    start = 0
    for size in chunks:
        part = gu[..., start : start + size].transpose(1, 3, 0, 2, 4)
        part = to_groups(part.reshape(n_tp, halves, rows_each, 2 * size))
        mine = pick(part, my_class)
        other = pick(part, 1 - my_class)
        chunk_weights.append(gather_rows(lambda g: other if g & PAIR else mine))
        start += size

    joined = dot(x_norm, jnp.concatenate(qkv_parts, axis=0))
    query = rotary(joined[:, :q_cols].reshape(seq_len, local_heads, head_dim), head_dim)
    keys = rotary(
        joined[:, q_cols : q_cols + k_cols].reshape(seq_len, local_kv, head_dim), head_dim
    )
    query16 = query.astype(BF).reshape(seq_len, local_kv, group, head_dim)
    keys16 = keys.astype(BF)
    values16 = joined[:, q_cols + k_cols :].reshape(seq_len, local_kv, head_dim).astype(BF)
    scores = jnp.einsum(
        "qkgd,skd->kgqs", query16, keys16, preferred_element_type=F32
    ) * head_dim ** (-0.5)
    slots = jnp.arange(seq_len, dtype=jnp.int32)
    length = lengths[0]
    allowed = (slots[None, :] <= slots[:, None]) & (slots[None, :] < length)
    scores = jnp.where(allowed[None, None], scores, -1e30)
    probs = jax.nn.softmax(scores, axis=-1).astype(BF)
    context = jnp.einsum(
        "kgqs,skd->qkgd", probs, values16, preferred_element_type=F32
    ).astype(BF)

    by_share = context.reshape(n_tp, share, q_cols)
    mixed = 0.0
    for s in range(n_tp):
        piece = pick(by_share, tp ^ s)
        if s:
            piece = swap(piece, 0, s)
        mixed = mixed + dot(piece, out_rel[s])
    resid_in = lax.dynamic_slice_in_dim(tokens_in, tp * share, share, 0) + mixed
    h_share = normed(resid_in, ffn_gain_in)

    coarse = resid_in.astype(BF)
    fine = (resid_in - coarse.astype(F32)).astype(BF)
    back = (((1,), (1,)), ((), ()))
    resid = lax.dot_general(coarse, onehot, back, preferred_element_type=F32) + lax.dot_general(
        fine, onehot, back, preferred_element_type=F32
    )

    cross = n_tp // 2
    rest = n_tp // 2
    own = [None] * n_tp
    theirs = [None] * n_tp
    own[0] = h_share
    own[cross] = swap(h_share, 0, cross)
    theirs[0] = swap(h_share, PAIR, 0)
    cut = share // 2
    theirs[cross] = jnp.concatenate(
        [swap(theirs[0][:cut], 0, cross), swap(own[cross][cut:], PAIR, 0)], axis=0
    )
    for s in range(1, rest):
        for base in (0, cross):
            own[base ^ s] = swap(own[base], 0, s)
            theirs[base ^ s] = swap(theirs[base], 0, s)
    h_own = jnp.concatenate(own, axis=0)
    h_theirs = jnp.concatenate(theirs, axis=0)
    width = model_dim // n_req
    h_theirs = jnp.concatenate(
        [h_theirs[:, (j ^ PAIR) * width : ((j ^ PAIR) + 1) * width] for j in range(n_req)], axis=1
    )
    h_all = jnp.concatenate([h_own, h_theirs], axis=0)

    down_rel = jnp.roll(down_proj.reshape(halves, units, model_dim), -my_class, axis=0)
    down = 0.0
    start = 0
    for size, parts in zip(chunks, chunk_weights):
        projected = dot(h_all, jnp.concatenate(parts, axis=0))
        hidden = (jax.nn.silu(projected[:, :size]) * projected[:, size:]).astype(BF)
        returned = swap(hidden[seq_len:], PAIR, 0)
        down = (
            down
            + dot(hidden[:seq_len], down_rel[0, start : start + size])
            + dot(returned, down_rel[1, start : start + size])
        )
        start += size

    down = down.reshape(n_tp, share, model_dim)
    keep = [down[s] for s in range(n_tp)]
    for bit in bits:
        keep = [
            keep[i] + swap(keep[i + 1].astype(BF), 0, bit).astype(F32)
            for i in range(0, len(keep), 2)
        ]
    added = keep[0]
    share_slots = tp * share + jnp.arange(share, dtype=jnp.int32)
    live_share = (share_slots < length).astype(F32)
    layer_out = ((resid + added) * live_share[:, None]).astype(BF)

    live_rows = (slots < length)[:, None]
    key_rows = keys16.reshape(seq_len, k_cols)
    value_rows = values16.reshape(seq_len, k_cols)
    cache_rows = jnp.concatenate(
        [
            jnp.where(live_rows, key_rows, jnp.zeros_like(key_rows)),
            jnp.where(live_rows, value_rows, jnp.zeros_like(value_rows)),
        ],
        axis=1,
    )
    pages = cache_rows.reshape(seq_len // PAGE, PAGE, 2 * k_cols)
    pool_size = pages.shape[0]
    holders = lax.dynamic_slice_in_dim(page_slot, req * pool_size, pool_size, 0) // pool_size
    arrived = []
    for r in range(n_req):
        sent = pick(pages, jnp.argmax(holders == (req ^ r)))
        arrived.append(swap(sent, r, 0) if r else sent)
    targets = req * pool_size + jnp.arange(pool_size, dtype=jnp.int32)
    source = jnp.argmax(page_slot[None, :] == targets[:, None], axis=1) // pool_size
    kv_cache = jnp.stack(arrived)[source ^ req]
    return (layer_out, kv_cache)


def solution(mesh):
    return jax.shard_map(
        body,
        mesh=mesh,
        in_specs=(
            P("req", None),
            P("req"),
            P(),
            P(),
            P(("req", "tp"), None),
            P(("req", "tp"), None),
            P(),
            P(),
            P("tp", None),
            P("tp", None),
        ),
        out_specs=(P(("req", "tp"), None), P("req", None, "tp")),
        check_vma=False,
    )
```

```python
import jax
import jax.numpy as jnp
from jax import lax
from jax.experimental import pallas as pl
from jax.experimental.pallas import tpu as pltpu
from jax.sharding import PartitionSpec as P

HD = 80
PAGE = 128
BF = jnp.bfloat16
F32 = jnp.float32

eps_norm = 1e-05
theta_base = 10000.0

PAIR = 2
CHUNKS = (512,)


def normed(values, gain):
    scale = lax.rsqrt(jnp.mean(values * values, axis=-1, keepdims=True) + eps_norm)
    return (values * scale * gain).astype(BF)


def dot(a, b):
    return jnp.dot(a, b, preferred_element_type=F32)


def on_device(kernel, place, ins, shapes, vmem_mib, name):
    def run(place_ref, *refs):
        n_in, n_out = len(ins), len(shapes)
        outs, bufs, sems = refs[n_in : n_in + n_out], refs[n_in + n_out : -1], refs[-1]
        kernel(place_ref, *refs[:n_in], *bufs)
        copies = [pltpu.make_async_copy(bufs[i], outs[i], sems.at[i]) for i in range(n_out)]
        for copy in copies:
            copy.start()
        for copy in copies:
            copy.wait()

    return pl.pallas_call(
        run,
        in_specs=[pl.BlockSpec(memory_space=pltpu.SMEM)]
        + [pl.BlockSpec(memory_space=pltpu.VMEM)] * len(ins),
        out_specs=[pl.BlockSpec(memory_space=pltpu.HBM)] * len(shapes),
        out_shape=[jax.ShapeDtypeStruct(shape, BF) for shape in shapes],
        scratch_shapes=[pltpu.VMEM(shape, BF) for shape in shapes]
        + [pltpu.SemaphoreType.DMA((len(shapes),))],
        compiler_params=pltpu.CompilerParams(vmem_limit_bytes=vmem_mib * 2**20),
        name=name,
    )(place, *ins)


def split_qkv(place, shard, n_tp):
    rows, columns = shard.shape
    width = columns // n_tp

    def kernel(place_ref, shard_ref, *bufs):
        tp = place_ref[0]
        for s in range(n_tp):
            for g in range(n_tp):

                @pl.when((tp ^ s) == g)
                def _(s=s, g=g):
                    bufs[s][...] = shard_ref[:, g * width : (g + 1) * width].astype(BF)

    return on_device(kernel, place, [shard], [(rows, width)] * n_tp, 60, "split_qkv")


def split_gateup(place, shard, n_tp, halves, chunks):
    rows, columns = shard.shape
    width = columns // n_tp
    units = width // 2 // halves

    def kernel(place_ref, shard_ref, *bufs):
        tp = place_ref[0]
        for s in range(n_tp):
            begin = pl.multiple_of((tp ^ s) * width, 128)
            group = shard_ref[:, pl.ds(begin, width)].astype(BF)
            for q in range(halves):
                start = q * units
                edge = 0
                for size in chunks:
                    up = width // 2 + start
                    bufs[s % 2][s // 2, q, :, edge : edge + 2 * size] = jnp.concatenate(
                        [group[:, start : start + size], group[:, up : up + size]], axis=1
                    )
                    start += size
                    edge += 2 * size

    shapes = [(n_tp // 2, halves, rows, 2 * units)] * 2
    return on_device(kernel, place, [shard], shapes, 60, "split_gateup")


def pack_far(place, own, near, chunks):
    n_far, halves, rows, _ = own.shape
    n_far -= 1

    def kernel(place_ref, own_ref, near_ref, *bufs):
        edge = 0
        for c, size in enumerate(chunks):
            for f in range(n_far):
                bufs[c][f, 0] = own_ref[f + 1, :, :, edge : edge + 2 * size]
                bufs[c][f, 1] = near_ref[f + 1, :, :, edge : edge + 2 * size]
            edge += 2 * size

    shapes = [(n_far, 2, halves, rows, 2 * size) for size in chunks]
    return on_device(kernel, place, [own, near], shapes, 60, "pack_far")


def join_qkv(place, parts):
    rows, columns = parts[0].shape
    n_tp = len(parts)

    def kernel(place_ref, *refs):
        for s in range(n_tp):
            refs[n_tp][place_ref[0] ^ s] = refs[s][...]

    out = on_device(kernel, place, parts, [(n_tp, rows, columns)], 60, "join_qkv")[0]
    return out.reshape(n_tp * rows, columns)


def join_gateup(place, own, near, far, start):
    n_far, _, halves, rows, columns = far.shape
    n_tp = 2 * n_far + 2

    def kernel(place_ref, own_ref, near_ref, far_ref, *bufs):
        tp, mine = place_ref[0], place_ref[1]
        for k in range(2):
            bufs[k][tp] = own_ref[0, mine ^ k, :, start : start + columns]
            bufs[k][tp ^ 1] = near_ref[0, mine ^ k, :, start : start + columns]
            for f in range(n_far):
                for j in range(2):
                    bufs[k][tp ^ (2 * f + 2 + j)] = far_ref[f, j, mine ^ k]

    shapes = [(n_tp, rows, columns)] * 2
    outs = on_device(kernel, place, [own, near, far], shapes, 60, "join_gateup")
    return [out.reshape(n_tp * rows, columns) for out in outs]


SMEM = pl.BlockSpec(memory_space=pltpu.SMEM)
VMEM = pl.BlockSpec(memory_space=pltpu.VMEM)


def call(kernel, smem, vmem, shapes, scratch, name, mib=48):
    return pl.pallas_call(
        kernel,
        in_specs=[SMEM] * len(smem) + [VMEM] * len(vmem),
        out_specs=[VMEM] * len(shapes),
        out_shape=[jax.ShapeDtypeStruct(*shape) for shape in shapes],
        scratch_shapes=[pltpu.VMEM(*shape) for shape in scratch],
        compiler_params=pltpu.CompilerParams(vmem_limit_bytes=mib * 2**20),
        cost_estimate=pl.CostEstimate(flops=1, transcendentals=0, bytes_accessed=1),
        name=name,
    )(*smem, *vmem)


def permute_columns(values, columns_at):
    rows, width = values.shape
    tile = 256

    def kernel(values_ref, at_ref, out_ref):
        @pl.loop(0, width // tile)
        def _(i):
            at = pl.ds(pl.multiple_of(i * tile, tile), tile)
            source = lax.broadcasted_iota(jnp.int32, (width, tile), 0)
            onehot = (source == at_ref[:, at]).astype(F32).astype(BF)
            out_ref[:, at] = dot(values_ref[...], onehot)

    return call(
        kernel, [], [values, columns_at[None]], [((rows, width), F32)], [], "permute_columns"
    )[0]


def attend(place, lengths, joined, x_last, w_last, tables, out_in, sizes, shares):
    seq_len, columns = joined.shape
    heads, kv_heads, head_dim = sizes
    group = heads // kv_heads
    q_cols, k_cols = heads * head_dim, kv_heads * head_dim
    half = head_dim // 2
    wide = tables[0].shape[1]
    width = w_last[0].shape[0]
    model_dim = out_in.shape[1]
    share = seq_len // len(shares)
    tile = 128

    def kernel(place_ref, length_ref, joined_ref, x_ref, cos_ref, sin_ref, out_in_ref, *refs):
        w_refs = refs[: len(w_last)]
        leaving_ref, staying_ref, cache_ref, qk, v, context = refs[len(w_last) :]
        tp, length = place_ref[0], length_ref[0]
        lane = lax.broadcasted_iota(jnp.int32, (tile, wide), 1)
        first = lax.rem(lane, head_dim) < half
        for t in range(seq_len // tile):
            at = slice(t * tile, (t + 1) * tile)
            rows = joined_ref[at, :]
            for i, w_ref in enumerate(w_refs):
                rows = rows + dot(x_ref[at, i * width : (i + 1) * width], w_ref[...])
            head = rows[:, :wide]
            ahead = pltpu.roll(head, wide - half, 1)
            behind = pltpu.roll(head, half, 1)
            turned = head * cos_ref[at, :] + jnp.where(first, -ahead, behind) * sin_ref[at, :]
            qk[at, :] = turned.astype(BF)
            v[at, :] = rows[:, q_cols + k_cols :].astype(BF)
            slot = t * tile + lax.broadcasted_iota(jnp.int32, (tile, 1), 0)
            live = (slot < length).astype(F32)
            cache_ref[at, :k_cols] = (turned[:, q_cols : q_cols + k_cols] * live).astype(BF)
            cache_ref[at, k_cols:] = (rows[:, q_cols + k_cols :] * live).astype(BF)
        for k in range(kv_heads):
            key_at = q_cols + k * head_dim
            for t in range(seq_len // tile):
                at = slice(t * tile, (t + 1) * tile)
                count = (t + 1) * tile
                q = jnp.concatenate(
                    [
                        qk[at, (k * group + g) * head_dim : (k * group + g + 1) * head_dim]
                        for g in range(group)
                    ],
                    axis=0,
                )
                scores = lax.dot_general(
                    q,
                    qk[:count, key_at : key_at + head_dim],
                    (((1,), (1,)), ((), ())),
                    preferred_element_type=F32,
                ) * head_dim ** (-0.5)
                shape = (tile, count)
                slot = t * tile + lax.broadcasted_iota(jnp.int32, shape, 0)
                key = lax.broadcasted_iota(jnp.int32, shape, 1)
                allowed = (key <= slot) & (key < length)
                scores = scores.reshape(group, tile, count)
                scores = jnp.where(allowed[None], scores, -1e30)
                top = jnp.max(scores, axis=-1, keepdims=True)
                weight = jnp.exp(scores - top)
                probs = (weight / jnp.sum(weight, axis=-1, keepdims=True)).astype(BF)
                mixed = dot(
                    probs.reshape(group * tile, count), v[:count, k * head_dim : (k + 1) * head_dim]
                ).astype(BF)
                for g in range(group):
                    h = k * group + g
                    context[at, h * head_dim : (h + 1) * head_dim] = mixed[
                        g * tile : (g + 1) * tile
                    ]
        for i, s in enumerate(shares):
            block = context[pl.ds(pl.multiple_of((tp ^ s) * share, share), share), :]
            product = dot(block, out_in_ref[...])
            j = i % (len(shares) // 2)
            if i < len(shares) // 2:
                staying_ref[j * share : (j + 1) * share, :] = product
            else:
                leaving_ref[j * share : (j + 1) * share, :] = product.astype(BF)

    return call(
        kernel,
        [place, lengths],
        [joined, x_last, *tables, out_in, *w_last],
        [
            ((seq_len // 2, model_dim), BF),
            ((seq_len // 2, model_dim), F32),
            ((seq_len, 2 * k_cols), BF),
        ],
        [((seq_len, wide), BF), ((seq_len, k_cols), BF), ((seq_len, q_cols), BF)],
        "attend",
    )


def gated(tokens, blocks):
    rows, model_dim = tokens.shape
    each, columns = blocks[0].shape
    size = columns // 2
    tile = 256

    def kernel(tokens_ref, *refs):
        out_ref, weight = refs[-2:]
        for i, ref in enumerate(refs[:-2]):
            weight[i * each : (i + 1) * each, :] = ref[...]

        @pl.loop(0, rows // tile)
        def _(i):
            at = pl.ds(pl.multiple_of(i * tile, tile), tile)
            projected = dot(tokens_ref[at, :], weight[...])
            gate, up = projected[:, :size], projected[:, size:]
            out_ref[at, :] = (gate / (1.0 + jnp.exp(-gate)) * up).astype(BF)

    return call(
        kernel, [], [tokens, *blocks], [((rows, size), BF)], [((model_dim, columns), BF)], "gated"
    )[0]


def down_product(place, kept, returned, weight):
    rows = kept[0].shape[0]
    units, model_dim = weight.shape[0] // 2, weight.shape[1]
    tile = 128

    def kernel(place_ref, *refs):
        ins = refs[: 2 * len(kept)]
        weight_ref, leaving_ref, staying_ref = refs[2 * len(kept) :]

        def product(at):
            total = 0.0
            for k in range(2):
                begin = (place_ref[1] ^ k) * units
                for ref in ins[k * len(kept) : (k + 1) * len(kept)]:
                    size = ref.shape[1]
                    total += dot(ref[at, :], weight_ref[pl.ds(pl.multiple_of(begin, 32), size), :])
                    begin += size
            return total

        @pl.loop(0, rows // 2 // tile)
        def _(i):
            out = pl.ds(pl.multiple_of(i * tile, tile), tile)
            leaving_ref[out, :] = product(
                pl.ds(pl.multiple_of(rows // 2 + i * tile, tile), tile)
            ).astype(BF)
            staying_ref[out, :] = product(out)

    return call(
        kernel,
        [place],
        [*kept, *returned, weight],
        [((rows // 2, model_dim), BF), ((rows // 2, model_dim), F32)],
        [],
        "down_product",
    )


def body(
    tokens,
    lengths,
    page_slot,
    trainer_layout,
    trainer_qkv,
    trainer_gateup,
    attn_gain,
    ffn_gain,
    out_proj,
    down_proj,
):
    n_tp = lax.axis_size("tp")
    n_req = lax.axis_size("req")
    devices = n_tp * n_req
    req = lax.axis_index("req")
    tp = lax.axis_index("tp")
    rows_each = trainer_qkv.shape[0]
    seq_len, model_dim = tokens.shape
    head_dim = HD
    local_heads = out_proj.shape[0] // head_dim
    group_cols = trainer_qkv.shape[1] // n_tp
    local_kv = (group_cols // head_dim - local_heads) // 2
    group = local_heads // local_kv
    q_cols = local_heads * head_dim
    k_cols = local_kv * head_dim
    ff_local = down_proj.shape[0]
    share = seq_len // n_tp

    def swap(value, req_mask, tp_mask):
        pairs = [(d, d ^ (req_mask * n_tp + tp_mask)) for d in range(devices)]
        return lax.ppermute(value, ("req", "tp"), pairs)

    def pick(stack, index):
        return lax.dynamic_index_in_dim(stack, index, 0, keepdims=False)

    def sync(values):
        return lax.optimization_barrier(values)

    halves = 2
    units = ff_local // halves
    chunks = list(CHUNKS) + [units - sum(CHUNKS)]
    bits = [1 << k for k in range(16) if 1 << k < n_tp]
    evens = list(range(2, n_req, 2))
    singles = [r for r in evens if r & (r - 1) == 0]
    doubles = [r for r in evens if r & (r - 1)]
    plain = [r for r in evens if not r & PAIR]
    crossed = [r for r in evens if r & PAIR and r != PAIR]

    def spread_z(held, group):
        for r in group:
            bit = r & -r
            held[r] = swap(held[r ^ bit], bit, 0)

    def spread_class(held, mine, other, group):
        for r in group:
            if r == PAIR:
                held[r] = swap(other, PAIR, 0)
                continue
            rest = r & ~PAIR
            bit = 1 << (rest.bit_length() - 1)
            held[r] = swap(held[r ^ bit] if r != bit else mine, bit, 0)

    place = jnp.stack([tp, (req // PAIR) % 2])
    qkv_split = split_qkv(place, trainer_qkv, n_tp)
    trainer_gateup, qkv_split = sync((trainer_gateup, qkv_split))
    gu_own, gu_odd = split_gateup(place, trainer_gateup, n_tp, halves, chunks)
    gu_near = swap(gu_odd, 0, 1)
    qkv_split = [qkv_split[0]] + [swap(qkv_split[s], 0, s) for s in range(1, n_tp)]
    st = sync(
        dict(
            qkv_split=qkv_split,
            gu_own=gu_own,
            gu_near=gu_near,
            tokens=tokens,
            layout=trainer_layout,
            slots=jnp.arange(seq_len, dtype=jnp.int32),
        )
    )

    tokens, trainer_layout, slots = st["tokens"], st["layout"], st["slots"]
    gu_own, gu_near = st["gu_own"], st["gu_near"]
    qkv_own = join_qkv(place, st["qkv_split"])
    qkv = {0: qkv_own}
    spread_z(qkv, singles)
    qkv[1] = swap(qkv_own, 1, 0)
    far = list(pack_far(place, gu_own, gu_near, chunks))
    for c in range(len(chunks)):
        moved = [swap(far[c][f], 0, 2 * f + 2) for f in range(n_tp // 2 - 1)]
        far[c] = jnp.stack(moved) if len(moved) > 1 else moved[0][None]
    order = jnp.arange(n_req, dtype=jnp.int32) ^ req
    shards = (order[:, None] * n_tp + jnp.arange(n_tp, dtype=jnp.int32)[None, :]).reshape(-1)
    blocks_at = trainer_layout[shards]
    columns_at = (
        blocks_at[:, None] * rows_each + jnp.arange(rows_each, dtype=jnp.int32)[None, :]
    ).reshape(-1)
    columns_back = (
        jnp.argmax(
            blocks_at[None, :] == jnp.arange(devices, dtype=jnp.int32)[:, None], axis=1
        ).astype(jnp.int32)[:, None]
        * rows_each
        + jnp.arange(rows_each, dtype=jnp.int32)[None, :]
    ).reshape(-1)
    tokens_in = permute_columns(tokens, columns_at)
    x_norm = normed(tokens_in, attn_gain.reshape(devices, rows_each)[blocks_at].reshape(-1))
    st = sync(
        dict(
            qkv=qkv,
            far=far,
            gu_own=gu_own,
            gu_near=gu_near,
            x_norm=x_norm,
            tokens_in=tokens_in,
            onehot_at=columns_at,
            out_proj=out_proj,
            page_slot=page_slot,
            ffn_gain=ffn_gain,
        )
    )

    qkv, far, x_norm, tokens_in = st["qkv"], st["far"], st["x_norm"], st["tokens_in"]
    columns_at, page_slot = st["onehot_at"], st["page_slot"]
    blocks = []
    for c in range(len(chunks)):
        blocks.append(
            join_gateup(place, st["gu_own"], st["gu_near"], far[c], 2 * sum(chunks[:c]))
        )
    spread_z(qkv, doubles)
    for r in singles[::-1]:
        qkv[r ^ 1] = swap(qkv[r], 1, 0)
    gu = [dict() for _ in chunks]
    spread_class(gu[0], *blocks[0], plain)
    out_in = permute_columns(st["out_proj"], columns_at).astype(BF)
    half = head_dim // 2
    wide = (q_cols + k_cols + 127) // 128 * 128
    lane = jnp.arange(wide, dtype=jnp.int32) % half
    freq = theta_base ** (-lane.astype(F32) * 2.0 / head_dim)
    angles = slots.astype(F32)[:, None] * freq[None, :]
    tables = (jnp.cos(angles), jnp.sin(angles))
    ffn_gain_in = st["ffn_gain"].reshape(devices, rows_each)[blocks_at].reshape(-1)
    n_pages = seq_len // PAGE
    holders = lax.dynamic_slice_in_dim(page_slot, req * n_pages, n_pages, 0) // n_pages
    relative = jnp.arange(n_req, dtype=jnp.int32) ^ req
    chosen = jnp.argmax(holders[None, :] == relative[:, None], axis=1)
    targets = req * n_pages + jnp.arange(n_pages, dtype=jnp.int32)
    source = jnp.argmax(page_slot[None, :] == targets[:, None], axis=1) // n_pages
    st = sync(
        dict(
            qkv=qkv,
            gu=gu,
            blocks=blocks,
            x_norm=x_norm,
            out_in=out_in,
            ffn_gain_in=ffn_gain_in,
            tables=tables,
            pages=(chosen, source),
        )
    )

    qkv, gu, blocks, x_norm, out_in = (st[k] for k in ("qkv", "gu", "blocks", "x_norm", "out_in"))
    chosen, source = st["pages"]
    spread_class(gu[0], *blocks[0], [PAIR])
    for r in doubles:
        qkv[r ^ 1] = swap(qkv[r], 1, 0)
    width = model_dim // n_req
    first = [0, 1] + [r | j for r in singles for j in (0, 1)]
    last = [r | j for r in doubles for j in (0, 1)]

    def part(rs):
        return dot(
            jnp.concatenate([x_norm[:, r * width : (r + 1) * width] for r in rs], axis=1),
            jnp.concatenate([qkv[r] for r in rs], axis=0),
        )

    joined = part(first)
    st = sync(
        dict(qkv=qkv, gu=gu, blocks=blocks, joined=joined, x_norm=x_norm, tables=st["tables"])
    )

    qkv, gu, blocks, x_norm = (st[k] for k in ("qkv", "gu", "blocks", "x_norm"))
    spread_class(gu[0], *blocks[0], crossed)
    spread_class(gu[1], *blocks[1], [PAIR])
    for c in range(len(chunks)):
        gu[c][0] = blocks[c][0]
        gu[c][1] = swap(blocks[c][0], 1, 0)
    shares = sorted(range(n_tp), key=lambda s: [(s >> k) & 1 for k in range(len(bits))])
    leaving, staying, cache_rows = attend(
        place,
        lengths,
        st["joined"],
        jnp.concatenate([x_norm[:, r * width : (r + 1) * width] for r in last], axis=1),
        [qkv[r] for r in last],
        st["tables"],
        out_in,
        (local_heads, local_kv, head_dim),
        shares,
    )
    st = sync(
        dict(gu=gu, blocks=blocks, leaving=leaving, staying=staying, pages=cache_rows, out=out_in)
    )

    def sum_rest(partial):
        for bit in bits[1:]:
            rows = partial.shape[0] // 2
            arrived = swap(partial[rows:].astype(BF), 0, bit)
            partial = partial[:rows] + arrived.astype(F32)
        return partial

    gu, blocks = st["gu"], st["blocks"]
    mixed = sum_rest(st["staying"] + swap(st["leaving"], 0, bits[0]).astype(F32))
    spread_class(gu[1], *blocks[1], plain)
    for r in plain:
        gu[0][r ^ 1] = swap(gu[0][r], 1, 0)
    resid_in = lax.dynamic_slice_in_dim(tokens_in, tp * share, share, 0) + mixed
    h_share = normed(resid_in, ffn_gain_in)
    box = st["pages"].reshape(n_pages, PAGE, 2 * k_cols)[chosen][:, None]
    st = sync(dict(gu=gu, h_share=h_share, resid_in=resid_in, box=box))

    def reordered(values):
        return jnp.concatenate(
            [values[:, (j ^ PAIR) * width : ((j ^ PAIR) + 1) * width] for j in range(n_req)], axis=1
        )

    def page_step(box, bit):
        box = box.reshape((-1, 2) + box.shape[1:])
        return jnp.concatenate([box[:, 0], swap(box[:, 1], bit, 0)], axis=1)

    gu, h_share, resid_in = st["gu"], st["h_share"], st["resid_in"]
    cross = n_tp // 2
    h_across = swap(h_share, 0, cross)
    h_pair = swap(reordered(h_share), PAIR, 0)
    spread_class(gu[1], None, None, crossed)
    gu[0][PAIR ^ 1] = swap(gu[0][PAIR], 1, 0)
    box = page_step(st["box"], 1)
    coarse = resid_in.astype(BF)
    fine = (resid_in - coarse.astype(F32)).astype(BF)
    terms = permute_columns(jnp.concatenate([coarse, fine], axis=0), columns_back)
    resid = terms[:share] + terms[share:]
    st = sync(dict(gu=gu, h=(h_share, h_across, h_pair), resid=resid, box=box))

    gu, resid, box = st["gu"], st["resid"], st["box"]
    h_share, h_across, h_pair = st["h"]
    cut = share // 2
    h_diag = jnp.concatenate(
        [swap(h_pair[:cut], 0, cross), swap(reordered(h_across[cut:]), PAIR, 0)], axis=0
    )
    for r in crossed:
        gu[0][r ^ 1] = swap(gu[0][r], 1, 0)
    gu[1][PAIR ^ 1] = swap(gu[1][PAIR], 1, 0)
    if n_req > 4:
        box = page_step(box, 2)
    st = sync(dict(gu=gu, own=(h_share, h_across), theirs=(h_pair, h_diag), resid=resid, box=box))

    gu, resid, box = st["gu"], st["resid"], st["box"]

    def whole(parts):
        rows = jnp.concatenate(parts, axis=0)
        for bit in range(1, cross):
            assert bit == 1
            rows = jnp.concatenate([rows, swap(rows, 0, bit)], axis=0)
        return rows

    h_own = whole(st["own"])
    h_theirs = whole(st["theirs"])
    for r in plain + crossed:
        gu[1][r ^ 1] = swap(gu[1][r], 1, 0)
    bit = 4
    while bit < n_req:
        box = page_step(box, bit)
        bit *= 2
    st = sync(
        dict(gu=gu, own=h_own, theirs=h_theirs, resid=resid, box=box)
    )

    h_own, h_theirs, resid, box = (st[k] for k in ("own", "theirs", "resid", "box"))
    weights = [[held[r] for r in range(n_req)] for held in st["gu"]]
    returned = [swap(gated(h_theirs, weight), PAIR, 0) for weight in weights]
    kept = [gated(h_own, weight) for weight in weights]
    leaving, staying = down_product(place, kept, returned, down_proj)
    arrived = swap(leaving, 0, bits[0])
    added = sum_rest(staying + arrived.astype(F32))
    share_slots = tp * share + jnp.arange(share, dtype=jnp.int32)
    live_share = (share_slots < lengths[0]).astype(F32)
    layer_out = ((resid + added) * live_share[:, None]).astype(BF)
    kv_cache = box[0][source ^ req]
    return (layer_out, kv_cache)


def solution(mesh):
    return jax.shard_map(
        body,
        mesh=mesh,
        in_specs=(
            P("req", None),
            P("req"),
            P(),
            P(),
            P(("req", "tp"), None),
            P(("req", "tp"), None),
            P(),
            P(),
            P("tp", None),
            P("tp", None),
        ),
        out_specs=(P(("req", "tp"), None), P("req", None, "tp")),
        check_vma=False,
    )
```

```python
import jax
import jax.numpy as jnp
from jax import lax
from jax.experimental import pallas as pl
from jax.experimental.pallas import tpu as pltpu
from jax.sharding import PartitionSpec as P

HD = 80
PAGE = 128
BF = jnp.bfloat16
F32 = jnp.float32

eps_norm = 1e-05
theta_base = 10000.0

PAIR = 2
CHUNKS = (512,)


def normed(values, gain):
    scale = lax.rsqrt(jnp.mean(values * values, axis=-1, keepdims=True) + eps_norm)
    return (values * scale * gain).astype(BF)


def dot(a, b):
    return jnp.dot(a, b, preferred_element_type=F32)


def on_device(kernel, place, ins, shapes, vmem_mib, name):
    def run(place_ref, *refs):
        n_in, n_out = len(ins), len(shapes)
        outs, bufs, sems = refs[n_in : n_in + n_out], refs[n_in + n_out : -1], refs[-1]
        kernel(place_ref, *refs[:n_in], *bufs)
        copies = [pltpu.make_async_copy(bufs[i], outs[i], sems.at[i]) for i in range(n_out)]
        for copy in copies:
            copy.start()
        for copy in copies:
            copy.wait()

    return pl.pallas_call(
        run,
        in_specs=[pl.BlockSpec(memory_space=pltpu.SMEM)]
        + [pl.BlockSpec(memory_space=pltpu.VMEM)] * len(ins),
        out_specs=[pl.BlockSpec(memory_space=pltpu.HBM)] * len(shapes),
        out_shape=[jax.ShapeDtypeStruct(shape, BF) for shape in shapes],
        scratch_shapes=[pltpu.VMEM(shape, BF) for shape in shapes]
        + [pltpu.SemaphoreType.DMA((len(shapes),))],
        compiler_params=pltpu.CompilerParams(vmem_limit_bytes=vmem_mib * 2**20),
        cost_estimate=pl.CostEstimate(flops=1, transcendentals=0, bytes_accessed=1),
        name=name,
    )(place, *ins)


def split_qkv(place, shard, n_tp):
    rows, columns = shard.shape
    width = columns // n_tp

    def kernel(place_ref, shard_ref, *bufs):
        tp = place_ref[0]
        for s in range(n_tp):
            for g in range(n_tp):

                @pl.when((tp ^ s) == g)
                def _(s=s, g=g):
                    bufs[s][...] = shard_ref[:, g * width : (g + 1) * width].astype(BF)

    return on_device(kernel, place, [shard], [(rows, width)] * n_tp, 60, "split_qkv")


def split_gateup(place, shard, n_tp, halves, chunks):
    rows, columns = shard.shape
    width = columns // n_tp
    units = width // 2 // halves

    def kernel(place_ref, shard_ref, *bufs):
        tp = place_ref[0]
        for s in range(n_tp):
            begin = pl.multiple_of((tp ^ s) * width, 128)
            group = shard_ref[:, pl.ds(begin, width)].astype(BF)
            for q in range(halves):
                start = q * units
                edge = 0
                for size in chunks:
                    up = width // 2 + start
                    bufs[s % 2][s // 2, q, :, edge : edge + 2 * size] = jnp.concatenate(
                        [group[:, start : start + size], group[:, up : up + size]], axis=1
                    )
                    start += size
                    edge += 2 * size

    shapes = [(n_tp // 2, halves, rows, 2 * units)] * 2
    return on_device(kernel, place, [shard], shapes, 60, "split_gateup")


def pack_far(place, own, near, chunks):
    n_far, halves, rows, _ = own.shape
    n_far -= 1

    def kernel(place_ref, own_ref, near_ref, *bufs):
        edge = 0
        for c, size in enumerate(chunks):
            for f in range(n_far):
                bufs[c][f, 0] = own_ref[f + 1, :, :, edge : edge + 2 * size]
                bufs[c][f, 1] = near_ref[f + 1, :, :, edge : edge + 2 * size]
            edge += 2 * size

    shapes = [(n_far, 2, halves, rows, 2 * size) for size in chunks]
    return on_device(kernel, place, [own, near], shapes, 60, "pack_far")


def join_qkv(place, parts):
    rows, columns = parts[0].shape
    n_tp = len(parts)

    def kernel(place_ref, *refs):
        for s in range(n_tp):
            refs[n_tp][place_ref[0] ^ s] = refs[s][...]

    out = on_device(kernel, place, parts, [(n_tp, rows, columns)], 60, "join_qkv")[0]
    return out.reshape(n_tp * rows, columns)


def join_gateup(place, own, near, far, start):
    n_far, _, halves, rows, columns = far.shape
    n_tp = 2 * n_far + 2

    def kernel(place_ref, own_ref, near_ref, far_ref, *bufs):
        tp, mine = place_ref[0], place_ref[1]
        for k in range(2):
            bufs[k][tp] = own_ref[0, mine ^ k, :, start : start + columns]
            bufs[k][tp ^ 1] = near_ref[0, mine ^ k, :, start : start + columns]
            for f in range(n_far):
                for j in range(2):
                    bufs[k][tp ^ (2 * f + 2 + j)] = far_ref[f, j, mine ^ k]

    shapes = [(n_tp, rows, columns)] * 2
    outs = on_device(kernel, place, [own, near, far], shapes, 60, "join_gateup")
    return [out.reshape(n_tp * rows, columns) for out in outs]


SMEM = pl.BlockSpec(memory_space=pltpu.SMEM)
VMEM = pl.BlockSpec(memory_space=pltpu.VMEM)


def call(kernel, smem, vmem, shapes, scratch, name, mib=48):
    return pl.pallas_call(
        kernel,
        in_specs=[SMEM] * len(smem) + [VMEM] * len(vmem),
        out_specs=[VMEM] * len(shapes),
        out_shape=[jax.ShapeDtypeStruct(*shape) for shape in shapes],
        scratch_shapes=[pltpu.VMEM(*shape) for shape in scratch],
        compiler_params=pltpu.CompilerParams(vmem_limit_bytes=mib * 2**20),
        cost_estimate=pl.CostEstimate(flops=1, transcendentals=0, bytes_accessed=1),
        name=name,
    )(*smem, *vmem)


def permute_columns(values, columns_at, gain=None, dtype=F32):
    rows, width = values.shape
    tile = 256

    def kernel(values_ref, at_ref, *refs):
        out_ref = refs[0] if gain is None else refs[1]

        @pl.loop(0, width // tile)
        def _(i):
            at = pl.ds(pl.multiple_of(i * tile, tile), tile)
            source = lax.broadcasted_iota(jnp.int32, (width, tile), 0)
            onehot = (source == at_ref[:, at]).astype(F32).astype(BF)
            out_ref[:, at] = dot(values_ref[...], onehot).astype(dtype)

        if gain is not None:

            @pl.loop(0, rows // 128)
            def _(i):
                at = pl.ds(pl.multiple_of(i * 128, 128), 128)
                refs[2][at, :] = normed(out_ref[at, :], refs[0][...])

    ins = [values, columns_at[None]] + ([] if gain is None else [gain[None]])
    shapes = [((rows, width), dtype)] + ([] if gain is None else [((rows, width), BF)])
    outs = call(kernel, [], ins, shapes, [], "permute_columns")
    return outs[0] if gain is None else outs


def hold(value, *others):
    def kernel(*refs):
        pass

    return pl.pallas_call(
        kernel,
        in_specs=[pl.BlockSpec(memory_space=pl.ANY)] * (1 + len(others)),
        out_specs=pl.BlockSpec(memory_space=pl.ANY),
        out_shape=jax.ShapeDtypeStruct(value.shape, value.dtype),
        input_output_aliases={0: 0},
        cost_estimate=pl.CostEstimate(flops=10**11, transcendentals=0, bytes_accessed=10**8),
        name="hold",
    )(value, *others)


def attend(place, lengths, joined, x_last, w_last, tables, out_in, sizes, shares):
    seq_len, columns = joined.shape
    heads, kv_heads, head_dim = sizes
    group = heads // kv_heads
    q_cols, k_cols = heads * head_dim, kv_heads * head_dim
    half = head_dim // 2
    wide = (q_cols + k_cols + 127) // 128 * 128
    width = w_last[0].shape[0]
    model_dim = out_in.shape[1]
    share = seq_len // len(shares)
    tile = 128

    def kernel(place_ref, length_ref, joined_ref, x_ref, cos_ref, sin_ref, out_in_ref, *refs):
        w_refs = refs[: len(w_last)]
        leaving_ref, staying_ref, cache_ref, qk, v, context = refs[len(w_last) :]
        tp, length = place_ref[0], length_ref[0]
        lane = lax.broadcasted_iota(jnp.int32, (tile, wide), 1)
        first = lax.rem(lane, head_dim) < half
        for t in range(seq_len // tile):
            at = slice(t * tile, (t + 1) * tile)
            rows = joined_ref[at, :]
            for i, w_ref in enumerate(w_refs):
                rows = rows + dot(x_ref[at, i * width : (i + 1) * width], w_ref[...])
            head = rows[:, :wide]
            ahead = pltpu.roll(head, wide - half, 1)
            behind = pltpu.roll(head, half, 1)
            cosine, sine = (
                jnp.concatenate([ref[at, :]] * (wide // half + 1), axis=1)[:, :wide]
                for ref in (cos_ref, sin_ref)
            )
            turned = head * cosine + jnp.where(first, -ahead, behind) * sine
            qk[at, :] = turned.astype(BF)
            v[at, :] = rows[:, q_cols + k_cols :].astype(BF)
            slot = t * tile + lax.broadcasted_iota(jnp.int32, (tile, 1), 0)
            live = (slot < length).astype(F32)
            cache_ref[at, :k_cols] = (turned[:, q_cols : q_cols + k_cols] * live).astype(BF)
            cache_ref[at, k_cols:] = (rows[:, q_cols + k_cols :] * live).astype(BF)
        for k in range(kv_heads):
            key_at = q_cols + k * head_dim
            for t in range(seq_len // tile):
                at = slice(t * tile, (t + 1) * tile)
                count = (t + 1) * tile
                q = jnp.concatenate(
                    [
                        qk[at, (k * group + g) * head_dim : (k * group + g + 1) * head_dim]
                        for g in range(group)
                    ],
                    axis=0,
                )
                scores = lax.dot_general(
                    q,
                    qk[:count, key_at : key_at + head_dim],
                    (((1,), (1,)), ((), ())),
                    preferred_element_type=F32,
                ) * head_dim ** (-0.5)
                shape = (tile, count)
                slot = t * tile + lax.broadcasted_iota(jnp.int32, shape, 0)
                key = lax.broadcasted_iota(jnp.int32, shape, 1)
                allowed = (key <= slot) & (key < length)
                scores = scores.reshape(group, tile, count)
                scores = jnp.where(allowed[None], scores, -1e30)
                top = jnp.max(scores, axis=-1, keepdims=True)
                weight = jnp.exp(scores - top)
                probs = (weight / jnp.sum(weight, axis=-1, keepdims=True)).astype(BF)
                mixed = dot(
                    probs.reshape(group * tile, count), v[:count, k * head_dim : (k + 1) * head_dim]
                ).astype(BF)
                for g in range(group):
                    h = k * group + g
                    context[at, h * head_dim : (h + 1) * head_dim] = mixed[
                        g * tile : (g + 1) * tile
                    ]
        for i, s in enumerate(shares):
            block = context[pl.ds(pl.multiple_of((tp ^ s) * share, share), share), :]
            product = dot(block, out_in_ref[...])
            j = i % (len(shares) // 2)
            if i < len(shares) // 2:
                staying_ref[j * share : (j + 1) * share, :] = product
            else:
                leaving_ref[j * share : (j + 1) * share, :] = product.astype(BF)

    return call(
        kernel,
        [place, lengths],
        [joined, x_last, *tables, out_in, *w_last],
        [
            ((seq_len // 2, model_dim), BF),
            ((seq_len // 2, model_dim), F32),
            ((seq_len, 2 * k_cols), BF),
        ],
        [((seq_len, wide), BF), ((seq_len, k_cols), BF), ((seq_len, q_cols), BF)],
        "attend",
    )


def assemble(blocks):
    each, columns = blocks[0].shape
    count = len(blocks)

    def kernel(*refs):
        for i in range(count):
            refs[count][i * each : (i + 1) * each, :] = refs[i][...]

    return call(kernel, [], blocks, [((count * each, columns), BF)], [], "assemble", 24)[0]


def rows_product(pieces, weight, first=0, count=None, base=None, dtype=F32):
    rows, columns = count or pieces[0].shape[0], weight.shape[1]
    tile = 128

    def kernel(*refs):
        weight_ref = refs[len(pieces)]

        @pl.loop(0, rows // tile)
        def _(i):
            source = pl.ds(pl.multiple_of(first + i * tile, tile), tile)
            total = 0.0 if base is None else refs[len(pieces) + 1][source, :]
            begin = 0
            for ref in refs[: len(pieces)]:
                end = begin + ref.shape[1]
                total = total + dot(ref[source, :], weight_ref[begin:end, :])
                begin = end
            refs[-1][pl.ds(pl.multiple_of(i * tile, tile), tile), :] = total.astype(dtype)

    ins = [*pieces, weight] + ([] if base is None else [base])
    return call(kernel, [], ins, [((rows, columns), dtype)], [], "rows_product", 24)[0]


def add_share(staying, arrived, extra):
    rows, columns = staying.shape
    half = rows // 2

    def kernel(staying_ref, arrived_ref, extra_ref, keep_ref, send_ref):
        keep_ref[...] = (
            staying_ref[:half, :] + arrived_ref[:half, :].astype(F32) + extra_ref[...]
        )
        send_ref[...] = (staying_ref[half:, :] + arrived_ref[half:, :].astype(F32)).astype(BF)

    return call(
        kernel,
        [],
        [staying, arrived, extra],
        [((half, columns), F32), ((half, columns), BF)],
        [],
        "add_share",
        24,
    )


def class_rows(place, weight):
    rows, columns = weight.shape
    half = rows // 2

    def kernel(place_ref, weight_ref, *outs):
        for k in range(2):
            begin = pl.multiple_of((place_ref[1] ^ k) * half, 16)
            outs[k][...] = weight_ref[pl.ds(begin, half), :]

    return call(kernel, [place], [weight], [((half, columns), BF)] * 2, [], "class_rows")


def gated(tokens, weight):
    rows = tokens.shape[0]
    size = weight.shape[1] // 2
    tile = 256

    def kernel(tokens_ref, weight_ref, out_ref):
        @pl.loop(0, rows // tile)
        def _(i):
            at = pl.ds(pl.multiple_of(i * tile, tile), tile)
            projected = dot(tokens_ref[at, :], weight_ref[...])
            gate, up = projected[:, :size], projected[:, size:]
            out_ref[at, :] = (gate / (1.0 + jnp.exp(-gate)) * up).astype(BF)

    return call(kernel, [], [tokens, weight], [((rows, size), BF)], [], "gated", 24)[0]


def body(
    tokens,
    lengths,
    page_slot,
    trainer_layout,
    trainer_qkv,
    trainer_gateup,
    attn_gain,
    ffn_gain,
    out_proj,
    down_proj,
):
    n_tp = lax.axis_size("tp")
    n_req = lax.axis_size("req")
    devices = n_tp * n_req
    req = lax.axis_index("req")
    tp = lax.axis_index("tp")
    rows_each = trainer_qkv.shape[0]
    seq_len, model_dim = tokens.shape
    head_dim = HD
    local_heads = out_proj.shape[0] // head_dim
    group_cols = trainer_qkv.shape[1] // n_tp
    local_kv = (group_cols // head_dim - local_heads) // 2
    group = local_heads // local_kv
    q_cols = local_heads * head_dim
    k_cols = local_kv * head_dim
    ff_local = down_proj.shape[0]
    share = seq_len // n_tp

    def swap(value, req_mask, tp_mask):
        pairs = [(d, d ^ (req_mask * n_tp + tp_mask)) for d in range(devices)]
        return lax.ppermute(value, ("req", "tp"), pairs)

    def pick(stack, index):
        return lax.dynamic_index_in_dim(stack, index, 0, keepdims=False)

    def sync(values):
        return lax.optimization_barrier(values)

    halves = 2
    units = ff_local // halves
    chunks = list(CHUNKS) + [units - sum(CHUNKS)]
    bits = [1 << k for k in range(16) if 1 << k < n_tp]
    evens = list(range(2, n_req, 2))
    zbits = [1 << k for k in range(1, 16) if 1 << k < n_req]
    singles = [r for r in evens if r & (r - 1) == 0]
    doubles = [r for r in evens if r & (r - 1)]
    plain = [r for r in evens if not r & PAIR]
    crossed = [r for r in evens if r & PAIR and r != PAIR]

    def spread_z(held, group):
        for r in group:
            bit = r & -r
            held[r] = swap(held[r ^ bit], bit, 0)

    def spread_class(held, mine, other, group):
        for r in group:
            if r == PAIR:
                held[r] = swap(other, PAIR, 0)
                continue
            rest = r & ~PAIR
            bit = 1 << (rest.bit_length() - 1)
            held[r] = swap(held[r ^ bit] if r != bit else mine, bit, 0)

    place = jnp.stack([tp, (req // PAIR) % 2])
    qkv_split = split_qkv(place, trainer_qkv, n_tp)
    half = head_dim // 2
    freq = theta_base ** (-jnp.arange(half, dtype=F32) * 2.0 / head_dim)
    angles = jnp.arange(seq_len, dtype=F32)[:, None] * freq[None, :]
    tables = (jnp.cos(angles), jnp.sin(angles))
    trainer_gateup, qkv_split = sync((trainer_gateup, qkv_split))
    gu_own, gu_odd = split_gateup(place, trainer_gateup, n_tp, halves, chunks)
    qkv_split = [qkv_split[0]] + [swap(qkv_split[s], 0, s) for s in range(1, n_tp)]
    st = sync(
        dict(
            qkv_split=qkv_split,
            gu_own=gu_own,
            gu_odd=gu_odd,
            tokens=tokens,
            layout=trainer_layout,
            tables=tables,
        )
    )

    tokens, trainer_layout, tables = st["tokens"], st["layout"], st["tables"]
    gu_own, gu_near = st["gu_own"], swap(st["gu_odd"], 0, 1)
    qkv_own = join_qkv(place, st["qkv_split"])
    qkv = {0: qkv_own}
    spread_z(qkv, singles)
    qkv[1] = swap(qkv_own, 1, 0)
    far = list(pack_far(place, gu_own, gu_near, chunks))
    tokens, far = sync((tokens, far))
    for c in range(len(chunks)):
        moved = [swap(far[c][f], 0, 2 * f + 2) for f in range(n_tp // 2 - 1)]
        far[c] = jnp.stack(moved) if len(moved) > 1 else moved[0][None]
    order = jnp.arange(n_req, dtype=jnp.int32) ^ req
    shards = (order[:, None] * n_tp + jnp.arange(n_tp, dtype=jnp.int32)[None, :]).reshape(-1)
    blocks_at = trainer_layout[shards]
    columns_at = (
        blocks_at[:, None] * rows_each + jnp.arange(rows_each, dtype=jnp.int32)[None, :]
    ).reshape(-1)
    columns_back = (
        jnp.argmax(
            blocks_at[None, :] == jnp.arange(devices, dtype=jnp.int32)[:, None], axis=1
        ).astype(jnp.int32)[:, None]
        * rows_each
        + jnp.arange(rows_each, dtype=jnp.int32)[None, :]
    ).reshape(-1)
    gain_in = attn_gain.reshape(devices, rows_each)[blocks_at].reshape(-1)
    tokens_in, x_norm = permute_columns(tokens, columns_at, gain_in)
    st = sync(
        dict(
            qkv=qkv,
            far=far,
            gu_own=gu_own,
            gu_near=gu_near,
            x_norm=x_norm,
            tokens_in=tokens_in,
            onehot_at=columns_at,
            out_proj=out_proj,
            down_proj=down_proj,
            page_slot=page_slot,
            ffn_gain=ffn_gain,
        )
    )

    qkv, far, x_norm, tokens_in = st["qkv"], st["far"], st["x_norm"], st["tokens_in"]
    columns_at, page_slot = st["onehot_at"], st["page_slot"]
    blocks = []
    for c in range(len(chunks)):
        blocks.append(
            join_gateup(place, st["gu_own"], st["gu_near"], far[c], 2 * sum(chunks[:c]))
        )
    spread_z(qkv, doubles)
    for r in singles[::-1]:
        qkv[r ^ 1] = swap(qkv[r], 1, 0)
    gu = [dict() for _ in chunks]
    spread_class(gu[0], *blocks[0], plain)
    out_in = permute_columns(st["out_proj"], columns_at, dtype=BF)
    down_rel = class_rows(place, st["down_proj"])
    ffn_gain_in = st["ffn_gain"].reshape(devices, rows_each)[blocks_at].reshape(-1)
    n_pages = seq_len // PAGE
    holders = lax.dynamic_slice_in_dim(page_slot, req * n_pages, n_pages, 0) // n_pages
    page_bits = [bit for bit in zbits if bit != PAIR] + [1, PAIR]
    at_slot = [
        sum(bit for k, bit in enumerate(page_bits) if (i >> k) & 1) for i in range(n_req)
    ]
    relative = jnp.asarray(at_slot, jnp.int32) ^ req
    chosen = jnp.argmax(holders[None, :] == relative[:, None], axis=1)
    targets = req * n_pages + jnp.arange(n_pages, dtype=jnp.int32)
    source = jnp.argmax(page_slot[None, :] == targets[:, None], axis=1) // n_pages
    source = jnp.argmax(relative[None, :] == source[:, None], axis=1)
    st = sync(
        dict(
            qkv=qkv,
            gu=gu,
            blocks=blocks,
            x_norm=x_norm,
            out_in=out_in,
            down_rel=down_rel,
            ffn_gain_in=ffn_gain_in,
            pages=(chosen, source),
        )
    )

    qkv, gu, blocks, x_norm, out_in = (st[k] for k in ("qkv", "gu", "blocks", "x_norm", "out_in"))
    chosen, source = st["pages"]
    down_rel, ffn_gain_in = st["down_rel"], st["ffn_gain_in"]
    spread_class(gu[0], *blocks[0], [PAIR])
    spread_class(gu[1], *blocks[1], plain)
    for r in doubles:
        qkv[r ^ 1] = swap(qkv[r], 1, 0)
    gu[1][0] = blocks[1][0]
    gu[1][1] = swap(blocks[1][0], 1, 0)
    width = model_dim // n_req
    first = [0, 1] + [r | j for r in singles for j in (0, 1)]
    last = [r | j for r in doubles for j in (0, 1)]

    def part(rs):
        return dot(
            jnp.concatenate([x_norm[:, r * width : (r + 1) * width] for r in rs], axis=1),
            jnp.concatenate([qkv[r] for r in rs], axis=0),
        )

    joined = part(first)
    st = sync(dict(qkv=qkv, gu=gu, blocks=blocks, joined=joined, x_norm=x_norm))

    qkv, gu, blocks, x_norm = (st[k] for k in ("qkv", "gu", "blocks", "x_norm"))
    spread_class(gu[0], *blocks[0], crossed)
    spread_class(gu[1], *blocks[1], [PAIR])
    gu[0][0] = blocks[0][0]
    gu[0][1] = swap(blocks[0][0], 1, 0)
    for r in plain:
        gu[0][r ^ 1] = swap(gu[0][r], 1, 0)
    shares = sorted(range(n_tp), key=lambda s: [(s >> k) & 1 for k in range(len(bits))])
    leaving, staying, cache_rows = attend(
        place,
        lengths,
        st["joined"],
        jnp.concatenate([x_norm[:, r * width : (r + 1) * width] for r in last], axis=1),
        [qkv[r] for r in last],
        tables,
        out_in,
        (local_heads, local_kv, head_dim),
        shares,
    )
    st = sync(
        dict(gu=gu, blocks=blocks, leaving=leaving, staying=staying, pages=cache_rows, out=out_in)
    )

    gu, blocks = st["gu"], st["blocks"]
    tokens_share = lax.dynamic_slice_in_dim(tokens_in, tp * share, share, 0)
    keep, send = add_share(st["staying"], swap(st["leaving"], 0, bits[0]), tokens_share)
    resid_in = keep + swap(send, 0, bits[1]).astype(F32)
    spread_class(gu[1], None, None, crossed)
    gu[0][PAIR ^ 1] = swap(gu[0][PAIR], 1, 0)
    for r in plain:
        gu[1][r ^ 1] = swap(gu[1][r], 1, 0)
    h_share = normed(resid_in, ffn_gain_in)

    def reordered(values):
        return jnp.concatenate(
            [values[:, (j ^ PAIR) * width : ((j ^ PAIR) + 1) * width] for j in range(n_req)], axis=1
        )

    def page_step(box, bit):
        box = box.reshape((-1, 2) + box.shape[1:])
        return jnp.concatenate([box[:, 0], swap(box[:, 1], bit, 0)], axis=1)

    late = crossed[0]
    gu[1][late] = hold(gu[1][late], gu[0][PAIR ^ 1], *[gu[1][r ^ 1] for r in plain])
    st = sync(dict(gu=gu, h=(h_share, reordered(h_share)), resid_in=resid_in, pages=st["pages"]))

    gu, resid_in = st["gu"], st["resid_in"]
    h_share, h_leaving = st["h"]
    cross = n_tp // 2
    h_across = swap(h_share, 0, cross)
    h_pair = swap(h_leaving, PAIR, 0)
    for r in crossed:
        gu[0][r ^ 1] = swap(gu[0][r], 1, 0)
    coarse = resid_in.astype(BF)
    fine = (resid_in - coarse.astype(F32)).astype(BF)
    terms = permute_columns(jnp.concatenate([coarse, fine], axis=0), columns_back)
    cut = share // 2
    st = sync(
        dict(
            gu=gu,
            own=(h_share, h_across),
            theirs=h_pair,
            halves=(h_pair[:cut], reordered(h_across[cut:])),
            terms=terms,
            box=st["pages"].reshape(n_pages, PAGE, 2 * k_cols)[chosen][:, None],
        )
    )

    gu, box = st["gu"], st["box"]
    over_y, over_pair = st["halves"]
    h_diag = [swap(over_y, 0, cross), swap(over_pair, PAIR, 0)]
    gu[1][PAIR ^ 1] = swap(gu[1][PAIR], 1, 0)
    for bit in page_bits[:-2]:
        box = page_step(box, bit)
    resid = st["terms"][:share] + st["terms"][share:]
    own = jnp.concatenate(st["own"], axis=0)
    theirs = jnp.concatenate([st["theirs"]] + h_diag, axis=0)
    st = sync(dict(gu=gu, h=(own, theirs), resid=resid, box=box))

    def whole(rows):
        for bit in bits[:-1]:
            rows = jnp.concatenate([rows, swap(rows, 0, bit)], axis=0)
        return rows

    gu, box = st["gu"], st["box"]
    h_own, h_theirs = (whole(rows) for rows in st["h"])
    for r in crossed:
        gu[1][r ^ 1] = swap(gu[1][r], 1, 0)
    weight = assemble([gu[0][r] for r in range(n_req)])
    theirs = gated(h_theirs, weight)
    kept = [gated(h_own, weight)]
    st = sync(
        dict(gu=gu[1], h=(h_own, h_theirs), hidden=(kept, theirs), resid=st["resid"], box=box)
    )

    resid, box = st["resid"], st["box"]
    h_own, h_theirs = st["h"]
    kept, theirs = st["hidden"]
    returned = [swap(theirs, PAIR, 0)]
    weight = assemble([st["gu"][r] for r in range(n_req)])
    theirs = gated(h_theirs, weight)
    box = page_step(box, page_bits[-2])
    h_own, theirs = sync((h_own, theirs))
    returned.append(swap(theirs, PAIR, 0))
    kept.append(gated(h_own, weight))
    product = rows_product(kept, down_rel[0])
    returned, box, product = sync((returned, box, product))
    rows = seq_len // 2
    leaving = rows_product(returned, down_rel[1], rows, rows, product, BF)
    arrived = swap(leaving, 0, bits[0])
    staying = rows_product(returned, down_rel[1], 0, rows, product)
    keep, send = add_share(staying, arrived, resid)
    box = page_step(box, page_bits[-1])
    share_slots = tp * share + jnp.arange(share, dtype=jnp.int32)
    live_share = (share_slots < lengths[0]).astype(F32)
    layer_out = ((keep + swap(send, 0, bits[1]).astype(F32)) * live_share[:, None]).astype(BF)
    kv_cache = box[0][source]
    return (layer_out, kv_cache)


def solution(mesh):
    return jax.shard_map(
        body,
        mesh=mesh,
        in_specs=(
            P("req", None),
            P("req"),
            P(),
            P(),
            P(("req", "tp"), None),
            P(("req", "tp"), None),
            P(),
            P(),
            P("tp", None),
            P("tp", None),
        ),
        out_specs=(P(("req", "tp"), None), P("req", None, "tp")),
        check_vma=False,
    )
```

```python
import jax
import jax.numpy as jnp
from jax import lax
from jax.experimental import pallas as pl
from jax.experimental.pallas import tpu as pltpu
from jax.sharding import PartitionSpec as P

HD = 80
PAGE = 128
BF = jnp.bfloat16
F32 = jnp.float32

eps_norm = 1e-05
theta_base = 10000.0

PAIR = 2
CHUNKS = (512,)


def normed(values, gain):
    scale = lax.rsqrt(jnp.mean(values * values, axis=-1, keepdims=True) + eps_norm)
    return (values * scale * gain).astype(BF)


def dot(a, b):
    return jnp.dot(a, b, preferred_element_type=F32)


def on_device(kernel, place, ins, shapes, vmem_mib, name):
    def run(place_ref, *refs):
        n_in, n_out = len(ins), len(shapes)
        outs, bufs, sems = refs[n_in : n_in + n_out], refs[n_in + n_out : -1], refs[-1]
        kernel(place_ref, *refs[:n_in], *bufs)
        copies = [pltpu.make_async_copy(bufs[i], outs[i], sems.at[i]) for i in range(n_out)]
        for copy in copies:
            copy.start()
        for copy in copies:
            copy.wait()

    return pl.pallas_call(
        run,
        in_specs=[pl.BlockSpec(memory_space=pltpu.SMEM)]
        + [pl.BlockSpec(memory_space=pltpu.VMEM)] * len(ins),
        out_specs=[pl.BlockSpec(memory_space=pltpu.HBM)] * len(shapes),
        out_shape=[jax.ShapeDtypeStruct(shape, BF) for shape in shapes],
        scratch_shapes=[pltpu.VMEM(shape, BF) for shape in shapes]
        + [pltpu.SemaphoreType.DMA((len(shapes),))],
        compiler_params=pltpu.CompilerParams(vmem_limit_bytes=vmem_mib * 2**20),
        cost_estimate=pl.CostEstimate(flops=1, transcendentals=0, bytes_accessed=1),
        name=name,
    )(place, *ins)


def split_qkv(place, shard, n_tp):
    rows, columns = shard.shape
    width = columns // n_tp

    def kernel(place_ref, shard_ref, *bufs):
        tp = place_ref[0]
        for s in range(n_tp):
            for g in range(n_tp):

                @pl.when((tp ^ s) == g)
                def _(s=s, g=g):
                    bufs[s][...] = shard_ref[:, g * width : (g + 1) * width].astype(BF)

    return on_device(kernel, place, [shard], [(rows, width)] * n_tp, 60, "split_qkv")


def split_gateup(place, shard, n_tp, halves, chunks):
    rows, columns = shard.shape
    width = columns // n_tp
    units = width // 2 // halves

    def kernel(place_ref, shard_ref, *bufs):
        tp = place_ref[0]
        for s in range(n_tp):
            begin = pl.multiple_of((tp ^ s) * width, 128)
            group = shard_ref[:, pl.ds(begin, width)].astype(BF)
            for q in range(halves):
                start = q * units
                edge = 0
                for size in chunks:
                    up = width // 2 + start
                    bufs[s % 2][s // 2, q, :, edge : edge + 2 * size] = jnp.concatenate(
                        [group[:, start : start + size], group[:, up : up + size]], axis=1
                    )
                    start += size
                    edge += 2 * size

    shapes = [(n_tp // 2, halves, rows, 2 * units)] * 2
    return on_device(kernel, place, [shard], shapes, 60, "split_gateup")


def pack_far(place, own, near, chunks):
    n_far, halves, rows, _ = own.shape
    n_far -= 1

    def kernel(place_ref, own_ref, near_ref, *bufs):
        edge = 0
        for c, size in enumerate(chunks):
            for f in range(n_far):
                bufs[c][f, 0] = own_ref[f + 1, :, :, edge : edge + 2 * size]
                bufs[c][f, 1] = near_ref[f + 1, :, :, edge : edge + 2 * size]
            edge += 2 * size

    shapes = [(n_far, 2, halves, rows, 2 * size) for size in chunks]
    return on_device(kernel, place, [own, near], shapes, 60, "pack_far")


def join_qkv(place, parts):
    rows, columns = parts[0].shape
    n_tp = len(parts)

    def kernel(place_ref, *refs):
        for s in range(n_tp):
            refs[n_tp][place_ref[0] ^ s] = refs[s][...]

    out = on_device(kernel, place, parts, [(n_tp, rows, columns)], 60, "join_qkv")[0]
    return out.reshape(n_tp * rows, columns)


def join_gateup(place, own, near, far, start):
    n_far, _, halves, rows, columns = far.shape
    n_tp = 2 * n_far + 2

    def kernel(place_ref, own_ref, near_ref, far_ref, *bufs):
        tp, mine = place_ref[0], place_ref[1]
        for k in range(2):
            bufs[k][tp] = own_ref[0, mine ^ k, :, start : start + columns]
            bufs[k][tp ^ 1] = near_ref[0, mine ^ k, :, start : start + columns]
            for f in range(n_far):
                for j in range(2):
                    bufs[k][tp ^ (2 * f + 2 + j)] = far_ref[f, j, mine ^ k]

    shapes = [(n_tp, rows, columns)] * 2
    outs = on_device(kernel, place, [own, near, far], shapes, 60, "join_gateup")
    return [out.reshape(n_tp * rows, columns) for out in outs]


SMEM = pl.BlockSpec(memory_space=pltpu.SMEM)
VMEM = pl.BlockSpec(memory_space=pltpu.VMEM)


def call(kernel, smem, vmem, shapes, scratch, name, mib=48, flops=1):
    return pl.pallas_call(
        kernel,
        in_specs=[SMEM] * len(smem) + [VMEM] * len(vmem),
        out_specs=[VMEM] * len(shapes),
        out_shape=[jax.ShapeDtypeStruct(*shape) for shape in shapes],
        scratch_shapes=[pltpu.VMEM(*shape) for shape in scratch],
        compiler_params=pltpu.CompilerParams(vmem_limit_bytes=mib * 2**20),
        cost_estimate=pl.CostEstimate(flops=flops, transcendentals=0, bytes_accessed=1),
        name=name,
    )(*smem, *vmem)


def permute_columns(values, columns_at, gain=None, dtype=F32):
    rows, width = values.shape
    tile = 256

    def kernel(values_ref, at_ref, *refs):
        out_ref = refs[0] if gain is None else refs[1]

        @pl.loop(0, width // tile)
        def _(i):
            at = pl.ds(pl.multiple_of(i * tile, tile), tile)
            source = lax.broadcasted_iota(jnp.int32, (width, tile), 0)
            onehot = (source == at_ref[:, at]).astype(F32).astype(BF)
            out_ref[:, at] = dot(values_ref[...], onehot).astype(dtype)

        if gain is not None:

            @pl.loop(0, rows // 128)
            def _(i):
                at = pl.ds(pl.multiple_of(i * 128, 128), 128)
                refs[2][at, :] = normed(out_ref[at, :], refs[0][...])

    ins = [values, columns_at[None]] + ([] if gain is None else [gain[None]])
    shapes = [((rows, width), dtype)] + ([] if gain is None else [((rows, width), BF)])
    outs = call(kernel, [], ins, shapes, [], "permute_columns")
    return outs[0] if gain is None else outs


def hold(value, *others):
    def kernel(*refs):
        pass

    return pl.pallas_call(
        kernel,
        in_specs=[pl.BlockSpec(memory_space=pl.ANY)] * (1 + len(others)),
        out_specs=pl.BlockSpec(memory_space=pl.ANY),
        out_shape=jax.ShapeDtypeStruct(value.shape, value.dtype),
        input_output_aliases={0: 0},
        cost_estimate=pl.CostEstimate(flops=10**11, transcendentals=0, bytes_accessed=10**8),
        name="hold",
    )(value, *others)


def attend(place, lengths, chosen, joined, x_last, w_last, tables, out_in, sizes, shares):
    seq_len, columns = joined.shape
    heads, kv_heads, head_dim = sizes
    group = heads // kv_heads
    q_cols, k_cols = heads * head_dim, kv_heads * head_dim
    half = head_dim // 2
    wide = (q_cols + k_cols + 127) // 128 * 128
    width = w_last[0].shape[0]
    model_dim = out_in.shape[1]
    share = seq_len // len(shares)
    slots = chosen.shape[0] // 2
    tile = 128

    def kernel(
        place_ref, length_ref, chosen_ref, joined_ref, x_ref, cos_ref, sin_ref, out_in_ref, *refs
    ):
        w_refs = refs[: len(w_last)]
        leaving_ref, staying_ref, *boxes, cache_ref, qk, v, context = refs[len(w_last) :]
        tp, length = place_ref[0], length_ref[0]
        lane = lax.broadcasted_iota(jnp.int32, (tile, wide), 1)
        first = lax.rem(lane, head_dim) < half
        for t in range(seq_len // tile):
            at = slice(t * tile, (t + 1) * tile)
            rows = joined_ref[at, :]
            for i, w_ref in enumerate(w_refs):
                rows = rows + dot(x_ref[at, i * width : (i + 1) * width], w_ref[...])
            head = rows[:, :wide]
            ahead = pltpu.roll(head, wide - half, 1)
            behind = pltpu.roll(head, half, 1)
            cosine, sine = (
                jnp.concatenate([ref[at, :]] * (wide // half + 1), axis=1)[:, :wide]
                for ref in (cos_ref, sin_ref)
            )
            turned = head * cosine + jnp.where(first, -ahead, behind) * sine
            qk[at, :] = turned.astype(BF)
            v[at, :] = rows[:, q_cols + k_cols :].astype(BF)
            slot = t * tile + lax.broadcasted_iota(jnp.int32, (tile, 1), 0)
            live = (slot < length).astype(F32)
            cache_ref[at, :k_cols] = (turned[:, q_cols : q_cols + k_cols] * live).astype(BF)
            cache_ref[at, k_cols:] = (rows[:, q_cols + k_cols :] * live).astype(BF)
        for i in range(chosen.shape[0]):
            page = cache_ref[pl.ds(pl.multiple_of(chosen_ref[i] * PAGE, PAGE), PAGE), :]
            boxes[i // slots][i % slots * PAGE : (i % slots + 1) * PAGE, :] = page
        for k in range(kv_heads):
            key_at = q_cols + k * head_dim
            for t in range(seq_len // tile):
                at = slice(t * tile, (t + 1) * tile)
                count = (t + 1) * tile
                q = jnp.concatenate(
                    [
                        qk[at, (k * group + g) * head_dim : (k * group + g + 1) * head_dim]
                        for g in range(group)
                    ],
                    axis=0,
                )
                scores = lax.dot_general(
                    q,
                    qk[:count, key_at : key_at + head_dim],
                    (((1,), (1,)), ((), ())),
                    preferred_element_type=F32,
                ) * head_dim ** (-0.5)
                shape = (tile, count)
                slot = t * tile + lax.broadcasted_iota(jnp.int32, shape, 0)
                key = lax.broadcasted_iota(jnp.int32, shape, 1)
                allowed = (key <= slot) & (key < length)
                scores = scores.reshape(group, tile, count)
                scores = jnp.where(allowed[None], scores, -1e30)
                top = jnp.max(scores, axis=-1, keepdims=True)
                weight = jnp.exp(scores - top)
                probs = (weight / jnp.sum(weight, axis=-1, keepdims=True)).astype(BF)
                mixed = dot(
                    probs.reshape(group * tile, count), v[:count, k * head_dim : (k + 1) * head_dim]
                ).astype(BF)
                for g in range(group):
                    h = k * group + g
                    context[at, h * head_dim : (h + 1) * head_dim] = mixed[
                        g * tile : (g + 1) * tile
                    ]
        for i, s in enumerate(shares):
            block = context[pl.ds(pl.multiple_of((tp ^ s) * share, share), share), :]
            product = dot(block, out_in_ref[...])
            j = i % (len(shares) // 2)
            if i < len(shares) // 2:
                staying_ref[j * share : (j + 1) * share, :] = product
            else:
                leaving_ref[j * share : (j + 1) * share, :] = product.astype(BF)

    return call(
        kernel,
        [place, lengths, chosen],
        [joined, x_last, *tables, out_in, *w_last],
        [
            ((seq_len // 2, model_dim), BF),
            ((seq_len // 2, model_dim), F32),
        ]
        + [((slots * PAGE, 2 * k_cols), BF)] * 2,
        [((seq_len, 2 * k_cols), BF), ((seq_len, wide), BF), ((seq_len, k_cols), BF), ((seq_len, q_cols), BF)],
        "attend",
    )


def assemble(blocks):
    each, columns = blocks[0].shape
    count = len(blocks)

    def kernel(*refs):
        for i in range(count):
            refs[count][i * each : (i + 1) * each, :] = refs[i][...]

    return call(kernel, [], blocks, [((count * each, columns), BF)], [], "assemble", 24)[0]


def rows_product(pieces, weight, at, count, base=None, dtype=F32):
    columns = weight.shape[1]
    tile = 128

    def kernel(*refs):
        weight_ref = refs[len(pieces)]

        @pl.loop(0, count // tile)
        def _(i):
            out = pl.ds(pl.multiple_of(i * tile, tile), tile)
            total = 0.0 if base is None else refs[len(pieces) + 1][out, :]
            begin = at
            for (piece, first), ref in zip(pieces, refs):
                end = begin + piece.shape[1]
                source = pl.ds(pl.multiple_of(first + i * tile, tile), tile)
                total = total + dot(ref[source, :], weight_ref[begin:end, :])
                begin = end
            refs[-1][out, :] = total.astype(dtype)

    ins = [piece for piece, _ in pieces] + [weight] + ([] if base is None else [base])
    return call(kernel, [], ins, [((count, columns), dtype)], [], "rows_product", 24)[0]


def add_share(staying, arrived, extra):
    rows, columns = staying.shape
    half = rows // 2

    def kernel(staying_ref, arrived_ref, extra_ref, keep_ref, send_ref):
        keep_ref[...] = (
            staying_ref[:half, :] + arrived_ref[:half, :].astype(F32) + extra_ref[...]
        )
        send_ref[...] = (staying_ref[half:, :] + arrived_ref[half:, :].astype(F32)).astype(BF)

    return call(
        kernel,
        [],
        [staying, arrived, extra],
        [((half, columns), F32), ((half, columns), BF)],
        [],
        "add_share",
        24,
    )


def norm_share(keep, arrived, gain):
    rows, columns = keep.shape
    step = columns * PAIR // gain.shape[0]

    def kernel(keep_ref, arrived_ref, gain_ref, resid_ref, norm_ref, turned_ref):
        resid = keep_ref[...] + arrived_ref[...].astype(F32)
        resid_ref[...] = resid
        norm = normed(resid, gain_ref[...])
        norm_ref[...] = norm
        for i in range(columns // step):
            at, source = i * step, (i ^ 1) * step
            turned_ref[:, at : at + step] = norm[:, source : source + step]

    shapes = [((rows, columns), F32)] + [((rows, columns), BF)] * 2
    return call(
        kernel, [], [keep, arrived, gain.reshape(1, columns)], shapes, [], "norm_share", 24
    )


def pick_pages(source, pages):
    count = source.shape[0]

    def kernel(source_ref, *refs):
        for p in range(count):
            for i, ref in enumerate(refs[:-1]):

                @pl.when(source_ref[p] == i)
                def _(p=p, ref=ref):
                    refs[-1][p] = ref[...]

    shapes = [((count, *pages[0].shape), BF)]
    return call(kernel, [source], pages, shapes, [], "pick_pages", 16, 5 * 10**9)[0]


def class_rows(place, weight):
    rows, columns = weight.shape
    half = rows // 2

    def kernel(place_ref, weight_ref, *outs):
        for k in range(2):
            begin = pl.multiple_of((place_ref[1] ^ k) * half, 16)
            outs[k][...] = weight_ref[pl.ds(begin, half), :]

    return call(kernel, [place], [weight], [((half, columns), BF)] * 2, [], "class_rows")


def gated(tokens, weight, parts=1):
    rows = tokens.shape[0] // parts
    size = weight.shape[1] // 2
    tile = 256

    def kernel(tokens_ref, weight_ref, *outs):
        for p, out_ref in enumerate(outs):

            @pl.loop(0, rows // tile)
            def _(i, p=p, out_ref=out_ref):
                source = pl.ds(pl.multiple_of(p * rows + i * tile, tile), tile)
                projected = dot(tokens_ref[source, :], weight_ref[...])
                gate, up = projected[:, :size], projected[:, size:]
                out_ref[pl.ds(pl.multiple_of(i * tile, tile), tile), :] = (
                    gate / (1.0 + jnp.exp(-gate)) * up
                ).astype(BF)

    shapes = [((rows, size), BF)] * parts
    return call(kernel, [], [tokens, weight], shapes, [], "gated", 24)


def body(
    tokens,
    lengths,
    page_slot,
    trainer_layout,
    trainer_qkv,
    trainer_gateup,
    attn_gain,
    ffn_gain,
    out_proj,
    down_proj,
):
    n_tp = lax.axis_size("tp")
    n_req = lax.axis_size("req")
    devices = n_tp * n_req
    req = lax.axis_index("req")
    tp = lax.axis_index("tp")
    rows_each = trainer_qkv.shape[0]
    seq_len, model_dim = tokens.shape
    head_dim = HD
    local_heads = out_proj.shape[0] // head_dim
    group_cols = trainer_qkv.shape[1] // n_tp
    local_kv = (group_cols // head_dim - local_heads) // 2
    group = local_heads // local_kv
    q_cols = local_heads * head_dim
    k_cols = local_kv * head_dim
    ff_local = down_proj.shape[0]
    share = seq_len // n_tp

    def swap(value, req_mask, tp_mask):
        pairs = [(d, d ^ (req_mask * n_tp + tp_mask)) for d in range(devices)]
        return lax.ppermute(value, ("req", "tp"), pairs)

    def pick(stack, index):
        return lax.dynamic_index_in_dim(stack, index, 0, keepdims=False)

    def sync(values):
        return lax.optimization_barrier(values)

    halves = 2
    units = ff_local // halves
    chunks = list(CHUNKS) + [units - sum(CHUNKS)]
    bits = [1 << k for k in range(16) if 1 << k < n_tp]
    evens = list(range(2, n_req, 2))
    zbits = [1 << k for k in range(1, 16) if 1 << k < n_req]
    singles = [r for r in evens if r & (r - 1) == 0]
    doubles = [r for r in evens if r & (r - 1)]
    plain = [r for r in evens if not r & PAIR]
    crossed = [r for r in evens if r & PAIR and r != PAIR]

    def spread_z(held, group):
        for r in group:
            bit = r & -r
            held[r] = swap(held[r ^ bit], bit, 0)

    def spread_class(held, mine, other, group):
        for r in group:
            if r == PAIR:
                held[r] = swap(other, PAIR, 0)
                continue
            rest = r & ~PAIR
            bit = 1 << (rest.bit_length() - 1)
            held[r] = swap(held[r ^ bit] if r != bit else mine, bit, 0)

    place = jnp.stack([tp, (req // PAIR) % 2])
    qkv_split = split_qkv(place, trainer_qkv, n_tp)
    half = head_dim // 2
    freq = theta_base ** (-jnp.arange(half, dtype=F32) * 2.0 / head_dim)
    angles = jnp.arange(seq_len, dtype=F32)[:, None] * freq[None, :]
    tables = (jnp.cos(angles), jnp.sin(angles))
    trainer_gateup, qkv_split = sync((trainer_gateup, qkv_split))
    gu_own, gu_odd = split_gateup(place, trainer_gateup, n_tp, halves, chunks)
    qkv_split = [qkv_split[0]] + [swap(qkv_split[s], 0, s) for s in range(1, n_tp)]
    st = sync(
        dict(
            qkv_split=qkv_split,
            gu_own=gu_own,
            gu_odd=gu_odd,
            tokens=tokens,
            layout=trainer_layout,
            tables=tables,
        )
    )

    tokens, trainer_layout, tables = st["tokens"], st["layout"], st["tables"]
    gu_own, gu_near = st["gu_own"], swap(st["gu_odd"], 0, 1)
    qkv_own = join_qkv(place, st["qkv_split"])
    qkv = {0: qkv_own}
    spread_z(qkv, singles)
    qkv[1] = swap(qkv_own, 1, 0)
    far = list(pack_far(place, gu_own, gu_near, chunks))
    tokens, far = sync((tokens, far))

    def over_y(value):
        moved = [swap(value[f], 0, 2 * f + 2) for f in range(n_tp // 2 - 1)]
        return jnp.stack(moved) if len(moved) > 1 else moved[0][None]

    blocks = [join_gateup(place, gu_own, gu_near, over_y(far[0]), 0)]
    order = jnp.arange(n_req, dtype=jnp.int32) ^ req
    shards = (order[:, None] * n_tp + jnp.arange(n_tp, dtype=jnp.int32)[None, :]).reshape(-1)
    blocks_at = trainer_layout[shards]
    columns_at = (
        blocks_at[:, None] * rows_each + jnp.arange(rows_each, dtype=jnp.int32)[None, :]
    ).reshape(-1)
    columns_back = (
        jnp.argmax(
            blocks_at[None, :] == jnp.arange(devices, dtype=jnp.int32)[:, None], axis=1
        ).astype(jnp.int32)[:, None]
        * rows_each
        + jnp.arange(rows_each, dtype=jnp.int32)[None, :]
    ).reshape(-1)
    gain_in = attn_gain.reshape(devices, rows_each)[blocks_at].reshape(-1)
    tokens_in, x_norm = permute_columns(tokens, columns_at, gain_in)
    st = sync(
        dict(
            qkv=qkv,
            far=far[1],
            blocks=blocks,
            gu_own=gu_own,
            gu_near=gu_near,
            x_norm=x_norm,
            tokens_in=tokens_in,
            onehot_at=columns_at,
            out_proj=out_proj,
            down_proj=down_proj,
            page_slot=page_slot,
            ffn_gain=ffn_gain,
        )
    )

    qkv, far, x_norm, tokens_in = st["qkv"], st["far"], st["x_norm"], st["tokens_in"]
    columns_at, page_slot = st["onehot_at"], st["page_slot"]
    blocks = list(st["blocks"])
    blocks.append(join_gateup(place, st["gu_own"], st["gu_near"], over_y(far), 2 * chunks[0]))
    spread_z(qkv, doubles)
    for r in singles[::-1]:
        qkv[r ^ 1] = swap(qkv[r], 1, 0)
    gu = [dict() for _ in chunks]
    spread_class(gu[0], *blocks[0], plain)
    out_in = permute_columns(st["out_proj"], columns_at, dtype=BF)
    down_rel = class_rows(place, st["down_proj"])
    ffn_gain_in = st["ffn_gain"].reshape(devices, rows_each)[blocks_at].reshape(-1)
    n_pages = seq_len // PAGE
    holders = lax.dynamic_slice_in_dim(page_slot, req * n_pages, n_pages, 0) // n_pages
    page_bits = [PAIR, 1] + [bit for bit in zbits if bit != PAIR]
    at_slot = [
        sum(bit for k, bit in enumerate(reversed(page_bits)) if (i >> k) & 1)
        for i in range(n_req)
    ]
    relative = jnp.asarray(at_slot, jnp.int32) ^ req
    chosen = jnp.argmax(holders[None, :] == relative[:, None], axis=1)
    targets = req * n_pages + jnp.arange(n_pages, dtype=jnp.int32)
    source = jnp.argmax(page_slot[None, :] == targets[:, None], axis=1) // n_pages
    arrival = [0]
    for bit in page_bits:
        arrival = arrival + [r ^ bit for r in arrival]
    arrival = jnp.asarray(arrival, jnp.int32) ^ req
    source = jnp.argmax(arrival[None, :] == source[:, None], axis=1)
    tokens_share = lax.dynamic_slice_in_dim(tokens_in, tp * share, share, 0)
    st = sync(
        dict(
            qkv=qkv,
            gu=gu,
            blocks=blocks,
            x_norm=x_norm,
            out_in=out_in,
            down_rel=down_rel,
            ffn_gain_in=ffn_gain_in,
            pages=(chosen, source),
            tokens_share=tokens_share,
        )
    )

    qkv, gu, blocks, x_norm, out_in = (st[k] for k in ("qkv", "gu", "blocks", "x_norm", "out_in"))
    chosen, source = st["pages"]
    tokens_share = st["tokens_share"]
    down_rel, ffn_gain_in = st["down_rel"], st["ffn_gain_in"]
    spread_class(gu[0], *blocks[0], [PAIR])
    spread_class(gu[1], *blocks[1], plain)
    for r in doubles:
        qkv[r ^ 1] = swap(qkv[r], 1, 0)
    gu[1][0] = blocks[1][0]
    gu[1][1] = swap(blocks[1][0], 1, 0)
    width = model_dim // n_req
    first = [0, 1] + [r | j for r in singles for j in (0, 1)]
    last = [r | j for r in doubles for j in (0, 1)]

    def part(rs):
        return dot(
            jnp.concatenate([x_norm[:, r * width : (r + 1) * width] for r in rs], axis=1),
            jnp.concatenate([qkv[r] for r in rs], axis=0),
        )

    joined = part(first)
    st = sync(dict(qkv=qkv, gu=gu, blocks=blocks, joined=joined, x_norm=x_norm))

    qkv, gu, blocks, x_norm = (st[k] for k in ("qkv", "gu", "blocks", "x_norm"))
    spread_class(gu[0], *blocks[0], crossed)
    spread_class(gu[1], *blocks[1], [PAIR])
    gu[0][0] = blocks[0][0]
    gu[0][1] = swap(blocks[0][0], 1, 0)
    for r in plain:
        gu[0][r ^ 1] = swap(gu[0][r], 1, 0)
    shares = sorted(range(n_tp), key=lambda s: [(s >> k) & 1 for k in range(len(bits))])
    leaving, staying, *box = attend(
        place,
        lengths,
        chosen.astype(jnp.int32),
        st["joined"],
        jnp.concatenate([x_norm[:, r * width : (r + 1) * width] for r in last], axis=1),
        [qkv[r] for r in last],
        tables,
        out_in,
        (local_heads, local_kv, head_dim),
        shares,
    )
    st = sync(dict(gu=gu, leaving=leaving, staying=staying, box=box))

    gu, box = st["gu"], st["box"]
    keep, send = add_share(st["staying"], swap(st["leaving"], 0, bits[0]), tokens_share)
    arrived = swap(send, 0, bits[1])
    spread_class(gu[1], None, None, crossed)
    gu[0][PAIR ^ 1] = swap(gu[0][PAIR], 1, 0)
    for r in plain:
        gu[1][r ^ 1] = swap(gu[1][r], 1, 0)

    def page_parts(box):
        half = box[0].shape[0] // 2
        return [pages[:half] for pages in box], jnp.concatenate(
            [pages[half:] for pages in box], axis=0
        )

    def page_step(parts, bit):
        kept, leaving = parts
        half = kept[0].shape[0]
        moved = swap(leaving, bit, 0)
        return kept + [moved[at : at + half] for at in range(0, leaving.shape[0], half)]

    late = crossed[0]
    box = [box[0], swap(box[1], page_bits[0], 0)]
    gu[1][late] = hold(gu[1][late], box[1], gu[0][PAIR ^ 1], *[gu[1][r ^ 1] for r in plain])
    resid_in, h_share, h_leaving = norm_share(
        keep, arrived, ffn_gain_in.reshape(n_req, model_dim // n_req)
    )
    st = sync(dict(gu=gu, h=(h_share, h_leaving), resid_in=resid_in, box=box))

    gu, resid_in = st["gu"], st["resid_in"]
    h_share, h_leaving = st["h"]
    cross = n_tp // 2
    own = (h_share, swap(h_share, 0, cross))
    theirs = (swap(h_leaving, PAIR, 0), swap(h_leaving, PAIR, cross))
    for r in crossed:
        gu[0][r ^ 1] = swap(gu[0][r], 1, 0)
    gu[1][PAIR ^ 1] = swap(gu[1][PAIR], 1, 0)
    coarse = resid_in.astype(BF)
    fine = (resid_in - coarse.astype(F32)).astype(BF)
    terms = permute_columns(jnp.concatenate([coarse, fine], axis=0), columns_back)
    st = sync(dict(gu=gu, own=own, theirs=theirs, terms=terms, box=page_parts(st["box"])))

    def whole(rows):
        for bit in bits[:-1]:
            rows = jnp.concatenate([rows, swap(rows, 0, bit)], axis=0)
        return rows

    gu, box = st["gu"], st["box"]
    resid = st["terms"][:share] + st["terms"][share:]
    h_own, h_theirs = (whole(jnp.concatenate(st[k], axis=0)) for k in ("own", "theirs"))
    for r in crossed:
        gu[1][r ^ 1] = swap(gu[1][r], 1, 0)
    weight = assemble([gu[0][r] for r in range(n_req)])
    theirs = gated(h_theirs, weight, 2)
    kept = gated(h_own, weight)
    st = sync(dict(gu=gu[1], h=(h_own, h_theirs), hidden=(kept, theirs), resid=resid, box=box))

    resid, box = st["resid"], st["box"]
    h_own, h_theirs = st["h"]
    kept, theirs = st["hidden"]
    returned = [swap(theirs[0], PAIR, 0)]
    second, _ = sync((theirs[1], returned[0]))
    returned.append(swap(second, PAIR, 0))
    weight = assemble([st["gu"][r] for r in range(n_req)])
    theirs = gated(h_theirs, weight)
    h_own, theirs = sync((h_own, theirs))
    kept = list(kept) + list(gated(h_own, weight))
    rows = seq_len // 2
    product = []
    for i in range(2):
        part = rows_product([(piece, i * rows) for piece in kept], down_rel[0], 0, rows)
        product.append(rows_product([(returned[i], 0)], down_rel[1], 0, rows, part))
    box = page_parts(page_step(box, page_bits[1]))
    returned, box, product = sync((swap(theirs[0], PAIR, 0), box, product))
    leaving = rows_product([(returned, rows)], down_rel[1], chunks[0], rows, product[1], BF)
    arrived = swap(leaving, 0, bits[0])
    staying = rows_product([(returned, 0)], down_rel[1], chunks[0], rows, product[0])
    keep, send = add_share(staying, arrived, resid)
    box = page_step(box, page_bits[2])
    for bit in page_bits[3:]:
        box = page_step(page_parts(box), bit)
    share_slots = tp * share + jnp.arange(share, dtype=jnp.int32)
    live_share = (share_slots < lengths[0]).astype(F32)
    layer_out = ((keep + swap(send, 0, bits[1]).astype(F32)) * live_share[:, None]).astype(BF)
    kv_cache = pick_pages(source.astype(jnp.int32), box)
    return (layer_out, kv_cache)


def solution(mesh):
    return jax.shard_map(
        body,
        mesh=mesh,
        in_specs=(
            P("req", None),
            P("req"),
            P(),
            P(),
            P(("req", "tp"), None),
            P(("req", "tp"), None),
            P(),
            P(),
            P("tp", None),
            P("tp", None),
        ),
        out_specs=(P(("req", "tp"), None), P("req", None, "tp")),
        check_vma=False,
    )
```

```python
import jax
import jax.numpy as jnp
from jax import lax
from jax.experimental import pallas as pl
from jax.experimental.pallas import tpu as pltpu
from jax.sharding import PartitionSpec as P

HD = 80
PAGE = 128
BF = jnp.bfloat16
F32 = jnp.float32

eps_norm = 1e-05
theta_base = 10000.0

PAIR = 2
CHUNKS = (512,)


def normed(values, gain):
    scale = lax.rsqrt(jnp.mean(values * values, axis=-1, keepdims=True) + eps_norm)
    return (values * scale * gain).astype(BF)


def dot(a, b):
    return jnp.dot(a, b, preferred_element_type=F32)


def on_device(kernel, place, ins, shapes, vmem_mib, name):
    def run(place_ref, *refs):
        n_in, n_out = len(ins), len(shapes)
        outs, bufs, sems = refs[n_in : n_in + n_out], refs[n_in + n_out : -1], refs[-1]
        kernel(place_ref, *refs[:n_in], *bufs)
        copies = [pltpu.make_async_copy(bufs[i], outs[i], sems.at[i]) for i in range(n_out)]
        for copy in copies:
            copy.start()
        for copy in copies:
            copy.wait()

    return pl.pallas_call(
        run,
        in_specs=[pl.BlockSpec(memory_space=pltpu.SMEM)]
        + [pl.BlockSpec(memory_space=pltpu.VMEM)] * len(ins),
        out_specs=[pl.BlockSpec(memory_space=pltpu.HBM)] * len(shapes),
        out_shape=[jax.ShapeDtypeStruct(shape, BF) for shape in shapes],
        scratch_shapes=[pltpu.VMEM(shape, BF) for shape in shapes]
        + [pltpu.SemaphoreType.DMA((len(shapes),))],
        compiler_params=pltpu.CompilerParams(vmem_limit_bytes=vmem_mib * 2**20),
        cost_estimate=pl.CostEstimate(flops=1, transcendentals=0, bytes_accessed=1),
        name=name,
    )(place, *ins)


def split_qkv(place, shard, n_tp):
    rows, columns = shard.shape
    width = columns // n_tp

    def kernel(place_ref, shard_ref, *bufs):
        tp = place_ref[0]
        for s in range(n_tp):
            for g in range(n_tp):

                @pl.when((tp ^ s) == g)
                def _(s=s, g=g):
                    bufs[s][...] = shard_ref[:, g * width : (g + 1) * width].astype(BF)

    return on_device(kernel, place, [shard], [(rows, width)] * n_tp, 60, "split_qkv")


def split_gateup(place, shard, n_tp, halves, chunks):
    rows, columns = shard.shape
    width = columns // n_tp
    units = width // 2 // halves

    def kernel(place_ref, shard_ref, *bufs):
        tp = place_ref[0]
        for s in range(n_tp):
            begin = pl.multiple_of((tp ^ s) * width, 128)
            group = shard_ref[:, pl.ds(begin, width)].astype(BF)
            for q in range(halves):
                start = q * units
                edge = 0
                for size in chunks:
                    up = width // 2 + start
                    bufs[s % 2][s // 2, q, :, edge : edge + 2 * size] = jnp.concatenate(
                        [group[:, start : start + size], group[:, up : up + size]], axis=1
                    )
                    start += size
                    edge += 2 * size

    shapes = [(n_tp // 2, halves, rows, 2 * units)] * 2
    return on_device(kernel, place, [shard], shapes, 60, "split_gateup")


def pack_far(place, own, near, chunks):
    n_far, halves, rows, _ = own.shape
    n_far -= 1

    def kernel(place_ref, own_ref, near_ref, *bufs):
        edge = 0
        for c, size in enumerate(chunks):
            for f in range(n_far):
                bufs[c][f, 0] = own_ref[f + 1, :, :, edge : edge + 2 * size]
                bufs[c][f, 1] = near_ref[f + 1, :, :, edge : edge + 2 * size]
            edge += 2 * size

    shapes = [(n_far, 2, halves, rows, 2 * size) for size in chunks]
    return on_device(kernel, place, [own, near], shapes, 60, "pack_far")


def join_qkv(place, parts):
    rows, columns = parts[0].shape
    n_tp = len(parts)

    def kernel(place_ref, *refs):
        for s in range(n_tp):
            refs[n_tp][place_ref[0] ^ s] = refs[s][...]

    out = on_device(kernel, place, parts, [(n_tp, rows, columns)], 60, "join_qkv")[0]
    return out.reshape(n_tp * rows, columns)


def join_gateup(place, own, near, far, start):
    n_far, _, halves, rows, columns = far.shape
    n_tp = 2 * n_far + 2

    def kernel(place_ref, own_ref, near_ref, far_ref, *bufs):
        tp, mine = place_ref[0], place_ref[1]
        for k in range(2):
            bufs[k][tp] = own_ref[0, mine ^ k, :, start : start + columns]
            bufs[k][tp ^ 1] = near_ref[0, mine ^ k, :, start : start + columns]
            for f in range(n_far):
                for j in range(2):
                    bufs[k][tp ^ (2 * f + 2 + j)] = far_ref[f, j, mine ^ k]

    shapes = [(n_tp, rows, columns)] * 2
    outs = on_device(kernel, place, [own, near, far], shapes, 60, "join_gateup")
    return [out.reshape(n_tp * rows, columns) for out in outs]


SMEM = pl.BlockSpec(memory_space=pltpu.SMEM)
VMEM = pl.BlockSpec(memory_space=pltpu.VMEM)


def call(kernel, smem, vmem, shapes, scratch, name, mib=48, flops=1):
    return pl.pallas_call(
        kernel,
        in_specs=[SMEM] * len(smem) + [VMEM] * len(vmem),
        out_specs=[VMEM] * len(shapes),
        out_shape=[jax.ShapeDtypeStruct(*shape) for shape in shapes],
        scratch_shapes=[pltpu.VMEM(*shape) for shape in scratch],
        compiler_params=pltpu.CompilerParams(vmem_limit_bytes=mib * 2**20),
        cost_estimate=pl.CostEstimate(flops=flops, transcendentals=0, bytes_accessed=1),
        name=name,
    )(*smem, *vmem)


def permute_columns(values, columns_at, gain=None, dtype=F32):
    rows, width = values.shape
    tile = 256

    def kernel(values_ref, at_ref, *refs):
        out_ref = refs[0] if gain is None else refs[1]

        @pl.loop(0, width // tile)
        def _(i):
            at = pl.ds(pl.multiple_of(i * tile, tile), tile)
            source = lax.broadcasted_iota(jnp.int32, (width, tile), 0)
            onehot = (source == at_ref[:, at]).astype(F32).astype(BF)
            out_ref[:, at] = dot(values_ref[...], onehot).astype(dtype)

        if gain is not None:

            @pl.loop(0, rows // 128)
            def _(i):
                at = pl.ds(pl.multiple_of(i * 128, 128), 128)
                refs[2][at, :] = normed(out_ref[at, :], refs[0][...])

    ins = [values, columns_at[None]] + ([] if gain is None else [gain[None]])
    shapes = [((rows, width), dtype)] + ([] if gain is None else [((rows, width), BF)])
    outs = call(kernel, [], ins, shapes, [], "permute_columns")
    return outs[0] if gain is None else outs


def hold(value, *others):
    def kernel(*refs):
        pass

    return pl.pallas_call(
        kernel,
        in_specs=[pl.BlockSpec(memory_space=pl.ANY)] * (1 + len(others)),
        out_specs=pl.BlockSpec(memory_space=pl.ANY),
        out_shape=jax.ShapeDtypeStruct(value.shape, value.dtype),
        input_output_aliases={0: 0},
        cost_estimate=pl.CostEstimate(flops=10**11, transcendentals=0, bytes_accessed=10**8),
        name="hold",
    )(value, *others)


def attend(place, lengths, chosen, joined, x_last, w_last, tables, out_in, sizes, shares):
    seq_len, columns = joined.shape
    heads, kv_heads, head_dim = sizes
    group = heads // kv_heads
    q_cols, k_cols = heads * head_dim, kv_heads * head_dim
    half = head_dim // 2
    wide = (q_cols + k_cols + 127) // 128 * 128
    width = w_last[0].shape[0]
    model_dim = out_in.shape[1]
    share = seq_len // len(shares)
    slots = chosen.shape[0] // 2
    tile = 128

    def kernel(
        place_ref, length_ref, chosen_ref, joined_ref, x_ref, cos_ref, sin_ref, out_in_ref, *refs
    ):
        w_refs = refs[: len(w_last)]
        leaving_ref, staying_ref, *boxes, cache_ref, qk, v, context = refs[len(w_last) :]
        tp, length = place_ref[0], length_ref[0]
        lane = lax.broadcasted_iota(jnp.int32, (tile, wide), 1)
        first = lax.rem(lane, head_dim) < half
        for t in range(seq_len // tile):
            at = slice(t * tile, (t + 1) * tile)
            rows = joined_ref[at, :]
            for i, w_ref in enumerate(w_refs):
                rows = rows + dot(x_ref[at, i * width : (i + 1) * width], w_ref[...])
            head = rows[:, :wide]
            ahead = pltpu.roll(head, wide - half, 1)
            behind = pltpu.roll(head, half, 1)
            cosine, sine = (
                jnp.concatenate([ref[at, :]] * (wide // half + 1), axis=1)[:, :wide]
                for ref in (cos_ref, sin_ref)
            )
            turned = head * cosine + jnp.where(first, -ahead, behind) * sine
            qk[at, :] = turned.astype(BF)
            v[at, :] = rows[:, q_cols + k_cols :].astype(BF)
            slot = t * tile + lax.broadcasted_iota(jnp.int32, (tile, 1), 0)
            live = (slot < length).astype(F32)
            cache_ref[at, :k_cols] = (turned[:, q_cols : q_cols + k_cols] * live).astype(BF)
            cache_ref[at, k_cols:] = (rows[:, q_cols + k_cols :] * live).astype(BF)
        for i in range(chosen.shape[0]):
            page = cache_ref[pl.ds(pl.multiple_of(chosen_ref[i] * PAGE, PAGE), PAGE), :]
            at, side = i % slots // 2 * PAGE, i % 2 * 2 * k_cols
            boxes[i // slots][at : at + PAGE, side : side + 2 * k_cols] = page
        for k in range(kv_heads):
            key_at = q_cols + k * head_dim
            for t in range(seq_len // tile):
                at = slice(t * tile, (t + 1) * tile)
                count = (t + 1) * tile
                q = jnp.concatenate(
                    [
                        qk[at, (k * group + g) * head_dim : (k * group + g + 1) * head_dim]
                        for g in range(group)
                    ],
                    axis=0,
                )
                scores = lax.dot_general(
                    q,
                    qk[:count, key_at : key_at + head_dim],
                    (((1,), (1,)), ((), ())),
                    preferred_element_type=F32,
                ) * head_dim ** (-0.5)
                shape = (tile, count)
                slot = t * tile + lax.broadcasted_iota(jnp.int32, shape, 0)
                key = lax.broadcasted_iota(jnp.int32, shape, 1)
                allowed = (key <= slot) & (key < length)
                scores = scores.reshape(group, tile, count)
                scores = jnp.where(allowed[None], scores, -1e30)
                top = jnp.max(scores, axis=-1, keepdims=True)
                weight = jnp.exp(scores - top)
                probs = (weight / jnp.sum(weight, axis=-1, keepdims=True)).astype(BF)
                mixed = dot(
                    probs.reshape(group * tile, count), v[:count, k * head_dim : (k + 1) * head_dim]
                ).astype(BF)
                for g in range(group):
                    h = k * group + g
                    context[at, h * head_dim : (h + 1) * head_dim] = mixed[
                        g * tile : (g + 1) * tile
                    ]
        for i, s in enumerate(shares):
            block = context[pl.ds(pl.multiple_of((tp ^ s) * share, share), share), :]
            product = dot(block, out_in_ref[...])
            j = i % (len(shares) // 2)
            if i < len(shares) // 2:
                staying_ref[j * share : (j + 1) * share, :] = product
            else:
                leaving_ref[j * share : (j + 1) * share, :] = product.astype(BF)

    return call(
        kernel,
        [place, lengths, chosen],
        [joined, x_last, *tables, out_in, *w_last],
        [
            ((seq_len // 2, model_dim), BF),
            ((seq_len // 2, model_dim), F32),
        ]
        + [((slots // 2 * PAGE, 4 * k_cols), BF)] * 2,
        [((seq_len, 2 * k_cols), BF), ((seq_len, wide), BF), ((seq_len, k_cols), BF), ((seq_len, q_cols), BF)],
        "attend",
    )


def assemble(blocks, flops=1):
    each, columns = blocks[0].shape
    count = len(blocks)

    def kernel(*refs):
        for i in range(count):
            refs[count][i * each : (i + 1) * each, :] = refs[i][...]

    shapes = [((count * each, columns), BF)]
    return call(kernel, [], blocks, shapes, [], "assemble", 24, flops)[0]


def rows_product(pieces, weight, at, count, base=None, dtype=F32):
    columns = weight.shape[1]
    tile = 128

    def kernel(*refs):
        weight_ref = refs[len(pieces)]

        @pl.loop(0, count // tile)
        def _(i):
            out = pl.ds(pl.multiple_of(i * tile, tile), tile)
            total = 0.0 if base is None else refs[len(pieces) + 1][out, :]
            begin = at
            for (piece, first), ref in zip(pieces, refs):
                end = begin + piece.shape[1]
                source = pl.ds(pl.multiple_of(first + i * tile, tile), tile)
                total = total + dot(ref[source, :], weight_ref[begin:end, :])
                begin = end
            refs[-1][out, :] = total.astype(dtype)

    ins = [piece for piece, _ in pieces] + [weight] + ([] if base is None else [base])
    return call(kernel, [], ins, [((count, columns), dtype)], [], "rows_product", 24)[0]


def add_share(staying, arrived, extra):
    rows, columns = staying.shape
    half = rows // 2

    def kernel(staying_ref, arrived_ref, extra_ref, keep_ref, send_ref):
        keep_ref[...] = (
            staying_ref[:half, :] + arrived_ref[:half, :].astype(F32) + extra_ref[...]
        )
        send_ref[...] = (staying_ref[half:, :] + arrived_ref[half:, :].astype(F32)).astype(BF)

    return call(
        kernel,
        [],
        [staying, arrived, extra],
        [((half, columns), F32), ((half, columns), BF)],
        [],
        "add_share",
        24,
    )


def norm_share(keep, arrived, gain):
    rows, columns = keep.shape
    step = columns * PAIR // gain.shape[0]

    def kernel(keep_ref, arrived_ref, gain_ref, resid_ref, norm_ref, turned_ref):
        resid = keep_ref[...] + arrived_ref[...].astype(F32)
        resid_ref[...] = resid
        norm = normed(resid, gain_ref[...])
        norm_ref[...] = norm
        for i in range(columns // step):
            at, source = i * step, (i ^ 1) * step
            turned_ref[:, at : at + step] = norm[:, source : source + step]

    shapes = [((rows, columns), F32)] + [((rows, columns), BF)] * 2
    return call(
        kernel, [], [keep, arrived, gain.reshape(1, columns)], shapes, [], "norm_share", 24
    )


def pack_pages(pairs):
    width = pairs[0].shape[1] // 2

    def kernel(*refs):
        for j, ref in enumerate(refs[:-1]):
            at, side = j // 2 * PAGE, j % 2 * width
            refs[-1][at : at + PAGE, side : side + width] = ref[:, width:]

    shapes = [((len(pairs) // 2 * PAGE, 2 * width), BF)]
    return call(kernel, [], pairs, shapes, [], "pack_pages", 16)[0]


def pick_pages(source, pairs, arrived, count):
    width = arrived.shape[1] // 2

    def kernel(source_ref, *refs):
        pages = [ref[:, :width] for ref in refs[: len(pairs)]]
        for j in range(len(pairs)):
            at, side = j // 2 * PAGE, j % 2 * width
            pages.append(refs[len(pairs)][at : at + PAGE, side : side + width])
        for p in range(count):
            for i, page in enumerate(pages):

                @pl.when(source_ref[p] == i)
                def _(p=p, page=page):
                    refs[-1][p] = page

    shapes = [((count, PAGE, width), BF)]
    return call(kernel, [source], [*pairs, arrived], shapes, [], "pick_pages", 16, 5 * 10**9)[0]


def class_rows(place, weight):
    rows, columns = weight.shape
    half = rows // 2

    def kernel(place_ref, weight_ref, *outs):
        for k in range(2):
            begin = pl.multiple_of((place_ref[1] ^ k) * half, 16)
            outs[k][...] = weight_ref[pl.ds(begin, half), :]

    return call(kernel, [place], [weight], [((half, columns), BF)] * 2, [], "class_rows")


def gated(tokens, weight, parts=1):
    rows = tokens.shape[0] // parts
    size = weight.shape[1] // 2
    tile = 256

    def kernel(tokens_ref, weight_ref, *outs):
        for p, out_ref in enumerate(outs):

            @pl.loop(0, rows // tile)
            def _(i, p=p, out_ref=out_ref):
                source = pl.ds(pl.multiple_of(p * rows + i * tile, tile), tile)
                projected = dot(tokens_ref[source, :], weight_ref[...])
                gate, up = projected[:, :size], projected[:, size:]
                out_ref[pl.ds(pl.multiple_of(i * tile, tile), tile), :] = (
                    gate / (1.0 + jnp.exp(-gate)) * up
                ).astype(BF)

    shapes = [((rows, size), BF)] * parts
    return call(kernel, [], [tokens, weight], shapes, [], "gated", 24)


def body(
    tokens,
    lengths,
    page_slot,
    trainer_layout,
    trainer_qkv,
    trainer_gateup,
    attn_gain,
    ffn_gain,
    out_proj,
    down_proj,
):
    n_tp = lax.axis_size("tp")
    n_req = lax.axis_size("req")
    devices = n_tp * n_req
    req = lax.axis_index("req")
    tp = lax.axis_index("tp")
    rows_each = trainer_qkv.shape[0]
    seq_len, model_dim = tokens.shape
    head_dim = HD
    local_heads = out_proj.shape[0] // head_dim
    group_cols = trainer_qkv.shape[1] // n_tp
    local_kv = (group_cols // head_dim - local_heads) // 2
    group = local_heads // local_kv
    q_cols = local_heads * head_dim
    k_cols = local_kv * head_dim
    ff_local = down_proj.shape[0]
    share = seq_len // n_tp

    def swap(value, req_mask, tp_mask):
        pairs = [(d, d ^ (req_mask * n_tp + tp_mask)) for d in range(devices)]
        return lax.ppermute(value, ("req", "tp"), pairs)

    def pick(stack, index):
        return lax.dynamic_index_in_dim(stack, index, 0, keepdims=False)

    def sync(values):
        return lax.optimization_barrier(values)

    halves = 2
    units = ff_local // halves
    chunks = list(CHUNKS) + [units - sum(CHUNKS)]
    bits = [1 << k for k in range(16) if 1 << k < n_tp]
    evens = list(range(2, n_req, 2))
    zbits = [1 << k for k in range(1, 16) if 1 << k < n_req]
    singles = [r for r in evens if r & (r - 1) == 0]
    doubles = [r for r in evens if r & (r - 1)]
    plain = [r for r in evens if not r & PAIR]
    crossed = [r for r in evens if r & PAIR and r != PAIR]

    def spread_z(held, group):
        for r in group:
            bit = r & -r
            held[r] = swap(held[r ^ bit], bit, 0)

    def spread_class(held, mine, other, group):
        for r in group:
            if r == PAIR:
                held[r] = swap(other, PAIR, 0)
                continue
            rest = r & ~PAIR
            bit = 1 << (rest.bit_length() - 1)
            held[r] = swap(held[r ^ bit] if r != bit else mine, bit, 0)

    place = jnp.stack([tp, (req // PAIR) % 2])
    qkv_split = split_qkv(place, trainer_qkv, n_tp)
    half = head_dim // 2
    freq = theta_base ** (-jnp.arange(half, dtype=F32) * 2.0 / head_dim)
    angles = jnp.arange(seq_len, dtype=F32)[:, None] * freq[None, :]
    tables = (jnp.cos(angles), jnp.sin(angles))
    trainer_gateup, qkv_split = sync((trainer_gateup, qkv_split))
    gu_own, gu_odd = split_gateup(place, trainer_gateup, n_tp, halves, chunks)
    qkv_split = [qkv_split[0]] + [swap(qkv_split[s], 0, s) for s in range(1, n_tp)]
    st = sync(
        dict(
            qkv_split=qkv_split,
            gu_own=gu_own,
            gu_odd=gu_odd,
            tokens=tokens,
            layout=trainer_layout,
            tables=tables,
        )
    )

    tokens, trainer_layout, tables = st["tokens"], st["layout"], st["tables"]
    gu_own, gu_near = st["gu_own"], swap(st["gu_odd"], 0, 1)
    qkv_own = join_qkv(place, st["qkv_split"])
    qkv = {0: qkv_own}
    spread_z(qkv, singles)
    qkv[1] = swap(qkv_own, 1, 0)
    far = list(pack_far(place, gu_own, gu_near, chunks))
    tokens, far = sync((tokens, far))

    def over_y(value):
        moved = [swap(value[f], 0, 2 * f + 2) for f in range(n_tp // 2 - 1)]
        return jnp.stack(moved) if len(moved) > 1 else moved[0][None]

    blocks = [join_gateup(place, gu_own, gu_near, over_y(far[0]), 0)]
    order = jnp.arange(n_req, dtype=jnp.int32) ^ req
    shards = (order[:, None] * n_tp + jnp.arange(n_tp, dtype=jnp.int32)[None, :]).reshape(-1)
    blocks_at = trainer_layout[shards]
    columns_at = (
        blocks_at[:, None] * rows_each + jnp.arange(rows_each, dtype=jnp.int32)[None, :]
    ).reshape(-1)
    columns_back = (
        jnp.argmax(
            blocks_at[None, :] == jnp.arange(devices, dtype=jnp.int32)[:, None], axis=1
        ).astype(jnp.int32)[:, None]
        * rows_each
        + jnp.arange(rows_each, dtype=jnp.int32)[None, :]
    ).reshape(-1)
    gain_in = attn_gain.reshape(devices, rows_each)[blocks_at].reshape(-1)
    tokens_in, x_norm = permute_columns(tokens, columns_at, gain_in)
    st = sync(
        dict(
            qkv=qkv,
            far=far[1],
            blocks=blocks,
            gu_own=gu_own,
            gu_near=gu_near,
            x_norm=x_norm,
            tokens_in=tokens_in,
            onehot_at=columns_at,
            out_proj=out_proj,
            down_proj=down_proj,
            page_slot=page_slot,
            ffn_gain=ffn_gain,
        )
    )

    qkv, far, x_norm, tokens_in = st["qkv"], st["far"], st["x_norm"], st["tokens_in"]
    columns_at, page_slot = st["onehot_at"], st["page_slot"]
    blocks = list(st["blocks"])
    blocks.append(join_gateup(place, st["gu_own"], st["gu_near"], over_y(far), 2 * chunks[0]))
    gu = [dict() for _ in chunks]
    spread_class(gu[0], *blocks[0], plain)
    spread_z(qkv, doubles)
    for r in singles[::-1]:
        qkv[r ^ 1] = swap(qkv[r], 1, 0)
    out_in = permute_columns(st["out_proj"], columns_at, dtype=BF)
    down_rel = class_rows(place, st["down_proj"])
    ffn_gain_in = st["ffn_gain"].reshape(devices, rows_each)[blocks_at].reshape(-1)
    n_pages = seq_len // PAGE
    holders = lax.dynamic_slice_in_dim(page_slot, req * n_pages, n_pages, 0) // n_pages
    page_bits = [PAIR, 1] + [bit for bit in zbits if bit != PAIR]
    at_slot = [
        sum(bit for k, bit in enumerate(reversed(page_bits)) if (i >> k) & 1)
        for i in range(n_req)
    ]
    relative = jnp.asarray(at_slot, jnp.int32) ^ req
    chosen = jnp.argmax(holders[None, :] == relative[:, None], axis=1)
    targets = req * n_pages + jnp.arange(n_pages, dtype=jnp.int32)
    source = jnp.argmax(page_slot[None, :] == targets[:, None], axis=1) // n_pages
    arrival = [0]
    for bit in page_bits:
        arrival = arrival + [r ^ bit for r in arrival]
    arrival = jnp.asarray(arrival, jnp.int32) ^ req
    source = jnp.argmax(arrival[None, :] == source[:, None], axis=1)
    tokens_share = lax.dynamic_slice_in_dim(tokens_in, tp * share, share, 0)
    st = sync(
        dict(
            qkv=qkv,
            gu=gu,
            blocks=blocks,
            x_norm=x_norm,
            out_in=out_in,
            down_rel=down_rel,
            ffn_gain_in=ffn_gain_in,
            pages=(chosen, source),
            tokens_share=tokens_share,
        )
    )

    qkv, gu, blocks, x_norm, out_in = (st[k] for k in ("qkv", "gu", "blocks", "x_norm", "out_in"))
    chosen, source = st["pages"]
    tokens_share = st["tokens_share"]
    down_rel, ffn_gain_in = st["down_rel"], st["ffn_gain_in"]
    spread_class(gu[0], *blocks[0], [PAIR])
    spread_class(gu[1], *blocks[1], plain)
    for r in doubles:
        qkv[r ^ 1] = swap(qkv[r], 1, 0)
    gu[1][0] = blocks[1][0]
    gu[1][1] = swap(blocks[1][0], 1, 0)
    width = model_dim // n_req
    first = [0, 1] + [r | j for r in singles for j in (0, 1)]
    last = [r | j for r in doubles for j in (0, 1)]

    def part(rs):
        return dot(
            jnp.concatenate([x_norm[:, r * width : (r + 1) * width] for r in rs], axis=1),
            jnp.concatenate([qkv[r] for r in rs], axis=0),
        )

    joined = part(first)
    st = sync(dict(qkv=qkv, gu=gu, blocks=blocks, joined=joined, x_norm=x_norm))

    qkv, gu, blocks, x_norm = (st[k] for k in ("qkv", "gu", "blocks", "x_norm"))
    spread_class(gu[0], *blocks[0], crossed)
    spread_class(gu[1], *blocks[1], [PAIR])
    gu[0][0] = blocks[0][0]
    gu[0][1] = swap(blocks[0][0], 1, 0)
    for r in plain:
        gu[0][r ^ 1] = swap(gu[0][r], 1, 0)
    shares = sorted(range(n_tp), key=lambda s: [(s >> k) & 1 for k in range(len(bits))])
    leaving, staying, *box = attend(
        place,
        lengths,
        chosen.astype(jnp.int32),
        st["joined"],
        jnp.concatenate([x_norm[:, r * width : (r + 1) * width] for r in last], axis=1),
        [qkv[r] for r in last],
        tables,
        out_in,
        (local_heads, local_kv, head_dim),
        shares,
    )
    st = sync(dict(gu=gu, leaving=leaving, staying=staying, box=box))

    gu, box = st["gu"], st["box"]
    keep, send = add_share(st["staying"], swap(st["leaving"], 0, bits[0]), tokens_share)
    arrived = swap(send, 0, bits[1])
    spread_class(gu[1], None, None, crossed)
    gu[0][PAIR ^ 1] = swap(gu[0][PAIR], 1, 0)
    for r in plain:
        gu[1][r ^ 1] = swap(gu[1][r], 1, 0)

    def page_parts(box):
        half = box[0].shape[0] // 2
        return [pages[:half] for pages in box], jnp.concatenate(
            [pages[half:] for pages in box], axis=0
        )

    def page_step(parts, bit):
        kept, leaving = parts
        half = kept[0].shape[0]
        moved = swap(leaving, bit, 0)
        return kept + [moved[at : at + half] for at in range(0, leaving.shape[0], half)]

    late = crossed[0]
    box = [box[0], swap(box[1], page_bits[0], 0)]
    gu[1][late] = hold(gu[1][late], box[1], gu[0][PAIR ^ 1], *[gu[1][r ^ 1] for r in plain])
    resid_in, h_share, h_leaving = norm_share(
        keep, arrived, ffn_gain_in.reshape(n_req, model_dim // n_req)
    )
    st = sync(dict(gu=gu, h=(h_share, h_leaving), resid_in=resid_in, box=box))

    gu, resid_in = st["gu"], st["resid_in"]
    h_share, h_leaving = st["h"]
    cross = n_tp // 2
    own = (h_share, swap(h_share, 0, cross))
    theirs = (swap(h_leaving, PAIR, 0), swap(h_leaving, PAIR, cross))
    for r in crossed:
        gu[0][r ^ 1] = swap(gu[0][r], 1, 0)
    gu[1][PAIR ^ 1] = swap(gu[1][PAIR], 1, 0)
    coarse = resid_in.astype(BF)
    fine = (resid_in - coarse.astype(F32)).astype(BF)
    terms = permute_columns(jnp.concatenate([coarse, fine], axis=0), columns_back)
    st = sync(dict(gu=gu, own=own, theirs=theirs, terms=terms, box=page_parts(st["box"])))

    gu, box = st["gu"], st["box"]
    resid = st["terms"][:share] + st["terms"][share:]
    own, theirs = (jnp.concatenate(st[k], axis=0) for k in ("own", "theirs"))
    weight = assemble([gu[0][r] for r in range(n_req)])
    hidden = gated(theirs, weight)[0]
    returned = [swap(hidden, PAIR, 0)]
    own_next, theirs_next = swap(own, 0, bits[0]), swap(theirs, 0, bits[0])
    for r in crossed:
        gu[1][r ^ 1] = swap(gu[1][r], 1, 0)
    hidden = gated(theirs_next, weight)[0]
    h_own = jnp.concatenate([own, own_next], axis=0)
    h_theirs = jnp.concatenate([theirs, theirs_next], axis=0)
    weights = [weight, assemble([gu[1][r] for r in range(n_req)], 4 * 10**9)]
    st = sync(
        dict(
            weights=weights,
            h=(h_own, h_theirs),
            hidden=(hidden, returned),
            resid=resid,
            box=box,
        )
    )

    resid, box = st["resid"], st["box"]
    h_own, h_theirs = st["h"]
    hidden, returned = st["hidden"]
    returned = list(returned) + [swap(hidden, PAIR, 0)]
    weights = st["weights"]
    theirs = gated(h_theirs, weights[1])
    h_own, theirs = sync((h_own, theirs))
    kept = [gated(h_own, weight)[0] for weight in weights]
    rows = seq_len // 2
    product = []
    for i in range(2):
        part = rows_product([(piece, i * rows) for piece in kept], down_rel[0], 0, rows)
        product.append(rows_product([(returned[i], 0)], down_rel[1], 0, rows, part))
    for bit in page_bits[1:-1]:
        box = page_step(box if bit == page_bits[1] else page_parts(box), bit)
    leaving_pages = pack_pages(box)
    returned, box, leaving_pages, product = sync(
        (swap(theirs[0], PAIR, 0), box, leaving_pages, product)
    )
    leaving = rows_product([(returned, rows)], down_rel[1], chunks[0], rows, product[1], BF)
    arrived = swap(leaving, 0, bits[0])
    staying = rows_product([(returned, 0)], down_rel[1], chunks[0], rows, product[0])
    keep, send = add_share(staying, arrived, resid)
    arrived_pages = swap(leaving_pages, page_bits[-1], 0)
    share_slots = tp * share + jnp.arange(share, dtype=jnp.int32)
    live_share = (share_slots < lengths[0]).astype(F32)
    layer_out = ((keep + swap(send, 0, bits[1]).astype(F32)) * live_share[:, None]).astype(BF)
    kv_cache = pick_pages(source.astype(jnp.int32), box, arrived_pages, n_pages)
    return (layer_out, kv_cache)


def solution(mesh):
    return jax.shard_map(
        body,
        mesh=mesh,
        in_specs=(
            P("req", None),
            P("req"),
            P(),
            P(),
            P(("req", "tp"), None),
            P(("req", "tp"), None),
            P(),
            P(),
            P("tp", None),
            P("tp", None),
        ),
        out_specs=(P(("req", "tp"), None), P("req", None, "tp")),
        check_vma=False,
    )
```

```python
import jax
import jax.numpy as jnp
from jax import lax
from jax.experimental import pallas as pl
from jax.experimental.pallas import tpu as pltpu
from jax.sharding import PartitionSpec as P

HD = 80
PAGE = 128
BF = jnp.bfloat16
F32 = jnp.float32

eps_norm = 1e-05
theta_base = 10000.0

PAIR = 2
CHUNKS = (512,)


def normed(values, gain):
    scale = lax.rsqrt(jnp.mean(values * values, axis=-1, keepdims=True) + eps_norm)
    return (values * scale * gain).astype(BF)


def dot(a, b):
    return jnp.dot(a, b, preferred_element_type=F32)


def on_device(kernel, place, ins, shapes, vmem_mib, name):
    def run(place_ref, *refs):
        n_in, n_out = len(ins), len(shapes)
        outs, bufs, sems = refs[n_in : n_in + n_out], refs[n_in + n_out : -1], refs[-1]
        kernel(place_ref, *refs[:n_in], *bufs)
        copies = [pltpu.make_async_copy(bufs[i], outs[i], sems.at[i]) for i in range(n_out)]
        for copy in copies:
            copy.start()
        for copy in copies:
            copy.wait()

    return pl.pallas_call(
        run,
        in_specs=[pl.BlockSpec(memory_space=pltpu.SMEM)]
        + [pl.BlockSpec(memory_space=pltpu.VMEM)] * len(ins),
        out_specs=[pl.BlockSpec(memory_space=pltpu.HBM)] * len(shapes),
        out_shape=[jax.ShapeDtypeStruct(shape, BF) for shape in shapes],
        scratch_shapes=[pltpu.VMEM(shape, BF) for shape in shapes]
        + [pltpu.SemaphoreType.DMA((len(shapes),))],
        compiler_params=pltpu.CompilerParams(vmem_limit_bytes=vmem_mib * 2**20),
        cost_estimate=pl.CostEstimate(flops=1, transcendentals=0, bytes_accessed=1),
        name=name,
    )(place, *ins)


def split_qkv(place, shard, n_tp):
    rows, columns = shard.shape
    width = columns // n_tp

    def kernel(place_ref, shard_ref, *bufs):
        tp = place_ref[0]
        for s in range(n_tp):
            for g in range(n_tp):

                @pl.when((tp ^ s) == g)
                def _(s=s, g=g):
                    bufs[s][...] = shard_ref[:, g * width : (g + 1) * width].astype(BF)

    return on_device(kernel, place, [shard], [(rows, width)] * n_tp, 60, "split_qkv")


def split_gateup(place, shard, n_tp, halves, chunks):
    rows, columns = shard.shape
    width = columns // n_tp
    units = width // 2 // halves

    def kernel(place_ref, shard_ref, *bufs):
        tp = place_ref[0]
        for s in range(n_tp):
            begin = pl.multiple_of((tp ^ s) * width, 128)
            group = shard_ref[:, pl.ds(begin, width)].astype(BF)
            for q in range(halves):
                start = q * units
                edge = 0
                for size in chunks:
                    up = width // 2 + start
                    bufs[s % 2][s // 2, q, :, edge : edge + 2 * size] = jnp.concatenate(
                        [group[:, start : start + size], group[:, up : up + size]], axis=1
                    )
                    start += size
                    edge += 2 * size

    shapes = [(n_tp // 2, halves, rows, 2 * units)] * 2
    return on_device(kernel, place, [shard], shapes, 60, "split_gateup")


def pack_far(place, own, near, chunks):
    n_far, halves, rows, _ = own.shape
    n_far -= 1

    def kernel(place_ref, own_ref, near_ref, *bufs):
        edge = 0
        for c, size in enumerate(chunks):
            for f in range(n_far):
                bufs[c][f, 0] = own_ref[f + 1, :, :, edge : edge + 2 * size]
                bufs[c][f, 1] = near_ref[f + 1, :, :, edge : edge + 2 * size]
            edge += 2 * size

    shapes = [(n_far, 2, halves, rows, 2 * size) for size in chunks]
    return on_device(kernel, place, [own, near], shapes, 60, "pack_far")


LANES = 128


def packed_shape(n_tp, rows, columns):
    full, rest = divmod(columns, LANES)
    return (full * n_tp + -(-rest * n_tp // LANES), rows, LANES)


def pack_rows(buf, t, n_tp, piece):
    full, rest = divmod(piece.shape[1], LANES)
    for i in range(full):
        buf[i * n_tp + t] = piece[:, i * LANES : (i + 1) * LANES]
    if rest:
        group = n_tp * rest // LANES
        for side in range(LANES // rest):

            @pl.when(lax.div(t, group) == side)
            def _(side=side):
                buf[full * n_tp + lax.rem(t, group), :, side * rest : (side + 1) * rest] = piece[
                    :, full * LANES :
                ]


def join_qkv(place, parts):
    rows, columns = parts[0].shape
    n_tp = len(parts)

    def kernel(place_ref, *refs):
        for s in range(n_tp):
            pack_rows(refs[n_tp], place_ref[0] ^ s, n_tp, refs[s][...])

    shapes = [packed_shape(n_tp, rows, columns)]
    return on_device(kernel, place, parts, shapes, 60, "join_qkv")[0]


def join_gateup(place, own, near, far, start):
    n_far, _, halves, rows, columns = far.shape
    n_tp = 2 * n_far + 2

    def kernel(place_ref, own_ref, near_ref, far_ref, *bufs):
        tp, mine = place_ref[0], place_ref[1]
        for k in range(2):
            q = mine ^ k
            pack_rows(bufs[k], tp, n_tp, own_ref[0, q, :, start : start + columns])
            pack_rows(bufs[k], tp ^ 1, n_tp, near_ref[0, q, :, start : start + columns])
            for f in range(n_far):
                for j in range(2):
                    pack_rows(bufs[k], tp ^ (2 * f + 2 + j), n_tp, far_ref[f, j, q])

    shapes = [packed_shape(n_tp, rows, columns)] * 2
    return on_device(kernel, place, [own, near, far], shapes, 60, "join_gateup")


SMEM = pl.BlockSpec(memory_space=pltpu.SMEM)
VMEM = pl.BlockSpec(memory_space=pltpu.VMEM)


def call(kernel, smem, vmem, shapes, scratch, name, mib=48, flops=1):
    return pl.pallas_call(
        kernel,
        in_specs=[SMEM] * len(smem) + [VMEM] * len(vmem),
        out_specs=[VMEM] * len(shapes),
        out_shape=[jax.ShapeDtypeStruct(*shape) for shape in shapes],
        scratch_shapes=[pltpu.VMEM(*shape) for shape in scratch],
        compiler_params=pltpu.CompilerParams(vmem_limit_bytes=mib * 2**20),
        cost_estimate=pl.CostEstimate(flops=flops, transcendentals=0, bytes_accessed=1),
        name=name,
    )(*smem, *vmem)


def permute_columns(values, columns_at, gain=None, dtype=F32):
    rows, width = values.shape
    tile = 256

    def kernel(values_ref, at_ref, *refs):
        out_ref = refs[0] if gain is None else refs[1]

        @pl.loop(0, width // tile)
        def _(i):
            at = pl.ds(pl.multiple_of(i * tile, tile), tile)
            source = lax.broadcasted_iota(jnp.int32, (width, tile), 0)
            onehot = (source == at_ref[:, at]).astype(F32).astype(BF)
            out_ref[:, at] = dot(values_ref[...], onehot).astype(dtype)

        if gain is not None:

            @pl.loop(0, rows // 128)
            def _(i):
                at = pl.ds(pl.multiple_of(i * 128, 128), 128)
                refs[2][at, :] = normed(out_ref[at, :], refs[0][...])

    ins = [values, columns_at[None]] + ([] if gain is None else [gain[None]])
    shapes = [((rows, width), dtype)] + ([] if gain is None else [((rows, width), BF)])
    outs = call(kernel, [], ins, shapes, [], "permute_columns")
    return outs[0] if gain is None else outs


def hold(value, *others):
    def kernel(*refs):
        pass

    return pl.pallas_call(
        kernel,
        in_specs=[pl.BlockSpec(memory_space=pl.ANY)] * (1 + len(others)),
        out_specs=pl.BlockSpec(memory_space=pl.ANY),
        out_shape=jax.ShapeDtypeStruct(value.shape, value.dtype),
        input_output_aliases={0: 0},
        cost_estimate=pl.CostEstimate(flops=10**11, transcendentals=0, bytes_accessed=10**8),
        name="hold",
    )(value, *others)


def attend(place, lengths, chosen, joined, x_last, w_last, tables, out_in, sizes, shares):
    seq_len, columns = joined.shape
    heads, kv_heads, head_dim = sizes
    group = heads // kv_heads
    q_cols, k_cols = heads * head_dim, kv_heads * head_dim
    half = head_dim // 2
    wide = (q_cols + k_cols + 127) // 128 * 128
    width = w_last[0].shape[0]
    model_dim = out_in.shape[1]
    share = seq_len // len(shares)
    slots = chosen.shape[0] // 2
    tile = 128

    def kernel(
        place_ref, length_ref, chosen_ref, joined_ref, x_ref, cos_ref, sin_ref, out_in_ref, *refs
    ):
        w_refs = refs[: len(w_last)]
        leaving_ref, staying_ref, *boxes, cache_ref, qk, v, context = refs[len(w_last) :]
        tp, length = place_ref[0], length_ref[0]
        lane = lax.broadcasted_iota(jnp.int32, (tile, wide), 1)
        first = lax.rem(lane, head_dim) < half
        for t in range(seq_len // tile):
            at = slice(t * tile, (t + 1) * tile)
            rows = joined_ref[at, :]
            for i, w_ref in enumerate(w_refs):
                rows = rows + dot(x_ref[at, i * width : (i + 1) * width], w_ref[...])
            head = rows[:, :wide]
            ahead = pltpu.roll(head, wide - half, 1)
            behind = pltpu.roll(head, half, 1)
            cosine, sine = (
                jnp.concatenate([ref[at, :]] * (wide // half + 1), axis=1)[:, :wide]
                for ref in (cos_ref, sin_ref)
            )
            turned = head * cosine + jnp.where(first, -ahead, behind) * sine
            qk[at, :] = turned.astype(BF)
            v[at, :] = rows[:, q_cols + k_cols :].astype(BF)
            slot = t * tile + lax.broadcasted_iota(jnp.int32, (tile, 1), 0)
            live = (slot < length).astype(F32)
            cache_ref[at, :k_cols] = (turned[:, q_cols : q_cols + k_cols] * live).astype(BF)
            cache_ref[at, k_cols:] = (rows[:, q_cols + k_cols :] * live).astype(BF)
        for i in range(chosen.shape[0]):
            page = cache_ref[pl.ds(pl.multiple_of(chosen_ref[i] * PAGE, PAGE), PAGE), :]
            at, side = i % slots // 2 * PAGE, i % 2 * 2 * k_cols
            boxes[i // slots][at : at + PAGE, side : side + 2 * k_cols] = page
        for k in range(kv_heads):
            key_at = q_cols + k * head_dim
            for t in range(seq_len // tile):
                at = slice(t * tile, (t + 1) * tile)
                count = (t + 1) * tile
                q = jnp.concatenate(
                    [
                        qk[at, (k * group + g) * head_dim : (k * group + g + 1) * head_dim]
                        for g in range(group)
                    ],
                    axis=0,
                )
                scores = lax.dot_general(
                    q,
                    qk[:count, key_at : key_at + head_dim],
                    (((1,), (1,)), ((), ())),
                    preferred_element_type=F32,
                ) * head_dim ** (-0.5)
                shape = (tile, count)
                slot = t * tile + lax.broadcasted_iota(jnp.int32, shape, 0)
                key = lax.broadcasted_iota(jnp.int32, shape, 1)
                allowed = (key <= slot) & (key < length)
                scores = scores.reshape(group, tile, count)
                scores = jnp.where(allowed[None], scores, -1e30)
                top = jnp.max(scores, axis=-1, keepdims=True)
                weight = jnp.exp(scores - top)
                probs = (weight / jnp.sum(weight, axis=-1, keepdims=True)).astype(BF)
                mixed = dot(
                    probs.reshape(group * tile, count), v[:count, k * head_dim : (k + 1) * head_dim]
                ).astype(BF)
                for g in range(group):
                    h = k * group + g
                    context[at, h * head_dim : (h + 1) * head_dim] = mixed[
                        g * tile : (g + 1) * tile
                    ]
        for i, s in enumerate(shares):
            block = context[pl.ds(pl.multiple_of((tp ^ s) * share, share), share), :]
            product = dot(block, out_in_ref[...])
            j = i % (len(shares) // 2)
            if i < len(shares) // 2:
                staying_ref[j * share : (j + 1) * share, :] = product
            else:
                leaving_ref[j * share : (j + 1) * share, :] = product.astype(BF)

    return call(
        kernel,
        [place, lengths, chosen],
        [joined, x_last, *tables, out_in, *w_last],
        [
            ((seq_len // 2, model_dim), BF),
            ((seq_len // 2, model_dim), F32),
        ]
        + [((slots // 2 * PAGE, 4 * k_cols), BF)] * 2,
        [((seq_len, 2 * k_cols), BF), ((seq_len, wide), BF), ((seq_len, k_cols), BF), ((seq_len, q_cols), BF)],
        "attend",
    )


def assemble(blocks, n_tp, columns, flops=1):
    rows = blocks[0].shape[1]
    full, rest = divmod(columns, LANES)
    group = n_tp * rest // LANES

    def kernel(*refs):
        out_ref = refs[-1]
        for b, ref in enumerate(refs[:-1]):
            for t in range(n_tp):
                first = (b * n_tp + t) * rows
                at = slice(first, first + rows)
                for i in range(full):
                    out_ref[at, i * LANES : (i + 1) * LANES] = ref[i * n_tp + t]
                if rest:
                    side = t // group * rest
                    out_ref[at, full * LANES :] = ref[
                        full * n_tp + t % group, :, side : side + rest
                    ]

    shapes = [((len(blocks) * n_tp * rows, columns), BF)]
    return call(kernel, [], blocks, shapes, [], "assemble", 24, flops)[0]


def rows_product(pieces, weight, at, count, base=None, dtype=F32):
    columns = weight.shape[1]
    tile = 128

    def kernel(*refs):
        weight_ref = refs[len(pieces)]

        @pl.loop(0, count // tile)
        def _(i):
            out = pl.ds(pl.multiple_of(i * tile, tile), tile)
            total = 0.0 if base is None else refs[len(pieces) + 1][out, :]
            begin = at
            for (piece, first), ref in zip(pieces, refs):
                end = begin + piece.shape[1]
                source = pl.ds(pl.multiple_of(first + i * tile, tile), tile)
                total = total + dot(ref[source, :], weight_ref[begin:end, :])
                begin = end
            refs[-1][out, :] = total.astype(dtype)

    ins = [piece for piece, _ in pieces] + [weight] + ([] if base is None else [base])
    return call(kernel, [], ins, [((count, columns), dtype)], [], "rows_product", 24)[0]


def add_share(staying, arrived, extra):
    rows, columns = staying.shape
    half = rows // 2

    def kernel(staying_ref, arrived_ref, extra_ref, keep_ref, send_ref):
        keep_ref[...] = (
            staying_ref[:half, :] + arrived_ref[:half, :].astype(F32) + extra_ref[...]
        )
        send_ref[...] = (staying_ref[half:, :] + arrived_ref[half:, :].astype(F32)).astype(BF)

    return call(
        kernel,
        [],
        [staying, arrived, extra],
        [((half, columns), F32), ((half, columns), BF)],
        [],
        "add_share",
        24,
    )


def norm_share(keep, arrived, gain):
    rows, columns = keep.shape
    step = columns * PAIR // gain.shape[0]

    def kernel(keep_ref, arrived_ref, gain_ref, resid_ref, norm_ref, turned_ref):
        resid = keep_ref[...] + arrived_ref[...].astype(F32)
        resid_ref[...] = resid
        norm = normed(resid, gain_ref[...])
        norm_ref[...] = norm
        for i in range(columns // step):
            at, source = i * step, (i ^ 1) * step
            turned_ref[:, at : at + step] = norm[:, source : source + step]

    shapes = [((rows, columns), F32)] + [((rows, columns), BF)] * 2
    return call(
        kernel, [], [keep, arrived, gain.reshape(1, columns)], shapes, [], "norm_share", 24
    )


def pack_pages(pairs):
    width = pairs[0].shape[1] // 2

    def kernel(*refs):
        for j, ref in enumerate(refs[:-1]):
            at, side = j // 2 * PAGE, j % 2 * width
            refs[-1][at : at + PAGE, side : side + width] = ref[:, width:]

    shapes = [((len(pairs) // 2 * PAGE, 2 * width), BF)]
    return call(kernel, [], pairs, shapes, [], "pack_pages", 16)[0]


def pick_pages(source, pairs, arrived, count):
    width = arrived.shape[1] // 2

    def kernel(source_ref, *refs):
        pages = [ref[:, :width] for ref in refs[: len(pairs)]]
        for j in range(len(pairs)):
            at, side = j // 2 * PAGE, j % 2 * width
            pages.append(refs[len(pairs)][at : at + PAGE, side : side + width])
        for p in range(count):
            for i, page in enumerate(pages):

                @pl.when(source_ref[p] == i)
                def _(p=p, page=page):
                    refs[-1][p] = page

    shapes = [((count, PAGE, width), BF)]
    return call(kernel, [source], [*pairs, arrived], shapes, [], "pick_pages", 16, 5 * 10**9)[0]


def class_rows(place, weight):
    rows, columns = weight.shape
    half = rows // 2

    def kernel(place_ref, weight_ref, *outs):
        for k in range(2):
            begin = pl.multiple_of((place_ref[1] ^ k) * half, 16)
            outs[k][...] = weight_ref[pl.ds(begin, half), :]

    return call(kernel, [place], [weight], [((half, columns), BF)] * 2, [], "class_rows")


def gated(tokens, early, late):
    rows = tokens.shape[0]
    split, columns = early.shape
    size = columns // 2
    tile = 256

    def kernel(tokens_ref, early_ref, late_ref, out_ref):
        @pl.loop(0, rows // tile)
        def _(i):
            at = pl.ds(pl.multiple_of(i * tile, tile), tile)
            projected = dot(tokens_ref[at, :split], early_ref[...])
            projected = projected + dot(tokens_ref[at, split:], late_ref[...])
            gate, up = projected[:, :size], projected[:, size:]
            out_ref[at, :] = (gate / (1.0 + jnp.exp(-gate)) * up).astype(BF)

    return call(kernel, [], [tokens, early, late], [((rows, size), BF)], [], "gated", 24)[0]


def finish(keep, arrived, lengths, place, share_rows):
    rows, columns = keep.shape

    def kernel(length_ref, place_ref, keep_ref, arrived_ref, out_ref):
        slot = place_ref[0] * share_rows + lax.broadcasted_iota(jnp.int32, (rows, 1), 0)
        live = (slot < length_ref[0]).astype(F32)
        out_ref[...] = ((keep_ref[...] + arrived_ref[...].astype(F32)) * live).astype(BF)

    shapes = [((rows, columns), BF)]
    return call(kernel, [lengths, place], [keep, arrived], shapes, [], "finish", 24)[0]


def body(
    tokens,
    lengths,
    page_slot,
    trainer_layout,
    trainer_qkv,
    trainer_gateup,
    attn_gain,
    ffn_gain,
    out_proj,
    down_proj,
):
    n_tp = lax.axis_size("tp")
    n_req = lax.axis_size("req")
    devices = n_tp * n_req
    req = lax.axis_index("req")
    tp = lax.axis_index("tp")
    rows_each = trainer_qkv.shape[0]
    seq_len, model_dim = tokens.shape
    head_dim = HD
    local_heads = out_proj.shape[0] // head_dim
    group_cols = trainer_qkv.shape[1] // n_tp
    local_kv = (group_cols // head_dim - local_heads) // 2
    group = local_heads // local_kv
    q_cols = local_heads * head_dim
    k_cols = local_kv * head_dim
    ff_local = down_proj.shape[0]
    share = seq_len // n_tp

    def swap(value, req_mask, tp_mask):
        pairs = [(d, d ^ (req_mask * n_tp + tp_mask)) for d in range(devices)]
        return lax.ppermute(value, ("req", "tp"), pairs)

    def pick(stack, index):
        return lax.dynamic_index_in_dim(stack, index, 0, keepdims=False)

    def sync(values):
        return lax.optimization_barrier(values)

    halves = 2
    units = ff_local // halves
    chunks = list(CHUNKS) + [units - sum(CHUNKS)]
    bits = [1 << k for k in range(16) if 1 << k < n_tp]
    evens = list(range(2, n_req, 2))
    zbits = [1 << k for k in range(1, 16) if 1 << k < n_req]
    singles = [r for r in evens if r & (r - 1) == 0]
    doubles = [r for r in evens if r & (r - 1)]
    plain = [r for r in evens if not r & PAIR]
    crossed = [r for r in evens if r & PAIR and r != PAIR]

    def spread_z(held, group):
        for r in group:
            bit = r & -r
            held[r] = swap(held[r ^ bit], bit, 0)

    def spread_class(held, mine, other, group):
        for r in group:
            if r == PAIR:
                held[r] = swap(other, PAIR, 0)
                continue
            rest = r & ~PAIR
            bit = 1 << (rest.bit_length() - 1)
            held[r] = swap(held[r ^ bit] if r != bit else mine, bit, 0)

    place = jnp.stack([tp, (req // PAIR) % 2])
    qkv_split = split_qkv(place, trainer_qkv, n_tp)
    half = head_dim // 2
    freq = theta_base ** (-jnp.arange(half, dtype=F32) * 2.0 / head_dim)
    angles = jnp.arange(seq_len, dtype=F32)[:, None] * freq[None, :]
    tables = (jnp.cos(angles), jnp.sin(angles))
    trainer_gateup, qkv_split = sync((trainer_gateup, qkv_split))
    gu_own, gu_odd = split_gateup(place, trainer_gateup, n_tp, halves, chunks)
    qkv_split = [qkv_split[0]] + [swap(qkv_split[s], 0, s) for s in range(1, n_tp)]
    st = sync(
        dict(
            qkv_split=qkv_split,
            gu_own=gu_own,
            gu_odd=gu_odd,
            tokens=tokens,
            layout=trainer_layout,
            tables=tables,
        )
    )

    tokens, trainer_layout, tables = st["tokens"], st["layout"], st["tables"]
    gu_own, gu_near = st["gu_own"], swap(st["gu_odd"], 0, 1)
    qkv_own = join_qkv(place, st["qkv_split"])
    qkv = {0: qkv_own}
    spread_z(qkv, singles)
    qkv[1] = swap(qkv_own, 1, 0)
    far = list(pack_far(place, gu_own, gu_near, chunks))
    tokens, far = sync((tokens, far))

    def over_y(value):
        moved = [swap(value[f], 0, 2 * f + 2) for f in range(n_tp // 2 - 1)]
        return jnp.stack(moved) if len(moved) > 1 else moved[0][None]

    blocks = [join_gateup(place, gu_own, gu_near, over_y(far[0]), 0)]
    order = jnp.arange(n_req, dtype=jnp.int32) ^ req
    shards = (order[:, None] * n_tp + jnp.arange(n_tp, dtype=jnp.int32)[None, :]).reshape(-1)
    blocks_at = trainer_layout[shards]
    columns_at = (
        blocks_at[:, None] * rows_each + jnp.arange(rows_each, dtype=jnp.int32)[None, :]
    ).reshape(-1)
    columns_back = (
        jnp.argmax(
            blocks_at[None, :] == jnp.arange(devices, dtype=jnp.int32)[:, None], axis=1
        ).astype(jnp.int32)[:, None]
        * rows_each
        + jnp.arange(rows_each, dtype=jnp.int32)[None, :]
    ).reshape(-1)
    gain_in = attn_gain.reshape(devices, rows_each)[blocks_at].reshape(-1)
    tokens_in, x_norm = permute_columns(tokens, columns_at, gain_in)
    st = sync(
        dict(
            qkv=qkv,
            far=far[1],
            blocks=blocks,
            gu_own=gu_own,
            gu_near=gu_near,
            x_norm=x_norm,
            tokens_in=tokens_in,
            onehot_at=columns_at,
            out_proj=out_proj,
            down_proj=down_proj,
            page_slot=page_slot,
            ffn_gain=ffn_gain,
        )
    )

    qkv, far, x_norm, tokens_in = st["qkv"], st["far"], st["x_norm"], st["tokens_in"]
    columns_at, page_slot = st["onehot_at"], st["page_slot"]
    blocks = list(st["blocks"])
    blocks.append(join_gateup(place, st["gu_own"], st["gu_near"], over_y(far), 2 * chunks[0]))
    gu = [dict() for _ in chunks]
    spread_class(gu[0], *blocks[0], plain)
    spread_z(qkv, doubles)
    for r in singles[::-1]:
        qkv[r ^ 1] = swap(qkv[r], 1, 0)
    out_in = permute_columns(st["out_proj"], columns_at, dtype=BF)
    down_rel = class_rows(place, st["down_proj"])
    ffn_gain_in = st["ffn_gain"].reshape(devices, rows_each)[blocks_at].reshape(-1)
    n_pages = seq_len // PAGE
    holders = lax.dynamic_slice_in_dim(page_slot, req * n_pages, n_pages, 0) // n_pages
    page_bits = [PAIR, 1] + [bit for bit in zbits if bit != PAIR]
    at_slot = [
        sum(bit for k, bit in enumerate(reversed(page_bits)) if (i >> k) & 1)
        for i in range(n_req)
    ]
    relative = jnp.asarray(at_slot, jnp.int32) ^ req
    chosen = jnp.argmax(holders[None, :] == relative[:, None], axis=1)
    targets = req * n_pages + jnp.arange(n_pages, dtype=jnp.int32)
    source = jnp.argmax(page_slot[None, :] == targets[:, None], axis=1) // n_pages
    arrival = [0]
    for bit in page_bits:
        arrival = arrival + [r ^ bit for r in arrival]
    arrival = jnp.asarray(arrival, jnp.int32) ^ req
    source = jnp.argmax(arrival[None, :] == source[:, None], axis=1)
    tokens_share = lax.dynamic_slice_in_dim(tokens_in, tp * share, share, 0)
    st = sync(
        dict(
            qkv=qkv,
            gu=gu,
            blocks=blocks,
            x_norm=x_norm,
            out_in=out_in,
            down_rel=down_rel,
            ffn_gain_in=ffn_gain_in,
            pages=(chosen, source),
            tokens_share=tokens_share,
        )
    )

    qkv, gu, blocks, x_norm, out_in = (st[k] for k in ("qkv", "gu", "blocks", "x_norm", "out_in"))
    chosen, source = st["pages"]
    tokens_share = st["tokens_share"]
    down_rel, ffn_gain_in = st["down_rel"], st["ffn_gain_in"]
    spread_class(gu[0], *blocks[0], [PAIR])
    spread_class(gu[1], *blocks[1], plain)
    for r in doubles:
        qkv[r ^ 1] = swap(qkv[r], 1, 0)
    gu[1][0] = blocks[1][0]
    gu[1][1] = swap(blocks[1][0], 1, 0)
    width = model_dim // n_req
    first = [0, 1] + [r | j for r in singles for j in (0, 1)]
    last = [r | j for r in doubles for j in (0, 1)]

    def part(rs):
        return dot(
            jnp.concatenate([x_norm[:, r * width : (r + 1) * width] for r in rs], axis=1),
            assemble([qkv[r] for r in rs], n_tp, group_cols),
        )

    joined = part(first)
    st = sync(dict(qkv=qkv, gu=gu, blocks=blocks, joined=joined, x_norm=x_norm))

    qkv, gu, blocks, x_norm = (st[k] for k in ("qkv", "gu", "blocks", "x_norm"))
    spread_class(gu[0], *blocks[0], crossed)
    spread_class(gu[1], *blocks[1], [PAIR])
    gu[0][0] = blocks[0][0]
    gu[0][1] = swap(blocks[0][0], 1, 0)
    for r in plain:
        gu[0][r ^ 1] = swap(gu[0][r], 1, 0)
    shares = sorted(range(n_tp), key=lambda s: [(s >> k) & 1 for k in range(len(bits))])
    leaving, staying, *box = attend(
        place,
        lengths,
        chosen.astype(jnp.int32),
        st["joined"],
        jnp.concatenate([x_norm[:, r * width : (r + 1) * width] for r in last], axis=1),
        [assemble([qkv[r] for r in last], n_tp, group_cols)],
        tables,
        out_in,
        (local_heads, local_kv, head_dim),
        shares,
    )
    st = sync(dict(gu=gu, leaving=leaving, staying=staying, box=box))

    gu, box = st["gu"], st["box"]
    keep, send = add_share(st["staying"], swap(st["leaving"], 0, bits[0]), tokens_share)
    arrived = swap(send, 0, bits[1])
    spread_class(gu[1], None, None, crossed)
    gu[0][PAIR ^ 1] = swap(gu[0][PAIR], 1, 0)
    for r in plain:
        gu[1][r ^ 1] = swap(gu[1][r], 1, 0)

    def page_parts(box):
        half = box[0].shape[0] // 2
        return [pages[:half] for pages in box], jnp.concatenate(
            [pages[half:] for pages in box], axis=0
        )

    def page_step(parts, bit):
        kept, leaving = parts
        half = kept[0].shape[0]
        moved = swap(leaving, bit, 0)
        return kept + [moved[at : at + half] for at in range(0, leaving.shape[0], half)]

    late = crossed[0]
    box = [box[0], swap(box[1], page_bits[0], 0)]
    gu[1][late] = hold(gu[1][late], box[1], gu[0][PAIR ^ 1], *[gu[1][r ^ 1] for r in plain])
    resid_in, h_share, h_leaving = norm_share(
        keep, arrived, ffn_gain_in.reshape(n_req, model_dim // n_req)
    )
    st = sync(dict(gu=gu, h=(h_share, h_leaving), resid_in=resid_in, box=box))

    gu, resid_in = st["gu"], st["resid_in"]
    h_share, h_leaving = st["h"]
    cross = n_tp // 2
    own = (h_share, swap(h_share, 0, cross))
    theirs = (swap(h_leaving, PAIR, 0), swap(h_leaving, PAIR, cross))
    for r in crossed:
        gu[0][r ^ 1] = swap(gu[0][r], 1, 0)
    gu[1][PAIR ^ 1] = swap(gu[1][PAIR], 1, 0)
    coarse = resid_in.astype(BF)
    fine = (resid_in - coarse.astype(F32)).astype(BF)
    terms = permute_columns(jnp.concatenate([coarse, fine], axis=0), columns_back)
    early = assemble([gu[0][r] for r in range(n_req - 2)], n_tp, 2 * chunks[0])
    st = sync(dict(gu=gu, own=own, theirs=theirs, terms=terms, early=early, box=page_parts(st["box"])))

    gu, box = st["gu"], st["box"]
    resid = st["terms"][:share] + st["terms"][share:]
    own, theirs = (jnp.concatenate(st[k], axis=0) for k in ("own", "theirs"))
    pair = [n_req - 2, n_req - 1]
    first = (st["early"], assemble([gu[0][r] for r in pair], n_tp, 2 * chunks[0]))
    hidden = gated(theirs, *first)
    returned = [swap(hidden, PAIR, 0)]
    own_next, theirs_next = swap(own, 0, bits[0]), swap(theirs, 0, bits[0])
    for r in crossed:
        gu[1][r ^ 1] = swap(gu[1][r], 1, 0)
    hidden = gated(theirs_next, *first)
    h_own = jnp.concatenate([own, own_next], axis=0)
    h_theirs = jnp.concatenate([theirs, theirs_next], axis=0)
    early = assemble([gu[1][r] for r in range(n_req - 2)], n_tp, 2 * chunks[1])
    ready, early = sync((gu[1][pair[0]], early))
    second = (early, assemble([ready, gu[1][pair[1]]], n_tp, 2 * chunks[1], 4 * 10**9))
    weights = [first, second]
    st = sync(
        dict(
            weights=weights,
            h=(h_own, h_theirs),
            hidden=(hidden, returned),
            resid=resid,
            box=box,
        )
    )

    resid, box = st["resid"], st["box"]
    h_own, h_theirs = st["h"]
    hidden, returned = st["hidden"]
    returned = list(returned) + [swap(hidden, PAIR, 0)]
    weights = st["weights"]
    theirs = gated(h_theirs, *weights[1])
    h_own, theirs = sync((h_own, theirs))
    kept = [gated(h_own, *weight) for weight in weights]
    rows = seq_len // 2
    product = []
    for i in range(2):
        part = rows_product([(piece, i * rows) for piece in kept], down_rel[0], 0, rows)
        product.append(rows_product([(returned[i], 0)], down_rel[1], 0, rows, part))
    for bit in page_bits[1:-1]:
        box = page_step(box if bit == page_bits[1] else page_parts(box), bit)
    leaving_pages = pack_pages(box)
    returned, box, leaving_pages, product = sync(
        (swap(theirs, PAIR, 0), box, leaving_pages, product)
    )
    leaving = rows_product([(returned, rows)], down_rel[1], chunks[0], rows, product[1], BF)
    arrived = swap(leaving, 0, bits[0])
    staying = rows_product([(returned, 0)], down_rel[1], chunks[0], rows, product[0])
    keep, send = add_share(staying, arrived, resid)
    arrived_pages = swap(leaving_pages, page_bits[-1], 0)
    layer_out = finish(keep, swap(send, 0, bits[1]), lengths, place, share)
    kv_cache = pick_pages(source.astype(jnp.int32), box, arrived_pages, n_pages)
    return (layer_out, kv_cache)


def solution(mesh):
    return jax.shard_map(
        body,
        mesh=mesh,
        in_specs=(
            P("req", None),
            P("req"),
            P(),
            P(),
            P(("req", "tp"), None),
            P(("req", "tp"), None),
            P(),
            P(),
            P("tp", None),
            P("tp", None),
        ),
        out_specs=(P(("req", "tp"), None), P("req", None, "tp")),
        check_vma=False,
    )
```

```python
import jax
import jax.numpy as jnp
from jax import lax
from jax.experimental import pallas as pl
from jax.experimental.pallas import tpu as pltpu
from jax.sharding import PartitionSpec as P

HD = 80
PAGE = 128
BF = jnp.bfloat16
F32 = jnp.float32

eps_norm = 1e-05
theta_base = 10000.0

PAIR = 2
CHUNKS = (512,)


def normed(values, gain):
    scale = lax.rsqrt(jnp.mean(values * values, axis=-1, keepdims=True) + eps_norm)
    return (values * scale * gain).astype(BF)


def dot(a, b):
    return jnp.dot(a, b, preferred_element_type=F32)


def on_device(kernel, place, ins, shapes, vmem_mib, name):
    def run(place_ref, *refs):
        n_in, n_out = len(ins), len(shapes)
        outs, bufs, sems = refs[n_in : n_in + n_out], refs[n_in + n_out : -1], refs[-1]
        kernel(place_ref, *refs[:n_in], *bufs)
        copies = [pltpu.make_async_copy(bufs[i], outs[i], sems.at[i]) for i in range(n_out)]
        for copy in copies:
            copy.start()
        for copy in copies:
            copy.wait()

    return pl.pallas_call(
        run,
        in_specs=[pl.BlockSpec(memory_space=pltpu.SMEM)]
        + [pl.BlockSpec(memory_space=pltpu.VMEM)] * len(ins),
        out_specs=[pl.BlockSpec(memory_space=pltpu.HBM)] * len(shapes),
        out_shape=[jax.ShapeDtypeStruct(shape, BF) for shape in shapes],
        scratch_shapes=[pltpu.VMEM(shape, BF) for shape in shapes]
        + [pltpu.SemaphoreType.DMA((len(shapes),))],
        compiler_params=pltpu.CompilerParams(vmem_limit_bytes=vmem_mib * 2**20),
        cost_estimate=pl.CostEstimate(flops=1, transcendentals=0, bytes_accessed=1),
        name=name,
    )(place, *ins)


def split_qkv(place, shard, n_tp):
    rows, columns = shard.shape
    width = columns // n_tp

    def kernel(place_ref, shard_ref, *bufs):
        tp = place_ref[0]
        for s in range(n_tp):
            for g in range(n_tp):

                @pl.when((tp ^ s) == g)
                def _(s=s, g=g):
                    bufs[s][...] = shard_ref[:, g * width : (g + 1) * width].astype(BF)

    return on_device(kernel, place, [shard], [(rows, width)] * n_tp, 60, "split_qkv")


def split_gateup(place, shard, n_tp, halves, chunks):
    rows, columns = shard.shape
    width = columns // n_tp
    units = width // 2 // halves

    def kernel(place_ref, shard_ref, *bufs):
        tp = place_ref[0]
        for s in range(n_tp):
            begin = pl.multiple_of((tp ^ s) * width, 128)
            group = shard_ref[:, pl.ds(begin, width)].astype(BF)
            for q in range(halves):
                start = q * units
                edge = 0
                for size in chunks:
                    up = width // 2 + start
                    bufs[s % 2][s // 2, q, :, edge : edge + 2 * size] = jnp.concatenate(
                        [group[:, start : start + size], group[:, up : up + size]], axis=1
                    )
                    start += size
                    edge += 2 * size

    shapes = [(n_tp // 2, halves, rows, 2 * units)] * 2
    return on_device(kernel, place, [shard], shapes, 60, "split_gateup")


def pack_far(place, own, near, chunks):
    n_far, halves, rows, _ = own.shape
    n_far -= 1

    def kernel(place_ref, own_ref, near_ref, *bufs):
        edge = 0
        for c, size in enumerate(chunks):
            for f in range(n_far):
                bufs[c][f, 0] = own_ref[f + 1, :, :, edge : edge + 2 * size]
                bufs[c][f, 1] = near_ref[f + 1, :, :, edge : edge + 2 * size]
            edge += 2 * size

    shapes = [(n_far, 2, halves, rows, 2 * size) for size in chunks]
    return on_device(kernel, place, [own, near], shapes, 60, "pack_far")


LANES = 128


def packed_shape(n_tp, rows, columns):
    full, rest = divmod(columns, LANES)
    return (full * n_tp + -(-rest * n_tp // LANES), rows, LANES)


def pack_rows(buf, t, n_tp, piece):
    full, rest = divmod(piece.shape[1], LANES)
    for i in range(full):
        buf[i * n_tp + t] = piece[:, i * LANES : (i + 1) * LANES]
    if rest:
        group = n_tp * rest // LANES
        for side in range(LANES // rest):

            @pl.when(lax.div(t, group) == side)
            def _(side=side):
                buf[full * n_tp + lax.rem(t, group), :, side * rest : (side + 1) * rest] = piece[
                    :, full * LANES :
                ]


def join_qkv(place, parts):
    rows, columns = parts[0].shape
    n_tp = len(parts)

    def kernel(place_ref, *refs):
        for s in range(n_tp):
            pack_rows(refs[n_tp], place_ref[0] ^ s, n_tp, refs[s][...])

    shapes = [packed_shape(n_tp, rows, columns)]
    return on_device(kernel, place, parts, shapes, 60, "join_qkv")[0]


def join_gateup(place, own, near, far, start):
    n_far, _, halves, rows, columns = far.shape
    n_tp = 2 * n_far + 2

    def kernel(place_ref, own_ref, near_ref, far_ref, *bufs):
        tp, mine = place_ref[0], place_ref[1]
        for k in range(2):
            q = mine ^ k
            pack_rows(bufs[k], tp, n_tp, own_ref[0, q, :, start : start + columns])
            pack_rows(bufs[k], tp ^ 1, n_tp, near_ref[0, q, :, start : start + columns])
            for f in range(n_far):
                for j in range(2):
                    pack_rows(bufs[k], tp ^ (2 * f + 2 + j), n_tp, far_ref[f, j, q])

    shapes = [packed_shape(n_tp, rows, columns)] * 2
    return on_device(kernel, place, [own, near, far], shapes, 60, "join_gateup")


SMEM = pl.BlockSpec(memory_space=pltpu.SMEM)
VMEM = pl.BlockSpec(memory_space=pltpu.VMEM)


def call(kernel, smem, vmem, shapes, scratch, name, mib=48, flops=1):
    return pl.pallas_call(
        kernel,
        in_specs=[SMEM] * len(smem) + [VMEM] * len(vmem),
        out_specs=[VMEM] * len(shapes),
        out_shape=[jax.ShapeDtypeStruct(*shape) for shape in shapes],
        scratch_shapes=[pltpu.VMEM(*shape) for shape in scratch],
        compiler_params=pltpu.CompilerParams(vmem_limit_bytes=mib * 2**20),
        cost_estimate=pl.CostEstimate(flops=flops, transcendentals=0, bytes_accessed=1),
        name=name,
    )(*smem, *vmem)


def permute_columns(values, columns_at, gain=None, dtype=F32):
    rows, width = values.shape
    tile = 256

    def kernel(values_ref, at_ref, *refs):
        out_ref = refs[0] if gain is None else refs[1]

        @pl.loop(0, width // tile)
        def _(i):
            at = pl.ds(pl.multiple_of(i * tile, tile), tile)
            source = lax.broadcasted_iota(jnp.int32, (width, tile), 0)
            onehot = (source == at_ref[:, at]).astype(F32).astype(BF)
            out_ref[:, at] = dot(values_ref[...], onehot).astype(dtype)

        if gain is not None:

            @pl.loop(0, rows // 128)
            def _(i):
                at = pl.ds(pl.multiple_of(i * 128, 128), 128)
                refs[2][at, :] = normed(out_ref[at, :], refs[0][...])

    ins = [values, columns_at[None]] + ([] if gain is None else [gain[None]])
    shapes = [((rows, width), dtype)] + ([] if gain is None else [((rows, width), BF)])
    outs = call(kernel, [], ins, shapes, [], "permute_columns")
    return outs[0] if gain is None else outs


def hold(value, *others):
    def kernel(*refs):
        pass

    return pl.pallas_call(
        kernel,
        in_specs=[pl.BlockSpec(memory_space=pl.ANY)] * (1 + len(others)),
        out_specs=pl.BlockSpec(memory_space=pl.ANY),
        out_shape=jax.ShapeDtypeStruct(value.shape, value.dtype),
        input_output_aliases={0: 0},
        cost_estimate=pl.CostEstimate(flops=10**11, transcendentals=0, bytes_accessed=10**8),
        name="hold",
    )(value, *others)


def attend(place, lengths, chosen, joined, x_last, w_last, tables, out_in, sizes, shares):
    seq_len, columns = joined.shape
    heads, kv_heads, head_dim = sizes
    group = heads // kv_heads
    q_cols, k_cols = heads * head_dim, kv_heads * head_dim
    half = head_dim // 2
    wide = (q_cols + k_cols + 127) // 128 * 128
    width = w_last[0].shape[0]
    model_dim = out_in.shape[1]
    share = seq_len // len(shares)
    slots = chosen.shape[0] // 2
    tile = 128

    def kernel(
        place_ref, length_ref, chosen_ref, joined_ref, x_ref, cos_ref, sin_ref, out_in_ref, *refs
    ):
        w_refs = refs[: len(w_last)]
        leaving_ref, staying_ref, *boxes, cache_ref, qk, v, context = refs[len(w_last) :]
        tp, length = place_ref[0], length_ref[0]
        lane = lax.broadcasted_iota(jnp.int32, (tile, wide), 1)
        first = lax.rem(lane, head_dim) < half
        for t in range(seq_len // tile):
            at = slice(t * tile, (t + 1) * tile)
            rows = joined_ref[at, :]
            for i, w_ref in enumerate(w_refs):
                rows = rows + dot(x_ref[at, i * width : (i + 1) * width], w_ref[...])
            head = rows[:, :wide]
            ahead = pltpu.roll(head, wide - half, 1)
            behind = pltpu.roll(head, half, 1)
            cosine, sine = (
                jnp.concatenate([ref[at, :]] * (wide // half + 1), axis=1)[:, :wide]
                for ref in (cos_ref, sin_ref)
            )
            turned = head * cosine + jnp.where(first, -ahead, behind) * sine
            qk[at, :] = turned.astype(BF)
            v[at, :] = rows[:, q_cols + k_cols :].astype(BF)
            slot = t * tile + lax.broadcasted_iota(jnp.int32, (tile, 1), 0)
            live = (slot < length).astype(F32)
            cache_ref[at, :k_cols] = (turned[:, q_cols : q_cols + k_cols] * live).astype(BF)
            cache_ref[at, k_cols:] = (rows[:, q_cols + k_cols :] * live).astype(BF)
        for i in range(chosen.shape[0]):
            page = cache_ref[pl.ds(pl.multiple_of(chosen_ref[i] * PAGE, PAGE), PAGE), :]
            at, side = i % slots // 2 * PAGE, i % 2 * 2 * k_cols
            boxes[i // slots][at : at + PAGE, side : side + 2 * k_cols] = page
        for k in range(kv_heads):
            key_at = q_cols + k * head_dim
            for t in range(seq_len // tile):
                at = slice(t * tile, (t + 1) * tile)
                count = (t + 1) * tile
                q = jnp.concatenate(
                    [
                        qk[at, (k * group + g) * head_dim : (k * group + g + 1) * head_dim]
                        for g in range(group)
                    ],
                    axis=0,
                )
                scores = lax.dot_general(
                    q,
                    qk[:count, key_at : key_at + head_dim],
                    (((1,), (1,)), ((), ())),
                    preferred_element_type=F32,
                ) * head_dim ** (-0.5)
                shape = (tile, count)
                slot = t * tile + lax.broadcasted_iota(jnp.int32, shape, 0)
                key = lax.broadcasted_iota(jnp.int32, shape, 1)
                allowed = (key <= slot) & (key < length)
                scores = scores.reshape(group, tile, count)
                scores = jnp.where(allowed[None], scores, -1e30)
                top = jnp.max(scores, axis=-1, keepdims=True)
                weight = jnp.exp(scores - top)
                probs = (weight / jnp.sum(weight, axis=-1, keepdims=True)).astype(BF)
                mixed = dot(
                    probs.reshape(group * tile, count), v[:count, k * head_dim : (k + 1) * head_dim]
                ).astype(BF)
                for g in range(group):
                    h = k * group + g
                    context[at, h * head_dim : (h + 1) * head_dim] = mixed[
                        g * tile : (g + 1) * tile
                    ]
        for i, s in enumerate(shares):
            block = context[pl.ds(pl.multiple_of((tp ^ s) * share, share), share), :]
            product = dot(block, out_in_ref[...])
            j = i % (len(shares) // 2)
            if i < len(shares) // 2:
                staying_ref[j * share : (j + 1) * share, :] = product
            else:
                leaving_ref[j * share : (j + 1) * share, :] = product.astype(BF)

    return call(
        kernel,
        [place, lengths, chosen],
        [joined, x_last, *tables, out_in, *w_last],
        [
            ((seq_len // 2, model_dim), BF),
            ((seq_len // 2, model_dim), F32),
        ]
        + [((slots // 2 * PAGE, 4 * k_cols), BF)] * 2,
        [((seq_len, 2 * k_cols), BF), ((seq_len, wide), BF), ((seq_len, k_cols), BF), ((seq_len, q_cols), BF)],
        "attend",
    )


def assemble(blocks, n_tp, columns, flops=1):
    rows = blocks[0].shape[1]
    full, rest = divmod(columns, LANES)
    group = n_tp * rest // LANES

    def kernel(*refs):
        out_ref = refs[-1]
        for b, ref in enumerate(refs[:-1]):
            for t in range(n_tp):
                first = (b * n_tp + t) * rows
                at = slice(first, first + rows)
                for i in range(full):
                    out_ref[at, i * LANES : (i + 1) * LANES] = ref[i * n_tp + t]
                if rest:
                    side = t // group * rest
                    out_ref[at, full * LANES :] = ref[
                        full * n_tp + t % group, :, side : side + rest
                    ]

    shapes = [((len(blocks) * n_tp * rows, columns), BF)]
    return call(kernel, [], blocks, shapes, [], "assemble", 24, flops)[0]


def rows_product(pieces, weight, at, count, base=None, dtype=F32):
    columns = weight.shape[1]
    tile = 128

    def kernel(*refs):
        weight_ref = refs[len(pieces)]

        @pl.loop(0, count // tile)
        def _(i):
            out = pl.ds(pl.multiple_of(i * tile, tile), tile)
            total = 0.0 if base is None else refs[len(pieces) + 1][out, :]
            begin = at
            for (piece, first), ref in zip(pieces, refs):
                end = begin + piece.shape[1]
                source = pl.ds(pl.multiple_of(first + i * tile, tile), tile)
                total = total + dot(ref[source, :], weight_ref[begin:end, :])
                begin = end
            refs[-1][out, :] = total.astype(dtype)

    ins = [piece for piece, _ in pieces] + [weight] + ([] if base is None else [base])
    return call(kernel, [], ins, [((count, columns), dtype)], [], "rows_product", 24)[0]


def add_share(staying, arrived, extra):
    rows, columns = staying.shape
    half = rows // 2

    def kernel(staying_ref, arrived_ref, extra_ref, keep_ref, send_ref):
        keep_ref[...] = (
            staying_ref[:half, :] + arrived_ref[:half, :].astype(F32) + extra_ref[...]
        )
        send_ref[...] = (staying_ref[half:, :] + arrived_ref[half:, :].astype(F32)).astype(BF)

    return call(
        kernel,
        [],
        [staying, arrived, extra],
        [((half, columns), F32), ((half, columns), BF)],
        [],
        "add_share",
        24,
    )


def norm_share(keep, arrived, gain):
    rows, columns = keep.shape
    step = columns * PAIR // gain.shape[0]

    def kernel(keep_ref, arrived_ref, gain_ref, resid_ref, norm_ref, turned_ref):
        resid = keep_ref[...] + arrived_ref[...].astype(F32)
        resid_ref[...] = resid
        norm = normed(resid, gain_ref[...])
        norm_ref[...] = norm
        for i in range(columns // step):
            at, source = i * step, (i ^ 1) * step
            turned_ref[:, at : at + step] = norm[:, source : source + step]

    shapes = [((rows, columns), F32)] + [((rows, columns), BF)] * 2
    return call(
        kernel, [], [keep, arrived, gain.reshape(1, columns)], shapes, [], "norm_share", 24
    )


def pack_pages(pairs):
    width = pairs[0].shape[1] // 2

    def kernel(*refs):
        for j, ref in enumerate(refs[:-1]):
            at, side = j // 2 * PAGE, j % 2 * width
            refs[-1][at : at + PAGE, side : side + width] = ref[:, width:]

    shapes = [((len(pairs) // 2 * PAGE, 2 * width), BF)]
    return call(kernel, [], pairs, shapes, [], "pack_pages", 16)[0]


def pick_pages(source, pairs, arrived, count):
    width = arrived.shape[1] // 2

    def kernel(source_ref, *refs):
        pages = [ref[:, :width] for ref in refs[: len(pairs)]]
        for j in range(len(pairs)):
            at, side = j // 2 * PAGE, j % 2 * width
            pages.append(refs[len(pairs)][at : at + PAGE, side : side + width])
        for p in range(count):
            for i, page in enumerate(pages):

                @pl.when(source_ref[p] == i)
                def _(p=p, page=page):
                    refs[-1][p] = page

    shapes = [((count, PAGE, width), BF)]
    return call(kernel, [source], [*pairs, arrived], shapes, [], "pick_pages", 16, 5 * 10**9)[0]


def class_rows(place, weight):
    rows, columns = weight.shape
    half = rows // 2

    def kernel(place_ref, weight_ref, *outs):
        for k in range(2):
            begin = pl.multiple_of((place_ref[1] ^ k) * half, 16)
            outs[k][...] = weight_ref[pl.ds(begin, half), :]

    return call(kernel, [place], [weight], [((half, columns), BF)] * 2, [], "class_rows")


def gated(tokens, early, late):
    rows = tokens.shape[0]
    split, columns = early.shape
    size = columns // 2
    tile = 256

    def kernel(tokens_ref, early_ref, late_ref, out_ref):
        @pl.loop(0, rows // tile)
        def _(i):
            at = pl.ds(pl.multiple_of(i * tile, tile), tile)
            projected = dot(tokens_ref[at, :split], early_ref[...])
            projected = projected + dot(tokens_ref[at, split:], late_ref[...])
            gate, up = projected[:, :size], projected[:, size:]
            out_ref[at, :] = (gate / (1.0 + jnp.exp(-gate)) * up).astype(BF)

    return call(kernel, [], [tokens, early, late], [((rows, size), BF)], [], "gated", 24)[0]


def body(
    tokens,
    lengths,
    page_slot,
    trainer_layout,
    trainer_qkv,
    trainer_gateup,
    attn_gain,
    ffn_gain,
    out_proj,
    down_proj,
):
    n_tp = lax.axis_size("tp")
    n_req = lax.axis_size("req")
    devices = n_tp * n_req
    req = lax.axis_index("req")
    tp = lax.axis_index("tp")
    rows_each = trainer_qkv.shape[0]
    seq_len, model_dim = tokens.shape
    head_dim = HD
    local_heads = out_proj.shape[0] // head_dim
    group_cols = trainer_qkv.shape[1] // n_tp
    local_kv = (group_cols // head_dim - local_heads) // 2
    group = local_heads // local_kv
    q_cols = local_heads * head_dim
    k_cols = local_kv * head_dim
    ff_local = down_proj.shape[0]
    share = seq_len // n_tp

    def swap(value, req_mask, tp_mask):
        pairs = [(d, d ^ (req_mask * n_tp + tp_mask)) for d in range(devices)]
        return lax.ppermute(value, ("req", "tp"), pairs)

    def pick(stack, index):
        return lax.dynamic_index_in_dim(stack, index, 0, keepdims=False)

    def sync(values):
        return lax.optimization_barrier(values)

    halves = 2
    units = ff_local // halves
    chunks = list(CHUNKS) + [units - sum(CHUNKS)]
    bits = [1 << k for k in range(16) if 1 << k < n_tp]
    evens = list(range(2, n_req, 2))
    zbits = [1 << k for k in range(1, 16) if 1 << k < n_req]
    singles = [r for r in evens if r & (r - 1) == 0]
    doubles = [r for r in evens if r & (r - 1)]
    plain = [r for r in evens if not r & PAIR]
    crossed = [r for r in evens if r & PAIR and r != PAIR]

    def spread_z(held, group):
        for r in group:
            bit = r & -r
            held[r] = swap(held[r ^ bit], bit, 0)

    def spread_class(held, mine, other, group):
        for r in group:
            if r == PAIR:
                held[r] = swap(other, PAIR, 0)
                continue
            rest = r & ~PAIR
            bit = 1 << (rest.bit_length() - 1)
            held[r] = swap(held[r ^ bit] if r != bit else mine, bit, 0)

    place = jnp.stack([tp, (req // PAIR) % 2])
    qkv_split = split_qkv(place, trainer_qkv, n_tp)
    half = head_dim // 2
    freq = theta_base ** (-jnp.arange(half, dtype=F32) * 2.0 / head_dim)
    angles = jnp.arange(seq_len, dtype=F32)[:, None] * freq[None, :]
    tables = (jnp.cos(angles), jnp.sin(angles))
    trainer_gateup, qkv_split = sync((trainer_gateup, qkv_split))
    gu_own, gu_odd = split_gateup(place, trainer_gateup, n_tp, halves, chunks)
    qkv_split = [qkv_split[0]] + [swap(qkv_split[s], 0, s) for s in range(1, n_tp)]
    st = sync(
        dict(
            qkv_split=qkv_split,
            gu_own=gu_own,
            gu_odd=gu_odd,
            tokens=tokens,
            layout=trainer_layout,
            tables=tables,
        )
    )

    tokens, trainer_layout, tables = st["tokens"], st["layout"], st["tables"]
    gu_own, gu_near = st["gu_own"], swap(st["gu_odd"], 0, 1)
    qkv_own = join_qkv(place, st["qkv_split"])
    qkv = {0: qkv_own}
    spread_z(qkv, singles)
    qkv[1] = swap(qkv_own, 1, 0)
    far = list(pack_far(place, gu_own, gu_near, chunks))
    tokens, far = sync((tokens, far))

    def over_y(value):
        moved = [swap(value[f], 0, 2 * f + 2) for f in range(n_tp // 2 - 1)]
        return jnp.stack(moved) if len(moved) > 1 else moved[0][None]

    blocks = [join_gateup(place, gu_own, gu_near, over_y(far[0]), 0)]
    order = jnp.arange(n_req, dtype=jnp.int32) ^ req
    shards = (order[:, None] * n_tp + jnp.arange(n_tp, dtype=jnp.int32)[None, :]).reshape(-1)
    blocks_at = trainer_layout[shards]
    columns_at = (
        blocks_at[:, None] * rows_each + jnp.arange(rows_each, dtype=jnp.int32)[None, :]
    ).reshape(-1)
    columns_back = (
        jnp.argmax(
            blocks_at[None, :] == jnp.arange(devices, dtype=jnp.int32)[:, None], axis=1
        ).astype(jnp.int32)[:, None]
        * rows_each
        + jnp.arange(rows_each, dtype=jnp.int32)[None, :]
    ).reshape(-1)
    gain_in = attn_gain.reshape(devices, rows_each)[blocks_at].reshape(-1)
    tokens_in, x_norm = permute_columns(tokens, columns_at, gain_in)
    st = sync(
        dict(
            qkv=qkv,
            far=far[1],
            blocks=blocks,
            gu_own=gu_own,
            gu_near=gu_near,
            x_norm=x_norm,
            tokens_in=tokens_in,
            onehot_at=columns_at,
            out_proj=out_proj,
            down_proj=down_proj,
            page_slot=page_slot,
            ffn_gain=ffn_gain,
        )
    )

    qkv, far, x_norm, tokens_in = st["qkv"], st["far"], st["x_norm"], st["tokens_in"]
    columns_at, page_slot = st["onehot_at"], st["page_slot"]
    blocks = list(st["blocks"])
    blocks.append(join_gateup(place, st["gu_own"], st["gu_near"], over_y(far), 2 * chunks[0]))
    gu = [dict() for _ in chunks]
    spread_class(gu[0], *blocks[0], plain)
    spread_z(qkv, doubles)
    for r in singles[::-1]:
        qkv[r ^ 1] = swap(qkv[r], 1, 0)
    out_in = permute_columns(st["out_proj"], columns_at, dtype=BF)
    down_rel = class_rows(place, st["down_proj"])
    ffn_gain_in = st["ffn_gain"].reshape(devices, rows_each)[blocks_at].reshape(-1)
    n_pages = seq_len // PAGE
    holders = lax.dynamic_slice_in_dim(page_slot, req * n_pages, n_pages, 0) // n_pages
    page_bits = [PAIR, 1] + [bit for bit in zbits if bit != PAIR]
    at_slot = [
        sum(bit for k, bit in enumerate(reversed(page_bits)) if (i >> k) & 1)
        for i in range(n_req)
    ]
    relative = jnp.asarray(at_slot, jnp.int32) ^ req
    chosen = jnp.argmax(holders[None, :] == relative[:, None], axis=1)
    targets = req * n_pages + jnp.arange(n_pages, dtype=jnp.int32)
    source = jnp.argmax(page_slot[None, :] == targets[:, None], axis=1) // n_pages
    arrival = [0]
    for bit in page_bits:
        arrival = arrival + [r ^ bit for r in arrival]
    arrival = jnp.asarray(arrival, jnp.int32) ^ req
    source = jnp.argmax(arrival[None, :] == source[:, None], axis=1)
    tokens_share = lax.dynamic_slice_in_dim(tokens_in, tp * share, share, 0)
    st = sync(
        dict(
            qkv=qkv,
            gu=gu,
            blocks=blocks,
            x_norm=x_norm,
            out_in=out_in,
            down_rel=down_rel,
            ffn_gain_in=ffn_gain_in,
            pages=(chosen, source),
            tokens_share=tokens_share,
        )
    )

    qkv, gu, blocks, x_norm, out_in = (st[k] for k in ("qkv", "gu", "blocks", "x_norm", "out_in"))
    chosen, source = st["pages"]
    tokens_share = st["tokens_share"]
    down_rel, ffn_gain_in = st["down_rel"], st["ffn_gain_in"]
    spread_class(gu[0], *blocks[0], [PAIR])
    spread_class(gu[1], *blocks[1], plain)
    for r in doubles:
        qkv[r ^ 1] = swap(qkv[r], 1, 0)
    gu[1][0] = blocks[1][0]
    gu[1][1] = swap(blocks[1][0], 1, 0)
    width = model_dim // n_req
    first = [0, 1] + [r | j for r in singles for j in (0, 1)]
    last = [r | j for r in doubles for j in (0, 1)]

    def part(rs):
        return dot(
            jnp.concatenate([x_norm[:, r * width : (r + 1) * width] for r in rs], axis=1),
            assemble([qkv[r] for r in rs], n_tp, group_cols),
        )

    joined = part(first)
    st = sync(dict(qkv=qkv, gu=gu, blocks=blocks, joined=joined, x_norm=x_norm))

    qkv, gu, blocks, x_norm = (st[k] for k in ("qkv", "gu", "blocks", "x_norm"))
    spread_class(gu[0], *blocks[0], crossed)
    spread_class(gu[1], *blocks[1], [PAIR])
    gu[0][0] = blocks[0][0]
    gu[0][1] = swap(blocks[0][0], 1, 0)
    for r in plain:
        gu[0][r ^ 1] = swap(gu[0][r], 1, 0)
    shares = sorted(range(n_tp), key=lambda s: [(s >> k) & 1 for k in range(len(bits))])
    leaving, staying, *box = attend(
        place,
        lengths,
        chosen.astype(jnp.int32),
        st["joined"],
        jnp.concatenate([x_norm[:, r * width : (r + 1) * width] for r in last], axis=1),
        [assemble([qkv[r] for r in last], n_tp, group_cols)],
        tables,
        out_in,
        (local_heads, local_kv, head_dim),
        shares,
    )
    st = sync(dict(gu=gu, leaving=leaving, staying=staying, box=box))

    gu, box = st["gu"], st["box"]
    keep, send = add_share(st["staying"], swap(st["leaving"], 0, bits[0]), tokens_share)
    arrived = swap(send, 0, bits[1])
    spread_class(gu[1], None, None, crossed)
    gu[0][PAIR ^ 1] = swap(gu[0][PAIR], 1, 0)
    for r in plain:
        gu[1][r ^ 1] = swap(gu[1][r], 1, 0)

    def page_parts(box):
        half = box[0].shape[0] // 2
        return [pages[:half] for pages in box], jnp.concatenate(
            [pages[half:] for pages in box], axis=0
        )

    def page_step(parts, bit):
        kept, leaving = parts
        half = kept[0].shape[0]
        moved = swap(leaving, bit, 0)
        return kept + [moved[at : at + half] for at in range(0, leaving.shape[0], half)]

    late = crossed[0]
    box = [box[0], swap(box[1], page_bits[0], 0)]
    gu[1][late] = hold(gu[1][late], box[1], gu[0][PAIR ^ 1], *[gu[1][r ^ 1] for r in plain])
    resid_in, h_share, h_leaving = norm_share(
        keep, arrived, ffn_gain_in.reshape(n_req, model_dim // n_req)
    )
    st = sync(dict(gu=gu, h=(h_share, h_leaving), resid_in=resid_in, box=box))

    gu, resid_in = st["gu"], st["resid_in"]
    h_share, h_leaving = st["h"]
    cross = n_tp // 2
    own = (h_share, swap(h_share, 0, cross))
    theirs = (swap(h_leaving, PAIR, 0), swap(h_leaving, PAIR, cross))
    for r in crossed:
        gu[0][r ^ 1] = swap(gu[0][r], 1, 0)
    gu[1][PAIR ^ 1] = swap(gu[1][PAIR], 1, 0)
    coarse = resid_in.astype(BF)
    fine = (resid_in - coarse.astype(F32)).astype(BF)
    terms = permute_columns(jnp.concatenate([coarse, fine], axis=0), columns_back)
    early = assemble([gu[0][r] for r in range(n_req - 2)], n_tp, 2 * chunks[0])
    st = sync(dict(gu=gu, own=own, theirs=theirs, terms=terms, early=early, box=page_parts(st["box"])))

    gu, box = st["gu"], st["box"]
    resid = st["terms"][:share] + st["terms"][share:]
    own, theirs = (jnp.concatenate(st[k], axis=0) for k in ("own", "theirs"))
    pair = [n_req - 2, n_req - 1]
    first = (st["early"], assemble([gu[0][r] for r in pair], n_tp, 2 * chunks[0]))
    hidden = gated(theirs, *first)
    returned = [swap(hidden, PAIR, 0)]
    own_next, theirs_next = swap(own, 0, bits[0]), swap(theirs, 0, bits[0])
    for r in crossed:
        gu[1][r ^ 1] = swap(gu[1][r], 1, 0)
    hidden = gated(theirs_next, *first)
    h_own = jnp.concatenate([own, own_next], axis=0)
    h_theirs = jnp.concatenate([theirs, theirs_next], axis=0)
    early = assemble([gu[1][r] for r in range(n_req - 2)], n_tp, 2 * chunks[1])
    ready, early = sync((gu[1][pair[0]], early))
    second = (early, assemble([ready, gu[1][pair[1]]], n_tp, 2 * chunks[1], 4 * 10**9))
    weights = [first, second]
    st = sync(
        dict(
            weights=weights,
            h=(h_own, h_theirs),
            hidden=(hidden, returned),
            resid=resid,
            box=box,
        )
    )

    resid, box = st["resid"], st["box"]
    h_own, h_theirs = st["h"]
    hidden, returned = st["hidden"]
    returned = list(returned) + [swap(hidden, PAIR, 0)]
    weights = st["weights"]
    theirs = gated(h_theirs, *weights[1])
    h_own, theirs = sync((h_own, theirs))
    kept = [gated(h_own, *weight) for weight in weights]
    rows = seq_len // 2
    product = []
    for i in range(2):
        part = rows_product([(piece, i * rows) for piece in kept], down_rel[0], 0, rows)
        product.append(rows_product([(returned[i], 0)], down_rel[1], 0, rows, part))
    for bit in page_bits[1:-1]:
        box = page_step(box if bit == page_bits[1] else page_parts(box), bit)
    leaving_pages = pack_pages(box)
    returned, box, leaving_pages, product = sync(
        (swap(theirs, PAIR, 0), box, leaving_pages, product)
    )
    leaving = rows_product([(returned, rows)], down_rel[1], chunks[0], rows, product[1], BF)
    arrived = swap(leaving, 0, bits[0])
    staying = rows_product([(returned, 0)], down_rel[1], chunks[0], rows, product[0])
    keep, send = add_share(staying, arrived, resid)
    arrived_pages = swap(leaving_pages, page_bits[-1], 0)
    share_slots = tp * share + jnp.arange(share, dtype=jnp.int32)
    live_share = (share_slots < lengths[0]).astype(F32)
    layer_out = ((keep + swap(send, 0, bits[1]).astype(F32)) * live_share[:, None]).astype(BF)
    kv_cache = pick_pages(source.astype(jnp.int32), box, arrived_pages, n_pages)
    return (layer_out, kv_cache)


def solution(mesh):
    return jax.shard_map(
        body,
        mesh=mesh,
        in_specs=(
            P("req", None),
            P("req"),
            P(),
            P(),
            P(("req", "tp"), None),
            P(("req", "tp"), None),
            P(),
            P(),
            P("tp", None),
            P("tp", None),
        ),
        out_specs=(P(("req", "tp"), None), P("req", None, "tp")),
        check_vma=False,
    )
```

```python
import jax
import jax.numpy as jnp
from jax import lax
from jax.experimental import pallas as pl
from jax.experimental.pallas import tpu as pltpu
from jax.sharding import PartitionSpec as P

HD = 80
PAGE = 128
BF = jnp.bfloat16
F32 = jnp.float32

eps_norm = 1e-05
theta_base = 10000.0

PAIR = 2
CHUNKS = (512,)


def normed(values, gain):
    scale = lax.rsqrt(jnp.mean(values * values, axis=-1, keepdims=True) + eps_norm)
    return (values * scale * gain).astype(BF)


def dot(a, b):
    return jnp.dot(a, b, preferred_element_type=F32)


def on_device(kernel, place, ins, shapes, vmem_mib, name):
    def run(place_ref, *refs):
        n_in, n_out = len(ins), len(shapes)
        outs, bufs, sems = refs[n_in : n_in + n_out], refs[n_in + n_out : -1], refs[-1]
        kernel(place_ref, *refs[:n_in], *bufs)
        copies = [pltpu.make_async_copy(bufs[i], outs[i], sems.at[i]) for i in range(n_out)]
        for copy in copies:
            copy.start()
        for copy in copies:
            copy.wait()

    return pl.pallas_call(
        run,
        in_specs=[pl.BlockSpec(memory_space=pltpu.SMEM)]
        + [pl.BlockSpec(memory_space=pltpu.VMEM)] * len(ins),
        out_specs=[pl.BlockSpec(memory_space=pltpu.HBM)] * len(shapes),
        out_shape=[jax.ShapeDtypeStruct(shape, BF) for shape in shapes],
        scratch_shapes=[pltpu.VMEM(shape, BF) for shape in shapes]
        + [pltpu.SemaphoreType.DMA((len(shapes),))],
        compiler_params=pltpu.CompilerParams(vmem_limit_bytes=vmem_mib * 2**20),
        cost_estimate=pl.CostEstimate(flops=1, transcendentals=0, bytes_accessed=1),
        name=name,
    )(place, *ins)


def split_qkv(place, shard, n_tp):
    rows, columns = shard.shape
    width = columns // n_tp

    def kernel(place_ref, shard_ref, *bufs):
        tp = place_ref[0]
        for s in range(n_tp):
            for g in range(n_tp):

                @pl.when((tp ^ s) == g)
                def _(s=s, g=g):
                    bufs[s][...] = shard_ref[:, g * width : (g + 1) * width].astype(BF)

    return on_device(kernel, place, [shard], [(rows, width)] * n_tp, 60, "split_qkv")


def split_gateup(place, shard, n_tp, halves, chunks):
    rows, columns = shard.shape
    width = columns // n_tp
    units = width // 2 // halves

    def kernel(place_ref, shard_ref, *bufs):
        tp = place_ref[0]
        for s in range(n_tp):
            begin = pl.multiple_of((tp ^ s) * width, 128)
            group = shard_ref[:, pl.ds(begin, width)].astype(BF)
            for q in range(halves):
                start = q * units
                edge = 0
                for size in chunks:
                    up = width // 2 + start
                    bufs[s % 2][s // 2, q, :, edge : edge + 2 * size] = jnp.concatenate(
                        [group[:, start : start + size], group[:, up : up + size]], axis=1
                    )
                    start += size
                    edge += 2 * size

    shapes = [(n_tp // 2, halves, rows, 2 * units)] * 2
    return on_device(kernel, place, [shard], shapes, 60, "split_gateup")


def pack_far(place, own, near, chunks):
    n_far, halves, rows, _ = own.shape
    n_far -= 1

    def kernel(place_ref, own_ref, near_ref, *bufs):
        edge = 0
        for c, size in enumerate(chunks):
            for f in range(n_far):
                bufs[c][f, 0] = own_ref[f + 1, :, :, edge : edge + 2 * size]
                bufs[c][f, 1] = near_ref[f + 1, :, :, edge : edge + 2 * size]
            edge += 2 * size

    shapes = [(n_far, 2, halves, rows, 2 * size) for size in chunks]
    return on_device(kernel, place, [own, near], shapes, 60, "pack_far")


LANES = 128


def packed_shape(n_tp, rows, columns):
    full, rest = divmod(columns, LANES)
    return (full * n_tp + -(-rest * n_tp // LANES), rows, LANES)


def pack_rows(buf, t, n_tp, piece):
    full, rest = divmod(piece.shape[1], LANES)
    for i in range(full):
        buf[i * n_tp + t] = piece[:, i * LANES : (i + 1) * LANES]
    if rest:
        group = n_tp * rest // LANES
        for side in range(LANES // rest):

            @pl.when(lax.div(t, group) == side)
            def _(side=side):
                buf[full * n_tp + lax.rem(t, group), :, side * rest : (side + 1) * rest] = piece[
                    :, full * LANES :
                ]


def join_qkv(place, parts):
    rows, columns = parts[0].shape
    n_tp = len(parts)

    def kernel(place_ref, *refs):
        for s in range(n_tp):
            pack_rows(refs[n_tp], place_ref[0] ^ s, n_tp, refs[s][...])

    shapes = [packed_shape(n_tp, rows, columns)]
    return on_device(kernel, place, parts, shapes, 60, "join_qkv")[0]


def join_gateup(place, own, near, far, start):
    n_far, _, halves, rows, columns = far.shape
    n_tp = 2 * n_far + 2

    def kernel(place_ref, own_ref, near_ref, far_ref, *bufs):
        tp, mine = place_ref[0], place_ref[1]
        for k in range(2):
            q = mine ^ k
            pack_rows(bufs[k], tp, n_tp, own_ref[0, q, :, start : start + columns])
            pack_rows(bufs[k], tp ^ 1, n_tp, near_ref[0, q, :, start : start + columns])
            for f in range(n_far):
                for j in range(2):
                    pack_rows(bufs[k], tp ^ (2 * f + 2 + j), n_tp, far_ref[f, j, q])

    shapes = [packed_shape(n_tp, rows, columns)] * 2
    return on_device(kernel, place, [own, near, far], shapes, 60, "join_gateup")


SMEM = pl.BlockSpec(memory_space=pltpu.SMEM)
VMEM = pl.BlockSpec(memory_space=pltpu.VMEM)


def call(kernel, smem, vmem, shapes, scratch, name, mib=48, flops=1):
    return pl.pallas_call(
        kernel,
        in_specs=[SMEM] * len(smem) + [VMEM] * len(vmem),
        out_specs=[VMEM] * len(shapes),
        out_shape=[jax.ShapeDtypeStruct(*shape) for shape in shapes],
        scratch_shapes=[pltpu.VMEM(*shape) for shape in scratch],
        compiler_params=pltpu.CompilerParams(vmem_limit_bytes=mib * 2**20),
        cost_estimate=pl.CostEstimate(flops=flops, transcendentals=0, bytes_accessed=1),
        name=name,
    )(*smem, *vmem)


def permute_columns(values, columns_at, gain=None, dtype=F32):
    rows, width = values.shape
    tile = 256

    def kernel(values_ref, at_ref, *refs):
        out_ref = refs[0] if gain is None else refs[1]

        @pl.loop(0, width // tile)
        def _(i):
            at = pl.ds(pl.multiple_of(i * tile, tile), tile)
            source = lax.broadcasted_iota(jnp.int32, (width, tile), 0)
            onehot = (source == at_ref[:, at]).astype(F32).astype(BF)
            out_ref[:, at] = dot(values_ref[...], onehot).astype(dtype)

        if gain is not None:

            @pl.loop(0, rows // 128)
            def _(i):
                at = pl.ds(pl.multiple_of(i * 128, 128), 128)
                refs[2][at, :] = normed(out_ref[at, :], refs[0][...])

    ins = [values, columns_at[None]] + ([] if gain is None else [gain[None]])
    shapes = [((rows, width), dtype)] + ([] if gain is None else [((rows, width), BF)])
    outs = call(kernel, [], ins, shapes, [], "permute_columns")
    return outs[0] if gain is None else outs


def hold(value, *others):
    def kernel(*refs):
        pass

    return pl.pallas_call(
        kernel,
        in_specs=[pl.BlockSpec(memory_space=pl.ANY)] * (1 + len(others)),
        out_specs=pl.BlockSpec(memory_space=pl.ANY),
        out_shape=jax.ShapeDtypeStruct(value.shape, value.dtype),
        input_output_aliases={0: 0},
        cost_estimate=pl.CostEstimate(flops=10**11, transcendentals=0, bytes_accessed=10**8),
        name="hold",
    )(value, *others)


def attend(place, lengths, chosen, joined, x_last, w_last, tables, out_in, sizes, shares):
    seq_len, columns = joined.shape
    heads, kv_heads, head_dim = sizes
    group = heads // kv_heads
    q_cols, k_cols = heads * head_dim, kv_heads * head_dim
    half = head_dim // 2
    wide = (q_cols + k_cols + 127) // 128 * 128
    width = w_last[0].shape[0]
    model_dim = out_in.shape[1]
    share = seq_len // len(shares)
    slots = chosen.shape[0] // 2
    tile = 128

    def kernel(
        place_ref, length_ref, chosen_ref, joined_ref, x_ref, cos_ref, sin_ref, out_in_ref, *refs
    ):
        w_refs = refs[: len(w_last)]
        leaving_ref, staying_ref, *boxes, cache_ref, qk, v, context = refs[len(w_last) :]
        tp, length = place_ref[0], length_ref[0]
        lane = lax.broadcasted_iota(jnp.int32, (tile, wide), 1)
        first = lax.rem(lane, head_dim) < half
        for t in range(seq_len // tile):
            at = slice(t * tile, (t + 1) * tile)
            rows = joined_ref[at, :]
            for i, w_ref in enumerate(w_refs):
                rows = rows + dot(x_ref[at, i * width : (i + 1) * width], w_ref[...])
            head = rows[:, :wide]
            ahead = pltpu.roll(head, wide - half, 1)
            behind = pltpu.roll(head, half, 1)
            cosine, sine = (
                jnp.concatenate([ref[at, :]] * (wide // half + 1), axis=1)[:, :wide]
                for ref in (cos_ref, sin_ref)
            )
            turned = head * cosine + jnp.where(first, -ahead, behind) * sine
            qk[at, :] = turned.astype(BF)
            v[at, :] = rows[:, q_cols + k_cols :].astype(BF)
            slot = t * tile + lax.broadcasted_iota(jnp.int32, (tile, 1), 0)
            live = (slot < length).astype(F32)
            cache_ref[at, :k_cols] = (turned[:, q_cols : q_cols + k_cols] * live).astype(BF)
            cache_ref[at, k_cols:] = (rows[:, q_cols + k_cols :] * live).astype(BF)
        for i in range(chosen.shape[0]):
            page = cache_ref[pl.ds(pl.multiple_of(chosen_ref[i] * PAGE, PAGE), PAGE), :]
            at, side = i % slots // 2 * PAGE, i % 2 * 2 * k_cols
            boxes[i // slots][at : at + PAGE, side : side + 2 * k_cols] = page
        for k in range(kv_heads):
            key_at = q_cols + k * head_dim
            for t in range(seq_len // tile):
                at = slice(t * tile, (t + 1) * tile)
                count = (t + 1) * tile
                q = jnp.concatenate(
                    [
                        qk[at, (k * group + g) * head_dim : (k * group + g + 1) * head_dim]
                        for g in range(group)
                    ],
                    axis=0,
                )
                scores = lax.dot_general(
                    q,
                    qk[:count, key_at : key_at + head_dim],
                    (((1,), (1,)), ((), ())),
                    preferred_element_type=F32,
                ) * head_dim ** (-0.5)
                shape = (tile, count)
                slot = t * tile + lax.broadcasted_iota(jnp.int32, shape, 0)
                key = lax.broadcasted_iota(jnp.int32, shape, 1)
                allowed = (key <= slot) & (key < length)
                scores = scores.reshape(group, tile, count)
                scores = jnp.where(allowed[None], scores, -1e30)
                top = jnp.max(scores, axis=-1, keepdims=True)
                weight = jnp.exp(scores - top)
                probs = (weight / jnp.sum(weight, axis=-1, keepdims=True)).astype(BF)
                mixed = dot(
                    probs.reshape(group * tile, count), v[:count, k * head_dim : (k + 1) * head_dim]
                ).astype(BF)
                for g in range(group):
                    h = k * group + g
                    context[at, h * head_dim : (h + 1) * head_dim] = mixed[
                        g * tile : (g + 1) * tile
                    ]
        for i, s in enumerate(shares):
            block = context[pl.ds(pl.multiple_of((tp ^ s) * share, share), share), :]
            product = dot(block, out_in_ref[...])
            j = i % (len(shares) // 2)
            if i < len(shares) // 2:
                staying_ref[j * share : (j + 1) * share, :] = product
            else:
                leaving_ref[j * share : (j + 1) * share, :] = product.astype(BF)

    return call(
        kernel,
        [place, lengths, chosen],
        [joined, x_last, *tables, out_in, *w_last],
        [
            ((seq_len // 2, model_dim), BF),
            ((seq_len // 2, model_dim), F32),
        ]
        + [((slots // 2 * PAGE, 4 * k_cols), BF)] * 2,
        [((seq_len, 2 * k_cols), BF), ((seq_len, wide), BF), ((seq_len, k_cols), BF), ((seq_len, q_cols), BF)],
        "attend",
    )


def assemble(blocks, n_tp, columns, flops=1):
    rows = blocks[0].shape[1]
    full, rest = divmod(columns, LANES)
    group = n_tp * rest // LANES

    def kernel(*refs):
        out_ref = refs[-1]
        for b, ref in enumerate(refs[:-1]):
            for t in range(n_tp):
                first = (b * n_tp + t) * rows
                at = slice(first, first + rows)

                @pl.loop(0, full)
                def _(i, at=at, ref=ref, t=t):
                    lanes = pl.ds(pl.multiple_of(i * LANES, LANES), LANES)
                    out_ref[at, lanes] = ref[i * n_tp + t]

                if rest:
                    side = t // group * rest
                    out_ref[at, full * LANES :] = ref[
                        full * n_tp + t % group, :, side : side + rest
                    ]

    shapes = [((len(blocks) * n_tp * rows, columns), BF)]
    return call(kernel, [], blocks, shapes, [], "assemble", 24, flops)[0]


def rows_product(pieces, weight, at, count, base=None, dtype=F32):
    columns = weight.shape[1]
    tile = 128

    def kernel(*refs):
        weight_ref = refs[len(pieces)]

        @pl.loop(0, count // tile)
        def _(i):
            out = pl.ds(pl.multiple_of(i * tile, tile), tile)
            total = 0.0 if base is None else refs[len(pieces) + 1][out, :]
            begin = at
            for (piece, first), ref in zip(pieces, refs):
                end = begin + piece.shape[1]
                source = pl.ds(pl.multiple_of(first + i * tile, tile), tile)
                total = total + dot(ref[source, :], weight_ref[begin:end, :])
                begin = end
            refs[-1][out, :] = total.astype(dtype)

    ins = [piece for piece, _ in pieces] + [weight] + ([] if base is None else [base])
    return call(kernel, [], ins, [((count, columns), dtype)], [], "rows_product", 24)[0]


def add_share(staying, arrived, extra):
    rows, columns = staying.shape
    half = rows // 2

    def kernel(staying_ref, arrived_ref, extra_ref, keep_ref, send_ref):
        keep_ref[...] = (
            staying_ref[:half, :] + arrived_ref[:half, :].astype(F32) + extra_ref[...]
        )
        send_ref[...] = (staying_ref[half:, :] + arrived_ref[half:, :].astype(F32)).astype(BF)

    return call(
        kernel,
        [],
        [staying, arrived, extra],
        [((half, columns), F32), ((half, columns), BF)],
        [],
        "add_share",
        24,
    )


def norm_share(keep, arrived, gain):
    rows, columns = keep.shape
    step = columns * PAIR // gain.shape[0]

    def kernel(keep_ref, arrived_ref, gain_ref, resid_ref, norm_ref, turned_ref):
        resid = keep_ref[...] + arrived_ref[...].astype(F32)
        resid_ref[...] = resid
        norm = normed(resid, gain_ref[...])
        norm_ref[...] = norm
        for i in range(columns // step):
            at, source = i * step, (i ^ 1) * step
            turned_ref[:, at : at + step] = norm[:, source : source + step]

    shapes = [((rows, columns), F32)] + [((rows, columns), BF)] * 2
    return call(
        kernel, [], [keep, arrived, gain.reshape(1, columns)], shapes, [], "norm_share", 24
    )


def pack_pages(pairs):
    width = pairs[0].shape[1] // 2

    def kernel(*refs):
        for j, ref in enumerate(refs[:-1]):
            at, side = j // 2 * PAGE, j % 2 * width
            refs[-1][at : at + PAGE, side : side + width] = ref[:, width:]

    shapes = [((len(pairs) // 2 * PAGE, 2 * width), BF)]
    return call(kernel, [], pairs, shapes, [], "pack_pages", 16)[0]


def pick_pages(source, pairs, arrived, count):
    width = arrived.shape[1] // 2

    def kernel(source_ref, *refs):
        pages = [ref[:, :width] for ref in refs[: len(pairs)]]
        for j in range(len(pairs)):
            at, side = j // 2 * PAGE, j % 2 * width
            pages.append(refs[len(pairs)][at : at + PAGE, side : side + width])
        for p in range(count):
            for i, page in enumerate(pages):

                @pl.when(source_ref[p] == i)
                def _(p=p, page=page):
                    refs[-1][p] = page

    shapes = [((count, PAGE, width), BF)]
    return call(kernel, [source], [*pairs, arrived], shapes, [], "pick_pages", 16, 5 * 10**9)[0]


def class_rows(place, weight):
    rows, columns = weight.shape
    half = rows // 2

    def kernel(place_ref, weight_ref, *outs):
        for k in range(2):
            begin = pl.multiple_of((place_ref[1] ^ k) * half, 16)
            outs[k][...] = weight_ref[pl.ds(begin, half), :]

    return call(kernel, [place], [weight], [((half, columns), BF)] * 2, [], "class_rows")


def gated(tokens, weight, parts=1):
    rows = tokens.shape[0] // parts
    size = weight.shape[1] // 2
    tile = 256

    def kernel(tokens_ref, weight_ref, *outs):
        for p, out_ref in enumerate(outs):

            @pl.loop(0, rows // tile)
            def _(i, p=p, out_ref=out_ref):
                source = pl.ds(pl.multiple_of(p * rows + i * tile, tile), tile)
                projected = dot(tokens_ref[source, :], weight_ref[...])
                gate, up = projected[:, :size], projected[:, size:]
                out_ref[pl.ds(pl.multiple_of(i * tile, tile), tile), :] = (
                    gate / (1.0 + jnp.exp(-gate)) * up
                ).astype(BF)

    shapes = [((rows, size), BF)] * parts
    return call(kernel, [], [tokens, weight], shapes, [], "gated", 24)


def body(
    tokens,
    lengths,
    page_slot,
    trainer_layout,
    trainer_qkv,
    trainer_gateup,
    attn_gain,
    ffn_gain,
    out_proj,
    down_proj,
):
    n_tp = lax.axis_size("tp")
    n_req = lax.axis_size("req")
    devices = n_tp * n_req
    req = lax.axis_index("req")
    tp = lax.axis_index("tp")
    rows_each = trainer_qkv.shape[0]
    seq_len, model_dim = tokens.shape
    head_dim = HD
    local_heads = out_proj.shape[0] // head_dim
    group_cols = trainer_qkv.shape[1] // n_tp
    local_kv = (group_cols // head_dim - local_heads) // 2
    group = local_heads // local_kv
    q_cols = local_heads * head_dim
    k_cols = local_kv * head_dim
    ff_local = down_proj.shape[0]
    share = seq_len // n_tp

    def swap(value, req_mask, tp_mask):
        pairs = [(d, d ^ (req_mask * n_tp + tp_mask)) for d in range(devices)]
        return lax.ppermute(value, ("req", "tp"), pairs)

    def pick(stack, index):
        return lax.dynamic_index_in_dim(stack, index, 0, keepdims=False)

    def sync(values):
        return lax.optimization_barrier(values)

    halves = 2
    units = ff_local // halves
    chunks = list(CHUNKS) + [units - sum(CHUNKS)]
    bits = [1 << k for k in range(16) if 1 << k < n_tp]
    evens = list(range(2, n_req, 2))
    zbits = [1 << k for k in range(1, 16) if 1 << k < n_req]
    singles = [r for r in evens if r & (r - 1) == 0]
    doubles = [r for r in evens if r & (r - 1)]
    plain = [r for r in evens if not r & PAIR]
    crossed = [r for r in evens if r & PAIR and r != PAIR]

    def spread_z(held, group):
        for r in group:
            bit = r & -r
            held[r] = swap(held[r ^ bit], bit, 0)

    def spread_class(held, mine, other, group):
        for r in group:
            if r == PAIR:
                held[r] = swap(other, PAIR, 0)
                continue
            rest = r & ~PAIR
            bit = 1 << (rest.bit_length() - 1)
            held[r] = swap(held[r ^ bit] if r != bit else mine, bit, 0)

    place = jnp.stack([tp, (req // PAIR) % 2])
    qkv_split = split_qkv(place, trainer_qkv, n_tp)
    half = head_dim // 2
    freq = theta_base ** (-jnp.arange(half, dtype=F32) * 2.0 / head_dim)
    angles = jnp.arange(seq_len, dtype=F32)[:, None] * freq[None, :]
    tables = (jnp.cos(angles), jnp.sin(angles))
    trainer_gateup, qkv_split = sync((trainer_gateup, qkv_split))
    gu_own, gu_odd = split_gateup(place, trainer_gateup, n_tp, halves, chunks)
    qkv_split = [qkv_split[0]] + [swap(qkv_split[s], 0, s) for s in range(1, n_tp)]
    st = sync(
        dict(
            qkv_split=qkv_split,
            gu_own=gu_own,
            gu_odd=gu_odd,
            tokens=tokens,
            layout=trainer_layout,
            tables=tables,
        )
    )

    tokens, trainer_layout, tables = st["tokens"], st["layout"], st["tables"]
    gu_own, gu_near = st["gu_own"], swap(st["gu_odd"], 0, 1)
    qkv_own = join_qkv(place, st["qkv_split"])
    qkv = {0: qkv_own}
    spread_z(qkv, singles)
    qkv[1] = swap(qkv_own, 1, 0)
    far = list(pack_far(place, gu_own, gu_near, chunks))
    tokens, far = sync((tokens, far))

    def over_y(value):
        moved = [swap(value[f], 0, 2 * f + 2) for f in range(n_tp // 2 - 1)]
        return jnp.stack(moved) if len(moved) > 1 else moved[0][None]

    blocks = [join_gateup(place, gu_own, gu_near, over_y(far[0]), 0)]
    order = jnp.arange(n_req, dtype=jnp.int32) ^ req
    shards = (order[:, None] * n_tp + jnp.arange(n_tp, dtype=jnp.int32)[None, :]).reshape(-1)
    blocks_at = trainer_layout[shards]
    columns_at = (
        blocks_at[:, None] * rows_each + jnp.arange(rows_each, dtype=jnp.int32)[None, :]
    ).reshape(-1)
    columns_back = (
        jnp.argmax(
            blocks_at[None, :] == jnp.arange(devices, dtype=jnp.int32)[:, None], axis=1
        ).astype(jnp.int32)[:, None]
        * rows_each
        + jnp.arange(rows_each, dtype=jnp.int32)[None, :]
    ).reshape(-1)
    gain_in = attn_gain.reshape(devices, rows_each)[blocks_at].reshape(-1)
    tokens_in, x_norm = permute_columns(tokens, columns_at, gain_in)
    st = sync(
        dict(
            qkv=qkv,
            far=far[1],
            blocks=blocks,
            gu_own=gu_own,
            gu_near=gu_near,
            x_norm=x_norm,
            tokens_in=tokens_in,
            onehot_at=columns_at,
            out_proj=out_proj,
            down_proj=down_proj,
            page_slot=page_slot,
            ffn_gain=ffn_gain,
        )
    )

    qkv, far, x_norm, tokens_in = st["qkv"], st["far"], st["x_norm"], st["tokens_in"]
    columns_at, page_slot = st["onehot_at"], st["page_slot"]
    blocks = list(st["blocks"])
    blocks.append(join_gateup(place, st["gu_own"], st["gu_near"], over_y(far), 2 * chunks[0]))
    gu = [dict() for _ in chunks]
    spread_class(gu[0], *blocks[0], plain)
    spread_z(qkv, doubles)
    for r in singles[::-1]:
        qkv[r ^ 1] = swap(qkv[r], 1, 0)
    out_in = permute_columns(st["out_proj"], columns_at, dtype=BF)
    down_rel = class_rows(place, st["down_proj"])
    ffn_gain_in = st["ffn_gain"].reshape(devices, rows_each)[blocks_at].reshape(-1)
    n_pages = seq_len // PAGE
    holders = lax.dynamic_slice_in_dim(page_slot, req * n_pages, n_pages, 0) // n_pages
    page_bits = [PAIR, 1] + [bit for bit in zbits if bit != PAIR]
    at_slot = [
        sum(bit for k, bit in enumerate(reversed(page_bits)) if (i >> k) & 1)
        for i in range(n_req)
    ]
    relative = jnp.asarray(at_slot, jnp.int32) ^ req
    chosen = jnp.argmax(holders[None, :] == relative[:, None], axis=1)
    targets = req * n_pages + jnp.arange(n_pages, dtype=jnp.int32)
    source = jnp.argmax(page_slot[None, :] == targets[:, None], axis=1) // n_pages
    arrival = [0]
    for bit in page_bits:
        arrival = arrival + [r ^ bit for r in arrival]
    arrival = jnp.asarray(arrival, jnp.int32) ^ req
    source = jnp.argmax(arrival[None, :] == source[:, None], axis=1)
    tokens_share = lax.dynamic_slice_in_dim(tokens_in, tp * share, share, 0)
    st = sync(
        dict(
            qkv=qkv,
            gu=gu,
            blocks=blocks,
            x_norm=x_norm,
            out_in=out_in,
            down_rel=down_rel,
            ffn_gain_in=ffn_gain_in,
            pages=(chosen, source),
            tokens_share=tokens_share,
        )
    )

    qkv, gu, blocks, x_norm, out_in = (st[k] for k in ("qkv", "gu", "blocks", "x_norm", "out_in"))
    chosen, source = st["pages"]
    tokens_share = st["tokens_share"]
    down_rel, ffn_gain_in = st["down_rel"], st["ffn_gain_in"]
    spread_class(gu[0], *blocks[0], [PAIR])
    spread_class(gu[1], *blocks[1], plain)
    for r in doubles:
        qkv[r ^ 1] = swap(qkv[r], 1, 0)
    gu[1][0] = blocks[1][0]
    gu[1][1] = swap(blocks[1][0], 1, 0)
    width = model_dim // n_req
    first = [0, 1] + [r | j for r in singles for j in (0, 1)]
    last = [r | j for r in doubles for j in (0, 1)]

    def part(rs):
        return dot(
            jnp.concatenate([x_norm[:, r * width : (r + 1) * width] for r in rs], axis=1),
            assemble([qkv[r] for r in rs], n_tp, group_cols),
        )

    joined = part(first)
    st = sync(dict(qkv=qkv, gu=gu, blocks=blocks, joined=joined, x_norm=x_norm))

    qkv, gu, blocks, x_norm = (st[k] for k in ("qkv", "gu", "blocks", "x_norm"))
    spread_class(gu[0], *blocks[0], crossed)
    spread_class(gu[1], *blocks[1], [PAIR])
    gu[0][0] = blocks[0][0]
    gu[0][1] = swap(blocks[0][0], 1, 0)
    for r in plain:
        gu[0][r ^ 1] = swap(gu[0][r], 1, 0)
    shares = sorted(range(n_tp), key=lambda s: [(s >> k) & 1 for k in range(len(bits))])
    leaving, staying, *box = attend(
        place,
        lengths,
        chosen.astype(jnp.int32),
        st["joined"],
        jnp.concatenate([x_norm[:, r * width : (r + 1) * width] for r in last], axis=1),
        [assemble([qkv[r] for r in last], n_tp, group_cols)],
        tables,
        out_in,
        (local_heads, local_kv, head_dim),
        shares,
    )
    st = sync(dict(gu=gu, leaving=leaving, staying=staying, box=box))

    gu, box = st["gu"], st["box"]
    keep, send = add_share(st["staying"], swap(st["leaving"], 0, bits[0]), tokens_share)
    arrived = swap(send, 0, bits[1])
    spread_class(gu[1], None, None, crossed)
    gu[0][PAIR ^ 1] = swap(gu[0][PAIR], 1, 0)
    for r in plain:
        gu[1][r ^ 1] = swap(gu[1][r], 1, 0)

    def page_parts(box):
        half = box[0].shape[0] // 2
        return [pages[:half] for pages in box], jnp.concatenate(
            [pages[half:] for pages in box], axis=0
        )

    def page_step(parts, bit):
        kept, leaving = parts
        half = kept[0].shape[0]
        moved = swap(leaving, bit, 0)
        return kept + [moved[at : at + half] for at in range(0, leaving.shape[0], half)]

    late = crossed[0]
    box = [box[0], swap(box[1], page_bits[0], 0)]
    gu[1][late] = hold(gu[1][late], box[1], gu[0][PAIR ^ 1], *[gu[1][r ^ 1] for r in plain])
    resid_in, h_share, h_leaving = norm_share(
        keep, arrived, ffn_gain_in.reshape(n_req, model_dim // n_req)
    )
    st = sync(dict(gu=gu, h=(h_share, h_leaving), resid_in=resid_in, box=box))

    gu, resid_in = st["gu"], st["resid_in"]
    h_share, h_leaving = st["h"]
    cross = n_tp // 2
    own = (h_share, swap(h_share, 0, cross))
    theirs = (swap(h_leaving, PAIR, 0), swap(h_leaving, PAIR, cross))
    for r in crossed:
        gu[0][r ^ 1] = swap(gu[0][r], 1, 0)
    gu[1][PAIR ^ 1] = swap(gu[1][PAIR], 1, 0)
    coarse = resid_in.astype(BF)
    fine = (resid_in - coarse.astype(F32)).astype(BF)
    terms = permute_columns(jnp.concatenate([coarse, fine], axis=0), columns_back)
    st = sync(dict(gu=gu, own=own, theirs=theirs, terms=terms, box=page_parts(st["box"])))

    gu, box = st["gu"], st["box"]
    resid = st["terms"][:share] + st["terms"][share:]
    own, theirs = (jnp.concatenate(st[k], axis=0) for k in ("own", "theirs"))
    weight = assemble([gu[0][r] for r in range(n_req)], n_tp, 2 * chunks[0])
    hidden = gated(theirs, weight)[0]
    returned = [swap(hidden, PAIR, 0)]
    own_next, theirs_next = swap(own, 0, bits[0]), swap(theirs, 0, bits[0])
    for r in crossed:
        gu[1][r ^ 1] = swap(gu[1][r], 1, 0)
    hidden = gated(theirs_next, weight)[0]
    h_own = jnp.concatenate([own, own_next], axis=0)
    h_theirs = jnp.concatenate([theirs, theirs_next], axis=0)
    weights = [weight, assemble([gu[1][r] for r in range(n_req)], n_tp, 2 * chunks[1], 4 * 10**9)]
    st = sync(
        dict(
            weights=weights,
            h=(h_own, h_theirs),
            hidden=(hidden, returned),
            resid=resid,
            box=box,
        )
    )

    resid, box = st["resid"], st["box"]
    h_own, h_theirs = st["h"]
    hidden, returned = st["hidden"]
    returned = list(returned) + [swap(hidden, PAIR, 0)]
    weights = st["weights"]
    theirs = gated(h_theirs, weights[1])
    h_own, theirs = sync((h_own, theirs))
    kept = [gated(h_own, weight)[0] for weight in weights]
    rows = seq_len // 2
    product = []
    for i in range(2):
        part = rows_product([(piece, i * rows) for piece in kept], down_rel[0], 0, rows)
        product.append(rows_product([(returned[i], 0)], down_rel[1], 0, rows, part))
    for bit in page_bits[1:-1]:
        box = page_step(box if bit == page_bits[1] else page_parts(box), bit)
    leaving_pages = pack_pages(box)
    returned, box, leaving_pages, product = sync(
        (swap(theirs[0], PAIR, 0), box, leaving_pages, product)
    )
    leaving = rows_product([(returned, rows)], down_rel[1], chunks[0], rows, product[1], BF)
    arrived = swap(leaving, 0, bits[0])
    staying = rows_product([(returned, 0)], down_rel[1], chunks[0], rows, product[0])
    keep, send = add_share(staying, arrived, resid)
    arrived_pages = swap(leaving_pages, page_bits[-1], 0)
    share_slots = tp * share + jnp.arange(share, dtype=jnp.int32)
    live_share = (share_slots < lengths[0]).astype(F32)
    layer_out = ((keep + swap(send, 0, bits[1]).astype(F32)) * live_share[:, None]).astype(BF)
    kv_cache = pick_pages(source.astype(jnp.int32), box, arrived_pages, n_pages)
    return (layer_out, kv_cache)


def solution(mesh):
    return jax.shard_map(
        body,
        mesh=mesh,
        in_specs=(
            P("req", None),
            P("req"),
            P(),
            P(),
            P(("req", "tp"), None),
            P(("req", "tp"), None),
            P(),
            P(),
            P("tp", None),
            P("tp", None),
        ),
        out_specs=(P(("req", "tp"), None), P("req", None, "tp")),
        check_vma=False,
    )
```
